32 devices in a mesh: grp: 4 (over y, core), wide: 4 (over z), tp: 2 (over x).
Axes of the slice: x: 2, y: 2, z: 4, core: 2. Of those that a mesh axis runs over, the one named last changes fastest.
Arguments:
- layer_input: bfloat16 [4096, 768], P(('grp', 'wide')), may hold values from -6 to 6
- memory: bfloat16 [4096, 768], P(('grp', 'wide')), may hold values from -6 to 6
- reader_map: int32 [4096], P('grp'), may hold values from 0 to 3, as said below
- target_ids: int32 [4096], P('grp'), may hold values from 0 to 32127
- target_lengths: int32 [16], replicated, may hold values from 128 to 256, as said below
- out_grad: bfloat16 [4096, 768], P(('grp', 'wide')), may hold values from -0.00036621094 to 0.00036621094
- self_q: bfloat16 [768, 768], P('wide', 'tp'), may hold values from -0.21875 to 0.21875
- self_k: bfloat16 [768, 768], P('wide', 'tp'), may hold values from -0.21875 to 0.21875
- self_v: bfloat16 [768, 768], P('wide', 'tp'), may hold values from -0.21875 to 0.21875
- self_o: bfloat16 [768, 768], P('wide', 'tp'), may hold values from -0.75 to 0.75
- cross_q: bfloat16 [768, 768], P('wide', 'tp'), may hold values from -0.21875 to 0.21875
- cross_k: bfloat16 [768, 768], P('wide', 'tp'), may hold values from -0.21875 to 0.21875
- cross_v: bfloat16 [768, 768], P('wide', 'tp'), may hold values from -0.21875 to 0.21875
- cross_o: bfloat16 [768, 768], P('wide', 'tp'), may hold values from -0.75 to 0.75
- ff_gate: bfloat16 [768, 2048], P('wide', 'tp'), may hold values from -0.21875 to 0.21875
- ff_up: bfloat16 [768, 2048], P('wide', 'tp'), may hold values from -0.21875 to 0.21875
- ff_out: bfloat16 [768, 2048], P('wide', 'tp'), may hold values from -0.125 to 0.125
- gain_self: bfloat16 [768], P('wide'), may hold values from 0.099609375 to 1.8984375
- gain_cross: bfloat16 [768], P('wide'), may hold values from 0.099609375 to 1.8984375
- gain_ff: bfloat16 [768], P('wide'), may hold values from 0.099609375 to 1.8984375
- gain_exit: bfloat16 [768], P('wide'), may hold values from 0.099609375 to 1.8984375
- exit_table: bfloat16 [32128, 768], P(('wide', 'tp')), may hold values from -9 to 9
Outputs:
- block_output: bfloat16 [4096, 768], P(('grp', 'wide'))
- loss: float32 [], replicated
- input_grad: float32 [4096, 768], P(('grp', 'wide'))
- memory_grad: float32 [4096, 768], P(('grp', 'wide'))
- self_q_grad: float32 [768, 768], P('wide', 'tp')
- self_k_grad: float32 [768, 768], P('wide', 'tp')
- self_v_grad: float32 [768, 768], P('wide', 'tp')
- self_o_grad: float32 [768, 768], P('wide', 'tp')
- cross_q_grad: float32 [768, 768], P('wide', 'tp')
- cross_k_grad: float32 [768, 768], P('wide', 'tp')
- cross_v_grad: float32 [768, 768], P('wide', 'tp')
- cross_o_grad: float32 [768, 768], P('wide', 'tp')
- ff_gate_grad: float32 [768, 2048], P('wide', 'tp')
- ff_up_grad: float32 [768, 2048], P('wide', 'tp')
- ff_out_grad: float32 [768, 2048], P('wide', 'tp')
- gain_self_grad: float32 [768], P('wide')
- gain_cross_grad: float32 [768], P('wide')
- gain_ff_grad: float32 [768], P('wide')
- gain_exit_grad: float32 [768], P('wide')
- exit_grad: float32 [32128, 768], P(('wide', 'tp'))
The draws below stay inside these ranges and needn't reach their ends.
Inputs may be any that keep to these rules, and one draw needn't show every extreme that they name: `reader_map`: each memory row is read by exactly one target sequence of its group; every sequence reads at least one row of its group; of the 256 rows held by one device, at most 128 are read by one sequence, and in each group one sequence reads exactly 128 rows held on every device of wide. `target_lengths`: some sequence has the full length 256.
All inputs are finite; a program needn't handle non-finite values.
Results may differ from the reference program's by a relative error of at most 0.03.
Values may be sent and summed in bfloat16 or wider, within the bound.
A program may use at most 192 MiB of HBM per device.

```python
import math
import jax
import jax.numpy as jnp
import numpy as np
from jax import lax

D = 768
HEADS = 12
HEAD_DIM = 64
FF = 2048
VOCAB = 32128
T_DEV = 256
M_DEV = 256
CAP = 128
ROWS = 4096
MEM_ROWS = 4096
N_GRP = 4
N_WIDE = 4


def draw_reader_map(key, part):
    first, second, third, fourth = jax.random.split(key, 4)
    slots = N_WIDE * CAP
    blocks = N_GRP * N_WIDE
    full_reader = jax.random.randint(first, (N_GRP,), 0, N_WIDE)
    ranking = jax.vmap(lambda k: jax.random.permutation(k, N_WIDE))(jax.random.split(second, N_GRP))
    noise = jax.random.randint(third, (blocks, slots), 0, 4 * slots)
    slot_ids = jnp.arange(slots, dtype=jnp.int32)
    label = slot_ids // CAP
    within = slot_ids % CAP
    block_ids = jnp.arange(blocks, dtype=jnp.int32)
    group = block_ids // N_WIDE
    holder = block_ids % N_WIDE
    forced_full = label[None, :] == full_reader[group][:, None]
    forced_own = (label[None, :] == holder[:, None]) & (within[None, :] == 0)
    tier = jnp.where(forced_full, 0, jnp.where(forced_own, 1, 2))
    popular = ranking[group][:, label]
    score = noise + popular * (2 * slots)
    total = tier * 2 ** 28 + score * slots + slot_ids[None, :]
    order = jnp.argsort(total, axis=1)[:, :M_DEV]
    chosen = label[order]
    shuffle = jax.vmap(lambda k: jax.random.permutation(k, M_DEV))(jax.random.split(fourth, blocks))
    chosen = jnp.take_along_axis(chosen, shuffle, axis=1)
    return chosen.reshape(-1).astype(jnp.int32)


def draw_target_lengths(key, part):
    first, second = jax.random.split(key)
    count = N_GRP * N_WIDE
    lengths = jax.random.randint(first, (count,), T_DEV // 2, T_DEV + 1)
    longest = jax.random.randint(second, (), 0, count)
    return jnp.where(jnp.arange(count) == longest, T_DEV, lengths).astype(jnp.int32)


def place_ends(values, own_key, smallest, top_value):
    longest = values.shape.index(max(values.shape))
    spots = []
    for shift in (0, 1):
        where = [jax.random.randint(jax.random.fold_in(own_key, axis), (), 0, length) for axis, length in enumerate(values.shape)]
        where[longest] = (where[longest] + shift) % values.shape[longest]
        spots.append(tuple(where))
    return values.at[spots[0]].set(smallest).at[spots[1]].set(top_value)


def levels(own_key, extent, pieces, least, top_value):
    level, own = 1.0, jax.random.fold_in(own_key, 6)
    for axis_at, blocks in pieces:
        draws = jnp.exp(jax.random.uniform(jax.random.fold_in(own, axis_at), (blocks,), jnp.float32, least / len(pieces), top_value / len(pieces)))
        level = level * jnp.repeat(draws, extent[axis_at] // blocks).reshape([-1 if axis == axis_at else 1 for axis in range(len(extent))])
    return level


def rank_table(count, skew):
    weights = [(1 << 20) // math.isqrt(standing ** skew) + 1 for standing in range(1, count + 1)]
    deviation = 1 + sum(weights) // (1 << 30)
    return np.cumsum(np.array([max(1, weight // deviation) for weight in weights]))


def skewed_ids(rng, extent, count, skew):
    grid = rank_table(count, skew)
    lot = jax.random.randint(jax.random.fold_in(rng, 1), extent, 0, int(grid[count - 1]))
    rank = jnp.searchsorted(jnp.asarray(grid, jnp.int32), lot, side="right")
    return jax.random.permutation(jax.random.fold_in(rng, 2), count)[rank].astype(jnp.int32)


def bell_draw(own_key, shape, scale, reach, shards=(), kind=jnp.bfloat16):
    factor_of = levels(own_key, shape, shards, -0.22, 0.18) if shards else 1.0
    values = jax.random.normal(own_key, shape, jnp.float32) * scale * factor_of
    return jnp.minimum(jnp.maximum(values, -reach), reach).astype(kind)


def setup_inputs(seed: int = 0) -> dict:
    seeds = jax.random.split(jax.random.key(seed), 23)
    return {
        "layer_input": bell_draw(seeds[0], (ROWS, D), 1.0, 6.0, ((0, 16),)),
        "memory": bell_draw(seeds[1], (MEM_ROWS, D), 1.0, 6.0, ((0, 16),)),
        "reader_map": draw_reader_map(jax.random.fold_in(seeds[22], 71), 0),
        "target_ids": place_ends(skewed_ids(seeds[3], (ROWS,), VOCAB, 2), jax.random.fold_in(seeds[3], 3), 0, VOCAB - 1).astype(jnp.int32),
        "target_lengths": draw_target_lengths(jax.random.fold_in(seeds[22], 71), 0),
        "out_grad": bell_draw(seeds[5], (ROWS, D), (0.1 * ROWS ** -1), 0.00036621094, ((0, 16),)),
        "self_q": bell_draw(seeds[6], (D, HEADS * HEAD_DIM), D ** -0.5, 0.21875, ((0, 4), (1, 2))),
        "self_k": bell_draw(seeds[7], (D, HEADS * HEAD_DIM), D ** -0.5, 0.21875, ((0, 4), (1, 2))),
        "self_v": bell_draw(seeds[8], (D, HEADS * HEAD_DIM), D ** -0.5, 0.21875, ((0, 4), (1, 2))),
        "self_o": bell_draw(seeds[9], (D, HEADS * HEAD_DIM), HEAD_DIM ** -0.5, 0.75, ((0, 4), (1, 2))),
        "cross_q": bell_draw(seeds[10], (D, HEADS * HEAD_DIM), D ** -0.5, 0.21875, ((0, 4), (1, 2))),
        "cross_k": bell_draw(seeds[11], (D, HEADS * HEAD_DIM), D ** -0.5, 0.21875, ((0, 4), (1, 2))),
        "cross_v": bell_draw(seeds[12], (D, HEADS * HEAD_DIM), D ** -0.5, 0.21875, ((0, 4), (1, 2))),
        "cross_o": bell_draw(seeds[13], (D, HEADS * HEAD_DIM), HEAD_DIM ** -0.5, 0.75, ((0, 4), (1, 2))),
        "ff_gate": bell_draw(seeds[14], (D, FF), D ** -0.5, 0.21875, ((0, 4), (1, 2))),
        "ff_up": bell_draw(seeds[15], (D, FF), D ** -0.5, 0.21875, ((0, 4), (1, 2))),
        "ff_out": bell_draw(seeds[16], (D, FF), FF ** -0.5, 0.125, ((0, 4), (1, 2))),
        "gain_self": jnp.clip(1.0 + 0.18 * jax.random.normal(seeds[17], (D,), jnp.float32), 0.099609375, 1.8984375).astype(jnp.bfloat16),
        "gain_cross": jnp.clip(1.0 + 0.18 * jax.random.normal(seeds[18], (D,), jnp.float32), 0.099609375, 1.8984375).astype(jnp.bfloat16),
        "gain_ff": jnp.clip(1.0 + 0.18 * jax.random.normal(seeds[19], (D,), jnp.float32), 0.099609375, 1.8984375).astype(jnp.bfloat16),
        "gain_exit": jnp.clip(1.0 + 0.18 * jax.random.normal(seeds[20], (D,), jnp.float32), 0.099609375, 1.8984375).astype(jnp.bfloat16),
        "exit_table": bell_draw(seeds[21], (VOCAB, D), 1.5, 9.0, ((0, 8),)),
    }


EPSILON = 1e-06
MASKED = -1e+30
HIGH = lax.Precision.HIGHEST

@jax.custom_vjp
def low(v):
    return lax.optimization_barrier(v.astype(jnp.bfloat16)).astype(jnp.float32)

@jax.custom_vjp
def low_back(v):
    return v

def low_keep(v):
    return (low(v), None)

def low_pass(kept, grad):
    return (grad,)

def back_keep(v):
    return (v, None)

def back_low(kept, grad):
    return (low(grad),)
low.defvjp(low_keep, low_pass)
low_back.defvjp(back_keep, back_low)

def both_ways(values):
    return low(low_back(values))

def matmul(left, right):
    return jnp.dot(left, right, precision=HIGH)

def rms(values, gain):
    return values * lax.rsqrt(lax.optimization_barrier(jnp.mean(values * values, axis=1, keepdims=True)) + EPSILON) * gain

def smooth_gate(values):
    return jax.nn.gelu(values, approximate=True)

def attention(queries, keys, values, allowed):
    scores = jnp.einsum('rhe,khe->hrk', queries, keys, precision=HIGH) * HEAD_DIM ** (-0.5)
    scores = low_back(jnp.where(allowed[None], scores, MASKED))
    highest = lax.optimization_barrier(jnp.max(scores, axis=2, keepdims=True))
    exponent = jnp.exp(scores - highest)
    soft = low(exponent / lax.optimization_barrier(jnp.sum(exponent, axis=2, keepdims=True)))
    context = jnp.einsum('hrk,khe->rhe', soft, values, precision=HIGH)
    return both_ways(context.reshape(queries.shape[0], -1))

def layer(floats, reader_map, target_ids, target_lengths):
    hidden, memory, self_q, self_k, self_v, self_o, cross_q, cross_k, cross_v, cross_o, ff_gate, ff_up, ff_out, gain_self, gain_cross, gain_ff, gain_exit, exit_table = floats
    rows = hidden.shape[0]
    seq_count = rows // T_DEV
    positions = jnp.arange(T_DEV, dtype=jnp.int32)
    norm_self = low(rms(hidden, gain_self))
    shape_heads = (seq_count, T_DEV, HEADS, HEAD_DIM)
    queries = both_ways(matmul(norm_self, self_q)).reshape(shape_heads)
    keys = both_ways(matmul(norm_self, self_k)).reshape(shape_heads)
    values = both_ways(matmul(norm_self, self_v)).reshape(shape_heads)

    def self_seq(parts):
        query, key_rows, value_rows, length = parts
        allowed = (positions[None, :] <= positions[:, None]) & (positions[None, :] < length)
        return attention(query, key_rows, value_rows, allowed)
    context_self = lax.map(jax.checkpoint(self_seq), (queries, keys, values, target_lengths)).reshape(rows, -1)
    resid_one = hidden + low_back(matmul(context_self, self_o.T))
    norm_cross = low(rms(resid_one, gain_cross))
    cross_queries = both_ways(matmul(norm_cross, cross_q)).reshape(shape_heads)
    memory_keys = both_ways(matmul(memory, cross_k)).reshape(N_GRP, -1, HEADS, HEAD_DIM)
    memory_values = both_ways(matmul(memory, cross_v)).reshape(N_GRP, -1, HEADS, HEAD_DIM)
    readers = reader_map.reshape(N_GRP, -1)

    def cross_seq(parts):
        query, index = parts
        group = index // N_WIDE
        allowed = (readers[group] == index % N_WIDE)[None, :]
        return attention(query, memory_keys[group], memory_values[group], allowed)
    context_cross = lax.map(jax.checkpoint(cross_seq), (cross_queries, jnp.arange(seq_count, dtype=jnp.int32))).reshape(rows, -1)
    resid_two = resid_one + low_back(matmul(context_cross, cross_o.T))
    norm_ff = low(rms(resid_two, gain_ff))
    gate_act = both_ways(matmul(norm_ff, ff_gate))
    up_act = both_ways(matmul(norm_ff, ff_up))
    ff_hidden = low(smooth_gate(gate_act) * up_act)
    resid_three = resid_two + low_back(matmul(ff_hidden, ff_out.T))
    norm_exit = low(rms(resid_three, gain_exit))
    block_rows = 512 if rows % 512 == 0 else rows

    def exit_block(parts):
        rows_block, targets_block = parts
        logits = low_back(matmul(rows_block, exit_table.T) * D ** (-0.5))
        highest = lax.optimization_barrier(jnp.max(logits, axis=1, keepdims=True))
        log_total = highest[:, 0] + jnp.log(lax.optimization_barrier(jnp.sum(jnp.exp(logits - highest), axis=1)))
        picked = jnp.take_along_axis(logits, targets_block[:, None], axis=1)[:, 0]
        return log_total - picked
    token_loss = lax.map(jax.checkpoint(exit_block), (norm_exit.reshape(-1, block_rows, D), target_ids.reshape(-1, block_rows))).reshape(rows)
    valid = jnp.arange(rows, dtype=jnp.int32) % T_DEV < jnp.repeat(target_lengths, T_DEV)
    loss = jnp.sum(jnp.where(valid, token_loss, 0.0)) / jnp.sum(target_lengths).astype(jnp.float32)
    return (resid_three, loss)

def reference(layer_input, memory, reader_map, target_ids, target_lengths, out_grad, self_q, self_k, self_v, self_o, cross_q, cross_k, cross_v, cross_o, ff_gate, ff_up, ff_out, gain_self, gain_cross, gain_ff, gain_exit, exit_table):
    floats = tuple((item.astype(jnp.float32) for item in (layer_input, memory, self_q, self_k, self_v, self_o, cross_q, cross_k, cross_v, cross_o, ff_gate, ff_up, ff_out, gain_self, gain_cross, gain_ff, gain_exit, exit_table)))

    def forward(*items):
        return layer(items, reader_map, target_ids, target_lengths)
    (resid_three, loss), pull = jax.vjp(forward, *floats)
    grads = pull((out_grad.astype(jnp.float32), jnp.ones((), jnp.float32)))
    return (resid_three.astype(jnp.bfloat16), loss, grads[0], grads[1], grads[2], grads[3], grads[4], grads[5], grads[6], grads[7], grads[8], grads[9], grads[10], grads[11], grads[12], grads[13], grads[14], grads[15], grads[16], grads[17])
```

```python
import jax
import jax.numpy as jnp
from jax import lax
from jax.experimental import pallas as pl
from jax.experimental.pallas import tpu as pltpu
from jax.sharding import PartitionSpec as P

HEAD_DIM = 64


EPSILON = 1e-06
MASKED = -1e30


def merged(shard, axis, combine):
    everything = jax.tree.map(
        lambda part, kind: lax.all_gather(part.astype(kind), axis),
        shard,
        (jnp.bfloat16, jnp.bfloat16, jnp.bfloat16),
    )

    def take(k):
        return jax.tree.map(lambda part, own: part[k].astype(own.dtype), everything, shard)

    return lax.fori_loop(
        1, lax.axis_size(axis), lambda k, so_far: combine(so_far, take(k)), take(0)
    )


def project(left, right):
    return jnp.dot(left, right, preferred_element_type=jnp.float32)


def project_back(left, right):
    return lax.dot_general(
        left, right, (((1,), (1,)), ((), ())), preferred_element_type=jnp.float32
    )


def outer_rows(left, right):
    return lax.dot_general(
        left, right, (((0,), (0,)), ((), ())), preferred_element_type=jnp.float32
    )


def smooth_gate(values):
    return jax.nn.gelu(values, approximate=True)


def normalize(values, gain):
    factor = lax.rsqrt(jnp.mean(values * values, axis=1, keepdims=True) + EPSILON)
    unit_rows = values * factor
    return ((unit_rows * gain).astype(jnp.bfloat16), unit_rows, factor)


def normalize_back(values, unit_rows, factor, gain, grad_rows):
    gain_grad = jnp.sum(grad_rows * unit_rows, axis=0)
    scaled = grad_rows * gain
    inner = jnp.mean(scaled * values, axis=1, keepdims=True)
    return (gain_grad, factor * scaled - unit_rows * factor * factor * inner)


def split_heads(values):
    return values.reshape(values.shape[0], -1, HEAD_DIM).transpose(1, 0, 2)


def join_heads(values):
    return values.transpose(1, 0, 2).reshape(values.shape[1], -1)


def read_slots(group_map, reader, holders, rows_each, capacity):
    matched = (group_map.reshape(holders, rows_each) == reader).astype(jnp.int32)
    ranks = jnp.cumsum(matched, axis=1) - 1
    counts = jnp.sum(matched, axis=1)
    place = lax.iota(jnp.int32, holders * capacity)
    valid = place % capacity < jnp.repeat(counts, capacity, total_repeat_length=holders * capacity)
    anchor = lax.iota(jnp.int32, holders)[:, None] * capacity + ranks
    target = jnp.where(matched > 0, anchor, holders * capacity)
    return (valid, target.reshape(-1))


def attend_forward(queries, keys, values, allowed):
    factor = HEAD_DIM ** (-0.5)

    def one_head(parts):
        query, key_rows, value_rows = parts
        scores = jnp.where(allowed, project_back(query, key_rows) * factor, MASKED)
        highest = jnp.max(scores, axis=1, keepdims=True)
        exponent = jnp.exp(scores - highest)
        total = jnp.sum(exponent, axis=1, keepdims=True)
        soft_weights = (exponent / total).astype(jnp.bfloat16)
        return (project(soft_weights, value_rows), (highest + jnp.log(total))[:, 0])

    context, log_total = lax.map(
        one_head, (split_heads(queries), split_heads(keys), split_heads(values))
    )
    return (join_heads(context).astype(jnp.bfloat16), log_total)


def attend_backward(queries, keys, values, context_grad, log_total, allowed):
    factor = HEAD_DIM ** (-0.5)

    def one_head(parts):
        query, key_rows, value_rows, grad_rows, log_row = parts
        scores = jnp.where(allowed, project_back(query, key_rows) * factor, MASKED)
        soft = jnp.exp(scores - log_row[:, None])
        soft_grad = project_back(grad_rows, value_rows)
        score_grad = (soft * (soft_grad - jnp.sum(soft * soft_grad, axis=1, keepdims=True))).astype(
            jnp.bfloat16
        )
        query_grad = project(score_grad, key_rows) * factor
        key_grad = outer_rows(score_grad, query) * factor
        value_grad = outer_rows(soft.astype(jnp.bfloat16), grad_rows)
        return (query_grad, key_grad, value_grad)

    grads = lax.map(
        one_head,
        (
            split_heads(queries),
            split_heads(keys),
            split_heads(values),
            split_heads(context_grad),
            log_total,
        ),
    )
    return (join_heads(grads[0]), join_heads(grads[1]), join_heads(grads[2]))


def heads_total(partial_rows):
    return lax.psum(partial_rows, "tp")


def input_total(partial_rows):
    return lax.psum(partial_rows.astype(jnp.bfloat16), "tp").astype(jnp.float32)


def merge_softmax(first, second):
    highest = jnp.maximum(first[0], second[0])
    total = first[1] * jnp.exp(first[0] - highest) + second[1] * jnp.exp(second[0] - highest)
    return (highest, total, first[2] + second[2])


def plain_body(
    layer_input,
    memory,
    reader_map,
    target_ids,
    target_lengths,
    out_grad,
    self_q,
    self_k,
    self_v,
    self_o,
    cross_q,
    cross_k,
    cross_v,
    cross_o,
    ff_gate,
    ff_up,
    ff_out,
    gain_self,
    gain_cross,
    gain_ff,
    gain_exit,
    exit_table,
):
    (
        w_query,
        w_key,
        w_value,
        w_output,
        c_query,
        c_key,
        c_value,
        c_output,
        w_gate,
        w_up,
        w_down,
        full_gain_self,
        full_gain_cross,
        full_gain_ff,
        full_gain_exit,
    ) = (
        lax.all_gather(self_q, "wide", axis=0, tiled=True),
        lax.all_gather(self_k, "wide", axis=0, tiled=True),
        lax.all_gather(self_v, "wide", axis=0, tiled=True),
        lax.all_gather(self_o, "wide", axis=0, tiled=True),
        lax.all_gather(cross_q, "wide", axis=0, tiled=True),
        lax.all_gather(cross_k, "wide", axis=0, tiled=True),
        lax.all_gather(cross_v, "wide", axis=0, tiled=True),
        lax.all_gather(cross_o, "wide", axis=0, tiled=True),
        lax.all_gather(ff_gate, "wide", axis=0, tiled=True),
        lax.all_gather(ff_up, "wide", axis=0, tiled=True),
        lax.all_gather(ff_out, "wide", axis=0, tiled=True),
        lax.all_gather(gain_self, "wide", axis=0, tiled=True),
        lax.all_gather(gain_cross, "wide", axis=0, tiled=True),
        lax.all_gather(gain_ff, "wide", axis=0, tiled=True),
        lax.all_gather(gain_exit, "wide", axis=0, tiled=True),
    )
    gain_one = full_gain_self.astype(jnp.float32)
    gain_two = full_gain_cross.astype(jnp.float32)
    gain_three = full_gain_ff.astype(jnp.float32)
    gain_last = full_gain_exit.astype(jnp.float32)
    seq_rows = layer_input.shape[0]
    wide_count = lax.axis_size("wide")
    wide_index = lax.axis_index("wide")
    group_index = lax.axis_index("grp")
    group_lengths = lax.dynamic_slice_in_dim(target_lengths, group_index * wide_count, wide_count)
    own_length = lax.dynamic_index_in_dim(group_lengths, wide_index, keepdims=False)
    hidden = layer_input.astype(jnp.float32)
    norm_self, unit_self, factor_self = normalize(hidden, gain_one)
    queries = project(norm_self, w_query).astype(jnp.bfloat16)
    keys = project(norm_self, w_key).astype(jnp.bfloat16)
    values = project(norm_self, w_value).astype(jnp.bfloat16)
    position = lax.iota(jnp.int32, seq_rows)
    allowed_self = (position[None, :] <= position[:, None]) & (position[None, :] < own_length)
    context_self, log_self = attend_forward(queries, keys, values, allowed_self)
    resid_one = hidden + heads_total(project_back(context_self, w_output))
    norm_cross, unit_cross, factor_cross = normalize(resid_one, gain_two)
    cross_queries = project(norm_cross, c_query).astype(jnp.bfloat16)
    memory_keys = project(memory, c_key).astype(jnp.bfloat16)
    memory_values = project(memory, c_value).astype(jnp.bfloat16)
    rows_each = memory.shape[0]
    capacity = max(2, 2 * rows_each // wide_count)
    slot_count = wide_count * capacity
    slot_valid, slot_target = read_slots(reader_map, wide_index, wide_count, rows_each, capacity)
    keys_all, values_all = (
        lax.all_gather(memory_keys, "wide", axis=0, tiled=True),
        lax.all_gather(memory_values, "wide", axis=0, tiled=True),
    )
    read_table = (
        jnp.zeros((slot_count,), jnp.int32)
        .at[slot_target]
        .set(lax.iota(jnp.int32, wide_count * rows_each), mode="drop")
    )
    keys_read = jnp.take(keys_all, read_table, axis=0)
    values_read = jnp.take(values_all, read_table, axis=0)
    allowed_cross = slot_valid[None, :]
    context_cross, log_cross = attend_forward(cross_queries, keys_read, values_read, allowed_cross)
    resid_two = resid_one + heads_total(project_back(context_cross, c_output))
    norm_ff, unit_ff, factor_ff = normalize(resid_two, gain_three)
    gate_float = project(norm_ff, w_gate).astype(jnp.bfloat16).astype(jnp.float32)
    up_float = project(norm_ff, w_up).astype(jnp.bfloat16).astype(jnp.float32)
    gelu_value, gelu_pull = jax.vjp(smooth_gate, gate_float)
    ff_hidden = (gelu_value * up_float).astype(jnp.bfloat16)
    resid_three = resid_two + heads_total(project_back(ff_hidden, w_down))
    block_output = resid_three.astype(jnp.bfloat16)
    norm_exit, unit_exit, factor_exit = normalize(resid_three, gain_last)
    rows_all = lax.all_gather(norm_exit, "wide", axis=0, tiled=True)
    group_tokens = rows_all.shape[0]
    vocab_rows = exit_table.shape[0]
    scale_exit = float(rows_all.shape[1]) ** (-0.5)
    logits = project_back(rows_all, exit_table) * scale_exit
    vocab_ids = lax.axis_index(("wide", "tp")) * vocab_rows + lax.iota(jnp.int32, vocab_rows)
    is_target = target_ids[:, None] == vocab_ids[None, :]
    local_high = jnp.max(logits, axis=1)
    local_total = jnp.sum(jnp.exp(logits - local_high[:, None]), axis=1)
    local_pick = jnp.sum(jnp.where(is_target, logits, 0.0), axis=1)
    highest, total_exp, target_logit = merged(
        (local_high, local_total, local_pick), ("wide", "tp"), merge_softmax
    )
    log_total = highest + jnp.log(total_exp)
    token_place = lax.iota(jnp.int32, group_tokens)
    valid = token_place % seq_rows < jnp.repeat(
        group_lengths, seq_rows, total_repeat_length=group_tokens
    )
    token_count = jnp.sum(target_lengths).astype(jnp.float32)
    token_weight = jnp.where(valid, 1.0, 0.0).astype(jnp.float32) / token_count
    group_loss = jnp.sum(token_weight * (log_total - target_logit))
    logit_grad = (
        (jnp.exp(logits - log_total[:, None]) - jnp.where(is_target, 1.0, 0.0))
        * token_weight[:, None]
    ).astype(jnp.bfloat16)
    rows_grad_all = project(logit_grad, exit_table) * scale_exit
    exit_grad = outer_rows(logit_grad, rows_all) * scale_exit
    rows_part = lax.psum_scatter(
        rows_grad_all.astype(jnp.bfloat16), "wide", scatter_dimension=0, tiled=True
    )
    norm_exit_grad = lax.psum(rows_part, "tp").astype(jnp.float32)
    gain_exit_grad, back_exit = normalize_back(
        resid_three, unit_exit, factor_exit, gain_last, norm_exit_grad
    )
    resid_three_grad = out_grad.astype(jnp.float32) + back_exit
    ff_branch = resid_three_grad.astype(jnp.bfloat16)
    w_down_grad = outer_rows(ff_branch, ff_hidden)
    hidden_grad = project(ff_branch, w_down)
    gate_grad = gelu_pull(hidden_grad * up_float)[0].astype(jnp.bfloat16)
    up_grad = (hidden_grad * gelu_value).astype(jnp.bfloat16)
    w_gate_grad = outer_rows(norm_ff, gate_grad)
    w_up_grad = outer_rows(norm_ff, up_grad)
    norm_ff_grad = input_total(project_back(gate_grad, w_gate) + project_back(up_grad, w_up))
    gain_ff_grad, back_ff = normalize_back(resid_two, unit_ff, factor_ff, gain_three, norm_ff_grad)
    resid_two_grad = resid_three_grad + back_ff
    cross_branch = resid_two_grad.astype(jnp.bfloat16)
    c_output_grad = outer_rows(cross_branch, context_cross)
    cross_context_grad = project(cross_branch, c_output).astype(jnp.bfloat16)
    cross_query_grad, keys_grad_read, values_grad_read = attend_backward(
        cross_queries, keys_read, values_read, cross_context_grad, log_cross, allowed_cross
    )
    empty_grads = jnp.zeros((wide_count * rows_each, keys_grad_read.shape[1]), jnp.float32)
    keys_grad_all = empty_grads.at[read_table].add(keys_grad_read)
    values_grad_all = empty_grads.at[read_table].add(values_grad_read)
    keys_grad, values_grad = (
        lax.psum_scatter(
            keys_grad_all.astype(jnp.bfloat16), "wide", scatter_dimension=0, tiled=True
        ).astype(jnp.float32),
        lax.psum_scatter(
            values_grad_all.astype(jnp.bfloat16), "wide", scatter_dimension=0, tiled=True
        ).astype(jnp.float32),
    )
    keys_grad = keys_grad.astype(jnp.bfloat16)
    values_grad = values_grad.astype(jnp.bfloat16)
    cross_query_grad = cross_query_grad.astype(jnp.bfloat16)
    c_query_grad = outer_rows(norm_cross, cross_query_grad)
    c_key_grad = outer_rows(memory, keys_grad)
    c_value_grad = outer_rows(memory, values_grad)
    norm_cross_grad, memory_grad = (
        lax.psum(project_back(cross_query_grad, c_query).astype(jnp.bfloat16), "tp").astype(
            jnp.float32
        ),
        lax.psum(
            (project_back(keys_grad, c_key) + project_back(values_grad, c_value)).astype(
                jnp.bfloat16
            ),
            "tp",
        ).astype(jnp.float32),
    )
    gain_cross_grad, back_cross = normalize_back(
        resid_one, unit_cross, factor_cross, gain_two, norm_cross_grad
    )
    resid_one_grad = resid_two_grad + back_cross
    self_branch = resid_one_grad.astype(jnp.bfloat16)
    w_output_grad = outer_rows(self_branch, context_self)
    self_context_grad = project(self_branch, w_output).astype(jnp.bfloat16)
    query_grad, key_grad, value_grad = attend_backward(
        queries, keys, values, self_context_grad, log_self, allowed_self
    )
    query_grad = query_grad.astype(jnp.bfloat16)
    key_grad = key_grad.astype(jnp.bfloat16)
    value_grad = value_grad.astype(jnp.bfloat16)
    w_query_grad = outer_rows(norm_self, query_grad)
    w_key_grad = outer_rows(norm_self, key_grad)
    w_value_grad = outer_rows(norm_self, value_grad)
    norm_self_grad = input_total(
        project_back(query_grad, w_query)
        + project_back(key_grad, w_key)
        + project_back(value_grad, w_value)
    )
    gain_self_grad, back_self = normalize_back(
        hidden, unit_self, factor_self, gain_one, norm_self_grad
    )
    input_grad = resid_one_grad + back_self
    shards = (
        lax.psum_scatter(
            w_query_grad.astype(jnp.bfloat16), "wide", scatter_dimension=0, tiled=True
        ).astype(jnp.float32),
        lax.psum_scatter(
            w_key_grad.astype(jnp.bfloat16), "wide", scatter_dimension=0, tiled=True
        ).astype(jnp.float32),
        lax.psum_scatter(
            w_value_grad.astype(jnp.bfloat16), "wide", scatter_dimension=0, tiled=True
        ).astype(jnp.float32),
        lax.psum_scatter(
            w_output_grad.astype(jnp.bfloat16), "wide", scatter_dimension=0, tiled=True
        ).astype(jnp.float32),
        lax.psum_scatter(
            c_query_grad.astype(jnp.bfloat16), "wide", scatter_dimension=0, tiled=True
        ).astype(jnp.float32),
        lax.psum_scatter(
            c_key_grad.astype(jnp.bfloat16), "wide", scatter_dimension=0, tiled=True
        ).astype(jnp.float32),
        lax.psum_scatter(
            c_value_grad.astype(jnp.bfloat16), "wide", scatter_dimension=0, tiled=True
        ).astype(jnp.float32),
        lax.psum_scatter(
            c_output_grad.astype(jnp.bfloat16), "wide", scatter_dimension=0, tiled=True
        ).astype(jnp.float32),
        lax.psum_scatter(
            w_gate_grad.astype(jnp.bfloat16), "wide", scatter_dimension=0, tiled=True
        ).astype(jnp.float32),
        lax.psum_scatter(
            w_up_grad.astype(jnp.bfloat16), "wide", scatter_dimension=0, tiled=True
        ).astype(jnp.float32),
        lax.psum_scatter(
            w_down_grad.astype(jnp.bfloat16), "wide", scatter_dimension=0, tiled=True
        ).astype(jnp.float32),
        lax.psum_scatter(
            gain_self_grad.astype(jnp.bfloat16), "wide", scatter_dimension=0, tiled=True
        ).astype(jnp.float32),
        lax.psum_scatter(
            gain_cross_grad.astype(jnp.bfloat16), "wide", scatter_dimension=0, tiled=True
        ).astype(jnp.float32),
        lax.psum_scatter(
            gain_ff_grad.astype(jnp.bfloat16), "wide", scatter_dimension=0, tiled=True
        ).astype(jnp.float32),
        lax.psum_scatter(
            gain_exit_grad.astype(jnp.bfloat16), "wide", scatter_dimension=0, tiled=True
        ).astype(jnp.float32),
    )
    totals = (
        lax.psum(shards[0].astype(jnp.bfloat16), "grp").astype(jnp.float32),
        lax.psum(shards[1].astype(jnp.bfloat16), "grp").astype(jnp.float32),
        lax.psum(shards[2].astype(jnp.bfloat16), "grp").astype(jnp.float32),
        lax.psum(shards[3].astype(jnp.bfloat16), "grp").astype(jnp.float32),
        lax.psum(shards[4].astype(jnp.bfloat16), "grp").astype(jnp.float32),
        lax.psum(shards[5].astype(jnp.bfloat16), "grp").astype(jnp.float32),
        lax.psum(shards[6].astype(jnp.bfloat16), "grp").astype(jnp.float32),
        lax.psum(shards[7].astype(jnp.bfloat16), "grp").astype(jnp.float32),
        lax.psum(shards[8].astype(jnp.bfloat16), "grp").astype(jnp.float32),
        lax.psum(shards[9].astype(jnp.bfloat16), "grp").astype(jnp.float32),
        lax.psum(shards[10].astype(jnp.bfloat16), "grp").astype(jnp.float32),
        lax.psum(shards[11].astype(jnp.bfloat16), "grp").astype(jnp.float32),
        lax.psum(shards[12].astype(jnp.bfloat16), "grp").astype(jnp.float32),
        lax.psum(shards[13].astype(jnp.bfloat16), "grp").astype(jnp.float32),
        lax.psum(shards[14].astype(jnp.bfloat16), "grp").astype(jnp.float32),
        lax.psum(exit_grad.astype(jnp.bfloat16), "grp").astype(jnp.float32),
        lax.psum(group_loss.astype(jnp.bfloat16), "grp").astype(jnp.float32),
    )
    return (
        block_output,
        totals[16],
        input_grad,
        memory_grad,
        totals[0],
        totals[1],
        totals[2],
        totals[3],
        totals[4],
        totals[5],
        totals[6],
        totals[7],
        totals[8],
        totals[9],
        totals[10],
        totals[11],
        totals[12],
        totals[13],
        totals[14],
        totals[15],
    )


MESH = pl.DeviceIdType.MESH
BF = jnp.bfloat16
F32 = jnp.float32


def dot_nn(left, right):
    return lax.dot_general(left, right, (((1,), (0,)), ((), ())), preferred_element_type=F32)


def dot_nt(left, right):
    return lax.dot_general(left, right, (((1,), (1,)), ((), ())), preferred_element_type=F32)


def dot_tn(left, right):
    return lax.dot_general(left, right, (((0,), (0,)), ((), ())), preferred_element_type=F32)


class Move:
    def __init__(self, out, arrival):
        self.out, self.arrival = out, arrival

    def start(self):
        self.out.start()
        return self

    def sent(self):
        self.out.wait_send()

    def landed(self):
        self.arrival.wait_recv()


class Links:
    def __init__(self, send_sems, recv_sems):
        self.send_sems, self.recv_sems = send_sems, recv_sems
        self.used = 0
        self.moves = []

    def move(self, src, dst, device, lands):
        k = self.used
        self.used += 1
        out = pltpu.make_async_remote_copy(
            src_ref=src, dst_ref=dst, send_sem=self.send_sems.at[k], recv_sem=self.recv_sems.at[k],
            device_id=device, device_id_type=MESH,
        )
        arrival = pltpu.make_async_remote_copy(
            src_ref=lands, dst_ref=lands, send_sem=self.send_sems.at[k], recv_sem=self.recv_sems.at[k],
            device_id=device, device_id_type=MESH,
        )
        made = Move(out, arrival)
        self.moves.append(made)
        return made

    def finish(self):
        for made in self.moves:
            made.sent()


class Copies:
    def __init__(self, sems):
        self.sems, self.used, self.pending = sems, 0, []

    def start(self, src, dst):
        made = pltpu.make_async_copy(src, dst, self.sems.at[self.used])
        self.used += 1
        made.start()
        return made

    def save(self, src, dst):
        self.pending.append(self.start(src, dst))

    def finish(self):
        for made in self.pending:
            made.wait()


def greet(devices):
    barrier = pltpu.get_barrier_semaphore()
    for device in devices:
        pl.semaphore_signal(barrier, inc=1, device_id=device, device_id_type=MESH)
    pl.semaphore_wait(barrier, len(devices))


def rms_rows(values, gain):
    factor = lax.rsqrt(jnp.mean(values * values, axis=1, keepdims=True) + EPSILON)
    return (values * factor * gain).astype(BF)


def lane_masks():
    lane = lax.broadcasted_iota(jnp.int32, (1, 2 * HEAD_DIM), 1)
    low = jnp.where(lane < HEAD_DIM, 1.0, 0.0).astype(F32)
    return low.astype(BF), (1.0 - low).astype(BF)


def both_heads(pair):
    low, high = lane_masks()
    return jnp.concatenate([pair * low, pair * high], axis=0)


def pick_heads(stacked):
    rows = stacked.shape[0] // 2
    lane = lax.broadcasted_iota(jnp.int32, (rows, 2 * HEAD_DIM), 1)
    return jnp.where(lane < HEAD_DIM, stacked[:rows], stacked[rows:])


def pair_columns(p):
    return pl.ds(pl.multiple_of(p * 2 * HEAD_DIM, 2 * HEAD_DIM), 2 * HEAD_DIM)


def attention_forward(pairs, queries, keys, values, probs, context, allowed):
    factor = HEAD_DIM ** (-0.5)

    def step(p, carry):
        cols = pair_columns(p)
        scores = dot_nt(both_heads(queries[:, cols]), keys[:, cols]) * factor
        scores = jnp.where(allowed, scores, MASKED)
        exponent = jnp.exp(scores - jnp.max(scores, axis=1, keepdims=True))
        soft = (exponent / jnp.sum(exponent, axis=1, keepdims=True)).astype(BF)
        probs[p] = soft
        context[:, cols] = pick_heads(dot_nn(soft, values[:, cols])).astype(BF)
        return carry

    lax.fori_loop(0, pairs, step, 0)


def forward_kernel(
    x_ref, mem_ref, map_ref, len_ref, gain_ref,
    q_in, k_in, v_in, so_in, cq_in, ck_in, cv_in, co_in, ga_in, up_in, dn_in,
    block_o, one_o, two_o, three_o, exit_o, q_o, k_o, v_o, cq_o, mk_o, mv_o, sc_o, cc_o, ps_o, pc_o,
    ga_o, up_o, sel_o, wa_o, wgu_o, wd_o, gain_o,
    wa, wgu, wd, gains, slots, packed, part_out, part_in,
    block, one, two, three, exit_rows, q, k, v, cq, mk, mv, sc, cc, ps, pc, ga, up, gain_sum,
    send_sems, recv_sems, copy_sems,
):
    count = map_ref.shape[0]
    g, w, t = lax.axis_index("grp"), lax.axis_index("wide"), lax.axis_index("tp")
    c = lax.rem(g, 2)
    left, right, far = (lax.rem(w + d, count) for d in (count - 1, 1, 2))
    to_left, to_right, to_far = {"wide": left}, {"wide": right}, {"wide": far}
    to_core, to_tp = {"grp": g + 1 - 2 * c}, {"tp": 1 - t}
    rows = x_ref.shape[0]
    links, copies = Links(send_sems, recv_sems), Copies(copy_sems)
    depth = q_in.shape[0]
    half = depth // 2
    wide_cols = dn_in.shape[1] // 2

    def own(at):
        return pl.ds(pl.multiple_of(at * depth, 16), depth)

    def part(at, which):
        return pl.ds(pl.multiple_of(at * depth + which * half, 16), half)

    order = (q_in, k_in, v_in, so_in, ck_in, cv_in, cq_in, co_in)
    placed = []
    for j in range(4):
        placed.append([copies.start(order[2 * j + e], wa.at[2 * j + e, own(w)]) for e in range(2)])
    placed.append([copies.start(ref, wgu.at[e, own(w)]) for e, ref in enumerate((ga_in, up_in))])
    placed.append(
        [copies.start(dn_in.at[:, pl.ds(e * wide_cols, wide_cols)], wd.at[e, own(w)]) for e in range(2)]
    )
    bufs = [(wa, 2 * j + c, 2 * j + 1 - c) for j in range(4)] + [(wgu, c, 1 - c), (wd, c, 1 - c)]
    greet([to_left, to_right, to_far, to_core, to_tp])

    gains[w] = gain_ref[...]
    gain_moves = [
        links.move(gain_ref, gains.at[w], device, gains.at[at]).start()
        for device, at in ((to_left, right), (to_right, left), (to_far, far))
    ]

    item = [{} for _ in bufs]

    def issue(i):
        buf, mine, other = bufs[i]
        for made in placed[i]:
            made.wait()
        src = buf.at[mine, own(w)]
        item[i]["from_left"] = links.move(src, src, to_right, buf.at[mine, own(left)]).start()
        item[i]["from_right"] = links.move(src, src, to_left, buf.at[mine, own(right)]).start()

    def to_other(i, where):
        buf, mine, other = bufs[i]
        src = buf.at[mine, where]
        item[i].setdefault("core", []).append(links.move(src, src, to_core, buf.at[other, where]).start())

    def forward(i):
        buf, mine, other = bufs[i]
        item[i]["from_left"].landed()
        src = buf.at[mine, part(left, 0)]
        item[i]["far_top"] = links.move(src, src, to_right, buf.at[mine, part(far, 0)]).start()
        to_other(i, own(left))
        item[i]["from_right"].landed()
        src = buf.at[mine, part(right, 1)]
        item[i]["far_low"] = links.move(src, src, to_left, buf.at[mine, part(far, 1)]).start()
        to_other(i, own(right))

    def complete(i):
        item[i]["far_top"].landed()
        to_other(i, part(far, 0))
        item[i]["far_low"].landed()
        to_other(i, part(far, 1))

    def ready(i):
        for made in item[i]["core"]:
            made.landed()

    issue(0)
    issue(1)

    capacity = slots.shape[0] // count
    readers = map_ref[...]
    own_map = map_ref[pl.ds(w, 1)]
    reader_iota = lax.broadcasted_iota(jnp.int32, (max(8, count), rows), 0)
    matched = jnp.where(reader_iota == own_map, 1.0, 0.0).astype(F32)
    before = lax.broadcasted_iota(jnp.int32, (rows, rows), 0) < lax.broadcasted_iota(
        jnp.int32, (rows, rows), 1
    )
    ranks = dot_nn(matched.astype(BF), jnp.where(before, 1.0, 0.0).astype(BF))
    rank = jnp.sum(matched * ranks, axis=0, keepdims=True).astype(jnp.int32)
    slot_of = own_map * capacity + rank
    slot_iota = lax.broadcasted_iota(jnp.int32, (slots.shape[0], rows), 0)
    choose = jnp.where(slot_iota == slot_of, 1.0, 0.0).astype(BF)
    packed[...] = dot_nn(choose, mem_ref[...]).astype(BF)

    def slot_rows(at, which):
        return pl.ds(pl.multiple_of(at * capacity + which * (capacity // 2), 16), capacity // 2)

    slot_moves = [
        links.move(packed.at[slot_rows(to, t)], slots.at[slot_rows(w, t)], device, slots.at[slot_rows(at, t)]).start()
        for device, to, at in ((to_left, left, right), (to_right, right, left), (to_far, far, far))
    ]
    slots[pl.ds(pl.multiple_of(w * capacity, 16), capacity), :] = packed[
        pl.ds(pl.multiple_of(w * capacity, 16), capacity), :
    ]
    issue(2)

    for made in gain_moves:
        made.landed()
    total_gain = gains[0]
    for at in range(1, count):
        total_gain = total_gain + gains[at]
    gain_sum[...] = total_gain

    hidden = x_ref[...].astype(F32)
    norm_self = rms_rows(hidden, gain_sum[0:1, :])
    forward(0)
    forward(1)
    issue(3)
    complete(0)
    complete(1)
    slot_fills = []
    for made, at in zip(slot_moves, (right, left, far)):
        made.landed()
        src = slots.at[slot_rows(at, t)]
        slot_fills.append(links.move(src, src, to_tp, slots.at[slot_rows(at, 1 - t)]).start())
    ready(0)
    q[...] = dot_nn(norm_self, wa[0]).astype(BF)
    k[...] = dot_nn(norm_self, wa[1]).astype(BF)
    ready(1)
    v[...] = dot_nn(norm_self, wa[2]).astype(BF)
    forward(2)
    issue(4)
    length = len_ref[g * count + w]
    query_at = lax.broadcasted_iota(jnp.int32, (2 * rows, rows), 0)
    query_at = jnp.where(query_at >= rows, query_at - rows, query_at)
    key_at = lax.broadcasted_iota(jnp.int32, (2 * rows, rows), 1)
    allowed_self = (key_at <= query_at) & (key_at < length)
    pairs = q.shape[1] // (2 * HEAD_DIM)
    attention_forward(pairs, q, k, v, ps, sc, allowed_self)

    def exchange_start(n):
        return links.move(part_out.at[n], part_in.at[n], to_tp, part_in.at[n]).start()

    def exchanged(n, made):
        made.landed()
        return part_out[n].astype(F32) + part_in[n].astype(F32)

    part_out[0] = dot_nt(sc[...], wa[3]).astype(BF)
    swap = exchange_start(0)
    complete(2)
    forward(3)
    issue(5)
    for made in slot_fills:
        made.landed()
    ready(2)
    mk[...] = dot_nn(slots[...], wa[4]).astype(BF)
    mv[...] = dot_nn(slots[...], wa[5]).astype(BF)
    complete(3)
    counts = jnp.sum(jnp.where(readers == w, 1.0, 0.0), axis=1, keepdims=True)
    slot_lane = lax.broadcasted_iota(jnp.int32, (count, slots.shape[0]), 1)
    slot_holder = lax.broadcasted_iota(jnp.int32, (count, slots.shape[0]), 0)
    slot_place = slot_lane - slot_holder * capacity
    filled = (slot_place >= 0) & (slot_place < capacity) & (slot_place.astype(F32) < counts)
    valid_slot = jnp.sum(jnp.where(filled, 1.0, 0.0), axis=0, keepdims=True)
    allowed_cross = jnp.broadcast_to(valid_slot, (2 * rows, slots.shape[0])) > 0.5
    one[...] = hidden + exchanged(0, swap)
    norm_cross = rms_rows(one[...], gain_sum[1:2, :])
    ready(3)
    cq[...] = dot_nn(norm_cross, wa[6]).astype(BF)
    attention_forward(pairs, cq, mk, mv, pc, cc, allowed_cross)
    part_out[1] = dot_nt(cc[...], wa[7]).astype(BF)
    swap = exchange_start(1)
    copies.save(wa, wa_o)
    for src, dst in ((q, q_o), (k, k_o), (v, v_o), (sc, sc_o), (ps, ps_o), (mk, mk_o), (mv, mv_o), (cq, cq_o), (cc, cc_o), (pc, pc_o), (slots, sel_o), (one, one_o), (gain_sum, gain_o)):
        copies.save(src, dst)
    forward(4)
    complete(4)
    forward(5)
    complete(5)
    two[...] = one[...] + exchanged(1, swap)
    copies.save(two, two_o)
    norm_ff = rms_rows(two[...], gain_sum[2:3, :])
    ready(4)
    copies.save(wgu, wgu_o)
    ga[...] = dot_nn(norm_ff, wgu[0]).astype(BF)
    up[...] = dot_nn(norm_ff, wgu[1]).astype(BF)
    copies.save(ga, ga_o)
    copies.save(up, up_o)
    ff_hidden = (smooth_gate(ga[...].astype(F32)) * up[...].astype(F32)).astype(BF)
    ready(5)
    copies.save(wd, wd_o)
    part_out[2] = (
        dot_nt(ff_hidden[:, :wide_cols], wd[0]) + dot_nt(ff_hidden[:, wide_cols:], wd[1])
    ).astype(BF)
    swap = exchange_start(2)
    three[...] = two[...] + exchanged(2, swap)
    block[...] = three[...].astype(BF)
    exit_rows[...] = rms_rows(three[...], gain_sum[3:4, :])
    copies.save(three, three_o)
    copies.save(block, block_o)
    copies.save(exit_rows, exit_o)
    links.finish()
    copies.finish()


def forward_layer(layer_input, memory, group_map, lengths, gain_rows, weights):
    count = group_map.shape[0]
    rows, width = layer_input.shape
    heads = weights[0].shape[1]
    units = weights[8].shape[1]
    slots = count * max(2, 2 * rows // count)
    pairs = heads // (2 * HEAD_DIM)
    kept = [
        ((rows, width), BF), ((rows, width), F32), ((rows, width), F32), ((rows, width), F32), ((rows, width), BF),
        ((rows, heads), BF), ((rows, heads), BF), ((rows, heads), BF), ((rows, heads), BF),
        ((slots, heads), BF), ((slots, heads), BF), ((rows, heads), BF), ((rows, heads), BF),
        ((pairs, 2 * rows, rows), BF), ((pairs, 2 * rows, slots), BF),
        ((rows, units), BF), ((rows, units), BF), ((slots, width), BF),
        ((8, width, heads), BF), ((2, width, units), BF), ((2, width, units // 2), BF), ((8, width), F32),
    ]
    vmem, hbm = pl.BlockSpec(memory_space=pltpu.VMEM), pl.BlockSpec(memory_space=pl.ANY)
    scratch = [
        pltpu.VMEM((8, width, heads), BF), pltpu.VMEM((2, width, units), BF), pltpu.VMEM((2, width, units // 2), BF),
        pltpu.VMEM((count, 8, width), F32), pltpu.VMEM((slots, width), BF), pltpu.VMEM((slots, width), BF),
        pltpu.VMEM((3, rows, width), BF), pltpu.VMEM((3, rows, width), BF),
    ]
    scratch += [pltpu.VMEM(shape, kind) for shape, kind in kept[:17]]
    scratch += [pltpu.VMEM((8, width), F32)]
    scratch += [pltpu.SemaphoreType.DMA((64,)), pltpu.SemaphoreType.DMA((64,)), pltpu.SemaphoreType.DMA((40,))]
    return pl.pallas_call(
        forward_kernel,
        out_shape=[jax.ShapeDtypeStruct(shape, kind) for shape, kind in kept],
        in_specs=[vmem, vmem, vmem, pl.BlockSpec(memory_space=pltpu.SMEM), vmem] + [hbm] * 11,
        out_specs=[hbm] * len(kept),
        scratch_shapes=scratch,
        compiler_params=pltpu.CompilerParams(
            collective_id=0, has_side_effects=True, vmem_limit_bytes=48 << 20
        ),
        name="forward_layer",
    )(layer_input, memory, group_map, lengths, gain_rows, *weights)


def saved_attend_backward(queries, keys, values, context_grad, probs):
    factor = HEAD_DIM ** (-0.5)
    rows = queries.shape[0]

    def one_head(parts):
        query, key_rows, value_rows, grad_rows, soft_bf = parts
        soft = soft_bf.astype(jnp.float32)
        soft_grad = project_back(grad_rows, value_rows)
        score_grad = (soft * (soft_grad - jnp.sum(soft * soft_grad, axis=1, keepdims=True))).astype(
            jnp.bfloat16
        )
        query_grad = project(score_grad, key_rows) * factor
        key_grad = outer_rows(score_grad, query) * factor
        value_grad = outer_rows(soft_bf, grad_rows)
        return (query_grad, key_grad, value_grad)

    grads = lax.map(
        one_head,
        (
            split_heads(queries),
            split_heads(keys),
            split_heads(values),
            split_heads(context_grad),
            probs.reshape(-1, rows, probs.shape[2]),
        ),
    )
    return (join_heads(grads[0]), join_heads(grads[1]), join_heads(grads[2]))


def fused_body(
    layer_input,
    memory,
    reader_map,
    target_ids,
    target_lengths,
    out_grad,
    self_q,
    self_k,
    self_v,
    self_o,
    cross_q,
    cross_k,
    cross_v,
    cross_o,
    ff_gate,
    ff_up,
    ff_out,
    gain_self,
    gain_cross,
    gain_ff,
    gain_exit,
    exit_table,
):
    wide_count = lax.axis_size("wide")
    wide_index = lax.axis_index("wide")
    seq_rows = layer_input.shape[0]
    group_index = lax.axis_index("grp")
    group_lengths = lax.dynamic_slice_in_dim(target_lengths, group_index * wide_count, wide_count)
    depth = gain_self.shape[0]
    stacked = jnp.stack([gain_self, gain_cross, gain_ff, gain_exit]).astype(jnp.float32)
    gain_rows = lax.dynamic_update_slice(
        jnp.zeros((8, wide_count * depth), jnp.float32), stacked, (0, wide_index * depth)
    )
    (
        block_output, resid_one, resid_two, resid_three, norm_exit, queries, keys, values, cross_queries,
        keys_read, values_read, context_self, context_cross, probs_self, probs_cross, gate_act, up_act, slots,
        attn_weights, gate_weights, down_weights, gains,
    ) = forward_layer(
        layer_input, memory, reader_map.reshape(wide_count, -1), target_lengths, gain_rows,
        (self_q, self_k, self_v, self_o, cross_q, cross_k, cross_v, cross_o, ff_gate, ff_up, ff_out),
    )
    w_query, w_key, w_value, w_output, c_key, c_value, c_query, c_output = attn_weights
    w_gate, w_up = gate_weights
    w_down = jnp.concatenate([down_weights[0], down_weights[1]], axis=1)
    gain_one, gain_two, gain_three, gain_last = gains[0], gains[1], gains[2], gains[3]
    hidden = layer_input.astype(jnp.float32)
    norm_self, unit_self, factor_self = normalize(hidden, gain_one)
    rows_each = memory.shape[0]
    capacity = max(2, 2 * rows_each // wide_count)
    slot_count = wide_count * capacity
    slot_valid, slot_target = read_slots(reader_map, wide_index, wide_count, rows_each, capacity)
    read_table = (
        jnp.zeros((slot_count,), jnp.int32)
        .at[slot_target]
        .set(lax.iota(jnp.int32, wide_count * rows_each), mode="drop")
    )
    norm_cross, unit_cross, factor_cross = normalize(resid_one, gain_two)
    norm_ff, unit_ff, factor_ff = normalize(resid_two, gain_three)
    up_float = up_act.astype(jnp.float32)
    gelu_value, gelu_pull = jax.vjp(smooth_gate, gate_act.astype(jnp.float32))
    ff_hidden = (gelu_value * up_float).astype(jnp.bfloat16)
    unit_exit, factor_exit = normalize(resid_three, gain_last)[1:]
    rows_all = lax.all_gather(norm_exit, "wide", axis=0, tiled=True)
    group_tokens = rows_all.shape[0]
    vocab_rows = exit_table.shape[0]
    scale_exit = float(rows_all.shape[1]) ** (-0.5)
    logits = project_back(rows_all, exit_table) * scale_exit
    vocab_ids = lax.axis_index(("wide", "tp")) * vocab_rows + lax.iota(jnp.int32, vocab_rows)
    is_target = target_ids[:, None] == vocab_ids[None, :]
    local_high = jnp.max(logits, axis=1)
    local_total = jnp.sum(jnp.exp(logits - local_high[:, None]), axis=1)
    local_pick = jnp.sum(jnp.where(is_target, logits, 0.0), axis=1)
    highest, total_exp, target_logit = merged(
        (local_high, local_total, local_pick), ("wide", "tp"), merge_softmax
    )
    log_total = highest + jnp.log(total_exp)
    token_place = lax.iota(jnp.int32, group_tokens)
    valid = token_place % seq_rows < jnp.repeat(
        group_lengths, seq_rows, total_repeat_length=group_tokens
    )
    token_count = jnp.sum(target_lengths).astype(jnp.float32)
    token_weight = jnp.where(valid, 1.0, 0.0).astype(jnp.float32) / token_count
    group_loss = jnp.sum(token_weight * (log_total - target_logit))
    logit_grad = (
        (jnp.exp(logits - log_total[:, None]) - jnp.where(is_target, 1.0, 0.0))
        * token_weight[:, None]
    ).astype(jnp.bfloat16)
    rows_grad_all = project(logit_grad, exit_table) * scale_exit
    exit_grad = outer_rows(logit_grad, rows_all) * scale_exit
    rows_part = lax.psum_scatter(
        rows_grad_all.astype(jnp.bfloat16), "wide", scatter_dimension=0, tiled=True
    )
    norm_exit_grad = lax.psum(rows_part, "tp").astype(jnp.float32)
    gain_exit_grad, back_exit = normalize_back(
        resid_three, unit_exit, factor_exit, gain_last, norm_exit_grad
    )
    resid_three_grad = out_grad.astype(jnp.float32) + back_exit
    ff_branch = resid_three_grad.astype(jnp.bfloat16)
    w_down_grad = outer_rows(ff_branch, ff_hidden)
    hidden_grad = project(ff_branch, w_down)
    gate_grad = gelu_pull(hidden_grad * up_float)[0].astype(jnp.bfloat16)
    up_grad = (hidden_grad * gelu_value).astype(jnp.bfloat16)
    w_gate_grad = outer_rows(norm_ff, gate_grad)
    w_up_grad = outer_rows(norm_ff, up_grad)
    norm_ff_grad = input_total(project_back(gate_grad, w_gate) + project_back(up_grad, w_up))
    gain_ff_grad, back_ff = normalize_back(resid_two, unit_ff, factor_ff, gain_three, norm_ff_grad)
    resid_two_grad = resid_three_grad + back_ff
    cross_branch = resid_two_grad.astype(jnp.bfloat16)
    c_output_grad = outer_rows(cross_branch, context_cross)
    cross_context_grad = project(cross_branch, c_output).astype(jnp.bfloat16)
    cross_query_grad, keys_grad_read, values_grad_read = saved_attend_backward(
        cross_queries, keys_read, values_read, cross_context_grad, probs_cross
    )
    empty_grads = jnp.zeros((wide_count * rows_each, keys_grad_read.shape[1]), jnp.float32)
    keys_grad_all = empty_grads.at[read_table].add(keys_grad_read)
    values_grad_all = empty_grads.at[read_table].add(values_grad_read)
    keys_grad, values_grad = (
        lax.psum_scatter(
            keys_grad_all.astype(jnp.bfloat16), "wide", scatter_dimension=0, tiled=True
        ).astype(jnp.float32),
        lax.psum_scatter(
            values_grad_all.astype(jnp.bfloat16), "wide", scatter_dimension=0, tiled=True
        ).astype(jnp.float32),
    )
    keys_grad = keys_grad.astype(jnp.bfloat16)
    values_grad = values_grad.astype(jnp.bfloat16)
    cross_query_grad = cross_query_grad.astype(jnp.bfloat16)
    c_query_grad = outer_rows(norm_cross, cross_query_grad)
    c_key_grad = outer_rows(memory, keys_grad)
    c_value_grad = outer_rows(memory, values_grad)
    norm_cross_grad, memory_grad = (
        lax.psum(project_back(cross_query_grad, c_query).astype(jnp.bfloat16), "tp").astype(
            jnp.float32
        ),
        lax.psum(
            (project_back(keys_grad, c_key) + project_back(values_grad, c_value)).astype(
                jnp.bfloat16
            ),
            "tp",
        ).astype(jnp.float32),
    )
    gain_cross_grad, back_cross = normalize_back(
        resid_one, unit_cross, factor_cross, gain_two, norm_cross_grad
    )
    resid_one_grad = resid_two_grad + back_cross
    self_branch = resid_one_grad.astype(jnp.bfloat16)
    w_output_grad = outer_rows(self_branch, context_self)
    self_context_grad = project(self_branch, w_output).astype(jnp.bfloat16)
    query_grad, key_grad, value_grad = saved_attend_backward(
        queries, keys, values, self_context_grad, probs_self
    )
    query_grad = query_grad.astype(jnp.bfloat16)
    key_grad = key_grad.astype(jnp.bfloat16)
    value_grad = value_grad.astype(jnp.bfloat16)
    w_query_grad = outer_rows(norm_self, query_grad)
    w_key_grad = outer_rows(norm_self, key_grad)
    w_value_grad = outer_rows(norm_self, value_grad)
    norm_self_grad = input_total(
        project_back(query_grad, w_query)
        + project_back(key_grad, w_key)
        + project_back(value_grad, w_value)
    )
    gain_self_grad, back_self = normalize_back(
        hidden, unit_self, factor_self, gain_one, norm_self_grad
    )
    input_grad = resid_one_grad + back_self
    shards = (
        lax.psum_scatter(
            w_query_grad.astype(jnp.bfloat16), "wide", scatter_dimension=0, tiled=True
        ).astype(jnp.float32),
        lax.psum_scatter(
            w_key_grad.astype(jnp.bfloat16), "wide", scatter_dimension=0, tiled=True
        ).astype(jnp.float32),
        lax.psum_scatter(
            w_value_grad.astype(jnp.bfloat16), "wide", scatter_dimension=0, tiled=True
        ).astype(jnp.float32),
        lax.psum_scatter(
            w_output_grad.astype(jnp.bfloat16), "wide", scatter_dimension=0, tiled=True
        ).astype(jnp.float32),
        lax.psum_scatter(
            c_query_grad.astype(jnp.bfloat16), "wide", scatter_dimension=0, tiled=True
        ).astype(jnp.float32),
        lax.psum_scatter(
            c_key_grad.astype(jnp.bfloat16), "wide", scatter_dimension=0, tiled=True
        ).astype(jnp.float32),
        lax.psum_scatter(
            c_value_grad.astype(jnp.bfloat16), "wide", scatter_dimension=0, tiled=True
        ).astype(jnp.float32),
        lax.psum_scatter(
            c_output_grad.astype(jnp.bfloat16), "wide", scatter_dimension=0, tiled=True
        ).astype(jnp.float32),
        lax.psum_scatter(
            w_gate_grad.astype(jnp.bfloat16), "wide", scatter_dimension=0, tiled=True
        ).astype(jnp.float32),
        lax.psum_scatter(
            w_up_grad.astype(jnp.bfloat16), "wide", scatter_dimension=0, tiled=True
        ).astype(jnp.float32),
        lax.psum_scatter(
            w_down_grad.astype(jnp.bfloat16), "wide", scatter_dimension=0, tiled=True
        ).astype(jnp.float32),
        lax.psum_scatter(
            gain_self_grad.astype(jnp.bfloat16), "wide", scatter_dimension=0, tiled=True
        ).astype(jnp.float32),
        lax.psum_scatter(
            gain_cross_grad.astype(jnp.bfloat16), "wide", scatter_dimension=0, tiled=True
        ).astype(jnp.float32),
        lax.psum_scatter(
            gain_ff_grad.astype(jnp.bfloat16), "wide", scatter_dimension=0, tiled=True
        ).astype(jnp.float32),
        lax.psum_scatter(
            gain_exit_grad.astype(jnp.bfloat16), "wide", scatter_dimension=0, tiled=True
        ).astype(jnp.float32),
    )
    totals = (
        lax.psum(shards[0].astype(jnp.bfloat16), "grp").astype(jnp.float32),
        lax.psum(shards[1].astype(jnp.bfloat16), "grp").astype(jnp.float32),
        lax.psum(shards[2].astype(jnp.bfloat16), "grp").astype(jnp.float32),
        lax.psum(shards[3].astype(jnp.bfloat16), "grp").astype(jnp.float32),
        lax.psum(shards[4].astype(jnp.bfloat16), "grp").astype(jnp.float32),
        lax.psum(shards[5].astype(jnp.bfloat16), "grp").astype(jnp.float32),
        lax.psum(shards[6].astype(jnp.bfloat16), "grp").astype(jnp.float32),
        lax.psum(shards[7].astype(jnp.bfloat16), "grp").astype(jnp.float32),
        lax.psum(shards[8].astype(jnp.bfloat16), "grp").astype(jnp.float32),
        lax.psum(shards[9].astype(jnp.bfloat16), "grp").astype(jnp.float32),
        lax.psum(shards[10].astype(jnp.bfloat16), "grp").astype(jnp.float32),
        lax.psum(shards[11].astype(jnp.bfloat16), "grp").astype(jnp.float32),
        lax.psum(shards[12].astype(jnp.bfloat16), "grp").astype(jnp.float32),
        lax.psum(shards[13].astype(jnp.bfloat16), "grp").astype(jnp.float32),
        lax.psum(shards[14].astype(jnp.bfloat16), "grp").astype(jnp.float32),
        lax.psum(exit_grad.astype(jnp.bfloat16), "grp").astype(jnp.float32),
        lax.psum(group_loss.astype(jnp.bfloat16), "grp").astype(jnp.float32),
    )
    return (
        block_output,
        totals[16],
        input_grad,
        memory_grad,
        totals[0],
        totals[1],
        totals[2],
        totals[3],
        totals[4],
        totals[5],
        totals[6],
        totals[7],
        totals[8],
        totals[9],
        totals[10],
        totals[11],
        totals[12],
        totals[13],
        totals[14],
        totals[15],
    )


def fits(mesh):
    return mesh.shape["wide"] == 4 and mesh.shape["tp"] == 2 and mesh.shape["grp"] == 4


def solution(mesh):
    placed = (
        P(("grp", "wide"), None),
        P(("grp", "wide"), None),
        P("grp"),
        P("grp"),
        P(),
        P(("grp", "wide"), None),
        P("wide", "tp"),
        P("wide", "tp"),
        P("wide", "tp"),
        P("wide", "tp"),
        P("wide", "tp"),
        P("wide", "tp"),
        P("wide", "tp"),
        P("wide", "tp"),
        P("wide", "tp"),
        P("wide", "tp"),
        P("wide", "tp"),
        P("wide"),
        P("wide"),
        P("wide"),
        P("wide"),
        P(("wide", "tp"), None),
    )
    return jax.shard_map(
        fused_body if fits(mesh) else plain_body,
        mesh=mesh,
        in_specs=placed,
        out_specs=(
            P(("grp", "wide"), None),
            P(),
            P(("grp", "wide"), None),
            P(("grp", "wide"), None),
            P("wide", "tp"),
            P("wide", "tp"),
            P("wide", "tp"),
            P("wide", "tp"),
            P("wide", "tp"),
            P("wide", "tp"),
            P("wide", "tp"),
            P("wide", "tp"),
            P("wide", "tp"),
            P("wide", "tp"),
            P("wide", "tp"),
            P("wide"),
            P("wide"),
            P("wide"),
            P("wide"),
            P(("wide", "tp"), None),
        ),
        check_vma=False,
    )
```

```python
import functools
import types

import jax
import jax.numpy as jnp
from jax import lax
from jax.experimental import pallas as pl
from jax.experimental.pallas import tpu as pltpu
from jax.sharding import PartitionSpec as P

HEAD_DIM = 64


EPSILON = 1e-06
MASKED = -1e30


def merged(shard, axis, combine):
    everything = jax.tree.map(
        lambda part, kind: lax.all_gather(part.astype(kind), axis),
        shard,
        (jnp.bfloat16, jnp.bfloat16, jnp.bfloat16),
    )

    def take(k):
        return jax.tree.map(lambda part, own: part[k].astype(own.dtype), everything, shard)

    return lax.fori_loop(
        1, lax.axis_size(axis), lambda k, so_far: combine(so_far, take(k)), take(0)
    )


def project(left, right):
    return jnp.dot(left, right, preferred_element_type=jnp.float32)


def project_back(left, right):
    return lax.dot_general(
        left, right, (((1,), (1,)), ((), ())), preferred_element_type=jnp.float32
    )


def outer_rows(left, right):
    return lax.dot_general(
        left, right, (((0,), (0,)), ((), ())), preferred_element_type=jnp.float32
    )


def smooth_gate(values):
    return jax.nn.gelu(values, approximate=True)


def normalize(values, gain):
    factor = lax.rsqrt(jnp.mean(values * values, axis=1, keepdims=True) + EPSILON)
    unit_rows = values * factor
    return ((unit_rows * gain).astype(jnp.bfloat16), unit_rows, factor)


def normalize_back(values, unit_rows, factor, gain, grad_rows):
    gain_grad = jnp.sum(grad_rows * unit_rows, axis=0)
    scaled = grad_rows * gain
    inner = jnp.mean(scaled * values, axis=1, keepdims=True)
    return (gain_grad, factor * scaled - unit_rows * factor * factor * inner)


def split_heads(values):
    return values.reshape(values.shape[0], -1, HEAD_DIM).transpose(1, 0, 2)


def join_heads(values):
    return values.transpose(1, 0, 2).reshape(values.shape[1], -1)


def read_slots(group_map, reader, holders, rows_each, capacity):
    matched = (group_map.reshape(holders, rows_each) == reader).astype(jnp.int32)
    ranks = jnp.cumsum(matched, axis=1) - 1
    counts = jnp.sum(matched, axis=1)
    place = lax.iota(jnp.int32, holders * capacity)
    valid = place % capacity < jnp.repeat(counts, capacity, total_repeat_length=holders * capacity)
    anchor = lax.iota(jnp.int32, holders)[:, None] * capacity + ranks
    target = jnp.where(matched > 0, anchor, holders * capacity)
    return (valid, target.reshape(-1))


def attend_forward(queries, keys, values, allowed):
    factor = HEAD_DIM ** (-0.5)

    def one_head(parts):
        query, key_rows, value_rows = parts
        scores = jnp.where(allowed, project_back(query, key_rows) * factor, MASKED)
        highest = jnp.max(scores, axis=1, keepdims=True)
        exponent = jnp.exp(scores - highest)
        total = jnp.sum(exponent, axis=1, keepdims=True)
        soft_weights = (exponent / total).astype(jnp.bfloat16)
        return (project(soft_weights, value_rows), (highest + jnp.log(total))[:, 0])

    context, log_total = lax.map(
        one_head, (split_heads(queries), split_heads(keys), split_heads(values))
    )
    return (join_heads(context).astype(jnp.bfloat16), log_total)


def attend_backward(queries, keys, values, context_grad, log_total, allowed):
    factor = HEAD_DIM ** (-0.5)

    def one_head(parts):
        query, key_rows, value_rows, grad_rows, log_row = parts
        scores = jnp.where(allowed, project_back(query, key_rows) * factor, MASKED)
        soft = jnp.exp(scores - log_row[:, None])
        soft_grad = project_back(grad_rows, value_rows)
        score_grad = (soft * (soft_grad - jnp.sum(soft * soft_grad, axis=1, keepdims=True))).astype(
            jnp.bfloat16
        )
        query_grad = project(score_grad, key_rows) * factor
        key_grad = outer_rows(score_grad, query) * factor
        value_grad = outer_rows(soft.astype(jnp.bfloat16), grad_rows)
        return (query_grad, key_grad, value_grad)

    grads = lax.map(
        one_head,
        (
            split_heads(queries),
            split_heads(keys),
            split_heads(values),
            split_heads(context_grad),
            log_total,
        ),
    )
    return (join_heads(grads[0]), join_heads(grads[1]), join_heads(grads[2]))


def heads_total(partial_rows):
    return lax.psum(partial_rows, "tp")


def input_total(partial_rows):
    return lax.psum(partial_rows.astype(jnp.bfloat16), "tp").astype(jnp.float32)


def merge_softmax(first, second):
    highest = jnp.maximum(first[0], second[0])
    total = first[1] * jnp.exp(first[0] - highest) + second[1] * jnp.exp(second[0] - highest)
    return (highest, total, first[2] + second[2])


def plain_body(
    layer_input,
    memory,
    reader_map,
    target_ids,
    target_lengths,
    out_grad,
    self_q,
    self_k,
    self_v,
    self_o,
    cross_q,
    cross_k,
    cross_v,
    cross_o,
    ff_gate,
    ff_up,
    ff_out,
    gain_self,
    gain_cross,
    gain_ff,
    gain_exit,
    exit_table,
):
    (
        w_query,
        w_key,
        w_value,
        w_output,
        c_query,
        c_key,
        c_value,
        c_output,
        w_gate,
        w_up,
        w_down,
        full_gain_self,
        full_gain_cross,
        full_gain_ff,
        full_gain_exit,
    ) = (
        lax.all_gather(self_q, "wide", axis=0, tiled=True),
        lax.all_gather(self_k, "wide", axis=0, tiled=True),
        lax.all_gather(self_v, "wide", axis=0, tiled=True),
        lax.all_gather(self_o, "wide", axis=0, tiled=True),
        lax.all_gather(cross_q, "wide", axis=0, tiled=True),
        lax.all_gather(cross_k, "wide", axis=0, tiled=True),
        lax.all_gather(cross_v, "wide", axis=0, tiled=True),
        lax.all_gather(cross_o, "wide", axis=0, tiled=True),
        lax.all_gather(ff_gate, "wide", axis=0, tiled=True),
        lax.all_gather(ff_up, "wide", axis=0, tiled=True),
        lax.all_gather(ff_out, "wide", axis=0, tiled=True),
        lax.all_gather(gain_self, "wide", axis=0, tiled=True),
        lax.all_gather(gain_cross, "wide", axis=0, tiled=True),
        lax.all_gather(gain_ff, "wide", axis=0, tiled=True),
        lax.all_gather(gain_exit, "wide", axis=0, tiled=True),
    )
    gain_one = full_gain_self.astype(jnp.float32)
    gain_two = full_gain_cross.astype(jnp.float32)
    gain_three = full_gain_ff.astype(jnp.float32)
    gain_last = full_gain_exit.astype(jnp.float32)
    seq_rows = layer_input.shape[0]
    wide_count = lax.axis_size("wide")
    wide_index = lax.axis_index("wide")
    group_index = lax.axis_index("grp")
    group_lengths = lax.dynamic_slice_in_dim(target_lengths, group_index * wide_count, wide_count)
    own_length = lax.dynamic_index_in_dim(group_lengths, wide_index, keepdims=False)
    hidden = layer_input.astype(jnp.float32)
    norm_self, unit_self, factor_self = normalize(hidden, gain_one)
    queries = project(norm_self, w_query).astype(jnp.bfloat16)
    keys = project(norm_self, w_key).astype(jnp.bfloat16)
    values = project(norm_self, w_value).astype(jnp.bfloat16)
    position = lax.iota(jnp.int32, seq_rows)
    allowed_self = (position[None, :] <= position[:, None]) & (position[None, :] < own_length)
    context_self, log_self = attend_forward(queries, keys, values, allowed_self)
    resid_one = hidden + heads_total(project_back(context_self, w_output))
    norm_cross, unit_cross, factor_cross = normalize(resid_one, gain_two)
    cross_queries = project(norm_cross, c_query).astype(jnp.bfloat16)
    memory_keys = project(memory, c_key).astype(jnp.bfloat16)
    memory_values = project(memory, c_value).astype(jnp.bfloat16)
    rows_each = memory.shape[0]
    capacity = max(2, 2 * rows_each // wide_count)
    slot_count = wide_count * capacity
    slot_valid, slot_target = read_slots(reader_map, wide_index, wide_count, rows_each, capacity)
    keys_all, values_all = (
        lax.all_gather(memory_keys, "wide", axis=0, tiled=True),
        lax.all_gather(memory_values, "wide", axis=0, tiled=True),
    )
    read_table = (
        jnp.zeros((slot_count,), jnp.int32)
        .at[slot_target]
        .set(lax.iota(jnp.int32, wide_count * rows_each), mode="drop")
    )
    keys_read = jnp.take(keys_all, read_table, axis=0)
    values_read = jnp.take(values_all, read_table, axis=0)
    allowed_cross = slot_valid[None, :]
    context_cross, log_cross = attend_forward(cross_queries, keys_read, values_read, allowed_cross)
    resid_two = resid_one + heads_total(project_back(context_cross, c_output))
    norm_ff, unit_ff, factor_ff = normalize(resid_two, gain_three)
    gate_float = project(norm_ff, w_gate).astype(jnp.bfloat16).astype(jnp.float32)
    up_float = project(norm_ff, w_up).astype(jnp.bfloat16).astype(jnp.float32)
    gelu_value, gelu_pull = jax.vjp(smooth_gate, gate_float)
    ff_hidden = (gelu_value * up_float).astype(jnp.bfloat16)
    resid_three = resid_two + heads_total(project_back(ff_hidden, w_down))
    block_output = resid_three.astype(jnp.bfloat16)
    norm_exit, unit_exit, factor_exit = normalize(resid_three, gain_last)
    rows_all = lax.all_gather(norm_exit, "wide", axis=0, tiled=True)
    group_tokens = rows_all.shape[0]
    vocab_rows = exit_table.shape[0]
    scale_exit = float(rows_all.shape[1]) ** (-0.5)
    logits = project_back(rows_all, exit_table) * scale_exit
    vocab_ids = lax.axis_index(("wide", "tp")) * vocab_rows + lax.iota(jnp.int32, vocab_rows)
    is_target = target_ids[:, None] == vocab_ids[None, :]
    local_high = jnp.max(logits, axis=1)
    local_total = jnp.sum(jnp.exp(logits - local_high[:, None]), axis=1)
    local_pick = jnp.sum(jnp.where(is_target, logits, 0.0), axis=1)
    highest, total_exp, target_logit = merged(
        (local_high, local_total, local_pick), ("wide", "tp"), merge_softmax
    )
    log_total = highest + jnp.log(total_exp)
    token_place = lax.iota(jnp.int32, group_tokens)
    valid = token_place % seq_rows < jnp.repeat(
        group_lengths, seq_rows, total_repeat_length=group_tokens
    )
    token_count = jnp.sum(target_lengths).astype(jnp.float32)
    token_weight = jnp.where(valid, 1.0, 0.0).astype(jnp.float32) / token_count
    group_loss = jnp.sum(token_weight * (log_total - target_logit))
    logit_grad = (
        (jnp.exp(logits - log_total[:, None]) - jnp.where(is_target, 1.0, 0.0))
        * token_weight[:, None]
    ).astype(jnp.bfloat16)
    rows_grad_all = project(logit_grad, exit_table) * scale_exit
    exit_grad = outer_rows(logit_grad, rows_all) * scale_exit
    rows_part = lax.psum_scatter(
        rows_grad_all.astype(jnp.bfloat16), "wide", scatter_dimension=0, tiled=True
    )
    norm_exit_grad = lax.psum(rows_part, "tp").astype(jnp.float32)
    gain_exit_grad, back_exit = normalize_back(
        resid_three, unit_exit, factor_exit, gain_last, norm_exit_grad
    )
    resid_three_grad = out_grad.astype(jnp.float32) + back_exit
    ff_branch = resid_three_grad.astype(jnp.bfloat16)
    w_down_grad = outer_rows(ff_branch, ff_hidden)
    hidden_grad = project(ff_branch, w_down)
    gate_grad = gelu_pull(hidden_grad * up_float)[0].astype(jnp.bfloat16)
    up_grad = (hidden_grad * gelu_value).astype(jnp.bfloat16)
    w_gate_grad = outer_rows(norm_ff, gate_grad)
    w_up_grad = outer_rows(norm_ff, up_grad)
    norm_ff_grad = input_total(project_back(gate_grad, w_gate) + project_back(up_grad, w_up))
    gain_ff_grad, back_ff = normalize_back(resid_two, unit_ff, factor_ff, gain_three, norm_ff_grad)
    resid_two_grad = resid_three_grad + back_ff
    cross_branch = resid_two_grad.astype(jnp.bfloat16)
    c_output_grad = outer_rows(cross_branch, context_cross)
    cross_context_grad = project(cross_branch, c_output).astype(jnp.bfloat16)
    cross_query_grad, keys_grad_read, values_grad_read = attend_backward(
        cross_queries, keys_read, values_read, cross_context_grad, log_cross, allowed_cross
    )
    empty_grads = jnp.zeros((wide_count * rows_each, keys_grad_read.shape[1]), jnp.float32)
    keys_grad_all = empty_grads.at[read_table].add(keys_grad_read)
    values_grad_all = empty_grads.at[read_table].add(values_grad_read)
    keys_grad, values_grad = (
        lax.psum_scatter(
            keys_grad_all.astype(jnp.bfloat16), "wide", scatter_dimension=0, tiled=True
        ).astype(jnp.float32),
        lax.psum_scatter(
            values_grad_all.astype(jnp.bfloat16), "wide", scatter_dimension=0, tiled=True
        ).astype(jnp.float32),
    )
    keys_grad = keys_grad.astype(jnp.bfloat16)
    values_grad = values_grad.astype(jnp.bfloat16)
    cross_query_grad = cross_query_grad.astype(jnp.bfloat16)
    c_query_grad = outer_rows(norm_cross, cross_query_grad)
    c_key_grad = outer_rows(memory, keys_grad)
    c_value_grad = outer_rows(memory, values_grad)
    norm_cross_grad, memory_grad = (
        lax.psum(project_back(cross_query_grad, c_query).astype(jnp.bfloat16), "tp").astype(
            jnp.float32
        ),
        lax.psum(
            (project_back(keys_grad, c_key) + project_back(values_grad, c_value)).astype(
                jnp.bfloat16
            ),
            "tp",
        ).astype(jnp.float32),
    )
    gain_cross_grad, back_cross = normalize_back(
        resid_one, unit_cross, factor_cross, gain_two, norm_cross_grad
    )
    resid_one_grad = resid_two_grad + back_cross
    self_branch = resid_one_grad.astype(jnp.bfloat16)
    w_output_grad = outer_rows(self_branch, context_self)
    self_context_grad = project(self_branch, w_output).astype(jnp.bfloat16)
    query_grad, key_grad, value_grad = attend_backward(
        queries, keys, values, self_context_grad, log_self, allowed_self
    )
    query_grad = query_grad.astype(jnp.bfloat16)
    key_grad = key_grad.astype(jnp.bfloat16)
    value_grad = value_grad.astype(jnp.bfloat16)
    w_query_grad = outer_rows(norm_self, query_grad)
    w_key_grad = outer_rows(norm_self, key_grad)
    w_value_grad = outer_rows(norm_self, value_grad)
    norm_self_grad = input_total(
        project_back(query_grad, w_query)
        + project_back(key_grad, w_key)
        + project_back(value_grad, w_value)
    )
    gain_self_grad, back_self = normalize_back(
        hidden, unit_self, factor_self, gain_one, norm_self_grad
    )
    input_grad = resid_one_grad + back_self
    shards = (
        lax.psum_scatter(
            w_query_grad.astype(jnp.bfloat16), "wide", scatter_dimension=0, tiled=True
        ).astype(jnp.float32),
        lax.psum_scatter(
            w_key_grad.astype(jnp.bfloat16), "wide", scatter_dimension=0, tiled=True
        ).astype(jnp.float32),
        lax.psum_scatter(
            w_value_grad.astype(jnp.bfloat16), "wide", scatter_dimension=0, tiled=True
        ).astype(jnp.float32),
        lax.psum_scatter(
            w_output_grad.astype(jnp.bfloat16), "wide", scatter_dimension=0, tiled=True
        ).astype(jnp.float32),
        lax.psum_scatter(
            c_query_grad.astype(jnp.bfloat16), "wide", scatter_dimension=0, tiled=True
        ).astype(jnp.float32),
        lax.psum_scatter(
            c_key_grad.astype(jnp.bfloat16), "wide", scatter_dimension=0, tiled=True
        ).astype(jnp.float32),
        lax.psum_scatter(
            c_value_grad.astype(jnp.bfloat16), "wide", scatter_dimension=0, tiled=True
        ).astype(jnp.float32),
        lax.psum_scatter(
            c_output_grad.astype(jnp.bfloat16), "wide", scatter_dimension=0, tiled=True
        ).astype(jnp.float32),
        lax.psum_scatter(
            w_gate_grad.astype(jnp.bfloat16), "wide", scatter_dimension=0, tiled=True
        ).astype(jnp.float32),
        lax.psum_scatter(
            w_up_grad.astype(jnp.bfloat16), "wide", scatter_dimension=0, tiled=True
        ).astype(jnp.float32),
        lax.psum_scatter(
            w_down_grad.astype(jnp.bfloat16), "wide", scatter_dimension=0, tiled=True
        ).astype(jnp.float32),
        lax.psum_scatter(
            gain_self_grad.astype(jnp.bfloat16), "wide", scatter_dimension=0, tiled=True
        ).astype(jnp.float32),
        lax.psum_scatter(
            gain_cross_grad.astype(jnp.bfloat16), "wide", scatter_dimension=0, tiled=True
        ).astype(jnp.float32),
        lax.psum_scatter(
            gain_ff_grad.astype(jnp.bfloat16), "wide", scatter_dimension=0, tiled=True
        ).astype(jnp.float32),
        lax.psum_scatter(
            gain_exit_grad.astype(jnp.bfloat16), "wide", scatter_dimension=0, tiled=True
        ).astype(jnp.float32),
    )
    totals = (
        lax.psum(shards[0].astype(jnp.bfloat16), "grp").astype(jnp.float32),
        lax.psum(shards[1].astype(jnp.bfloat16), "grp").astype(jnp.float32),
        lax.psum(shards[2].astype(jnp.bfloat16), "grp").astype(jnp.float32),
        lax.psum(shards[3].astype(jnp.bfloat16), "grp").astype(jnp.float32),
        lax.psum(shards[4].astype(jnp.bfloat16), "grp").astype(jnp.float32),
        lax.psum(shards[5].astype(jnp.bfloat16), "grp").astype(jnp.float32),
        lax.psum(shards[6].astype(jnp.bfloat16), "grp").astype(jnp.float32),
        lax.psum(shards[7].astype(jnp.bfloat16), "grp").astype(jnp.float32),
        lax.psum(shards[8].astype(jnp.bfloat16), "grp").astype(jnp.float32),
        lax.psum(shards[9].astype(jnp.bfloat16), "grp").astype(jnp.float32),
        lax.psum(shards[10].astype(jnp.bfloat16), "grp").astype(jnp.float32),
        lax.psum(shards[11].astype(jnp.bfloat16), "grp").astype(jnp.float32),
        lax.psum(shards[12].astype(jnp.bfloat16), "grp").astype(jnp.float32),
        lax.psum(shards[13].astype(jnp.bfloat16), "grp").astype(jnp.float32),
        lax.psum(shards[14].astype(jnp.bfloat16), "grp").astype(jnp.float32),
        lax.psum(exit_grad.astype(jnp.bfloat16), "grp").astype(jnp.float32),
        lax.psum(group_loss.astype(jnp.bfloat16), "grp").astype(jnp.float32),
    )
    return (
        block_output,
        totals[16],
        input_grad,
        memory_grad,
        totals[0],
        totals[1],
        totals[2],
        totals[3],
        totals[4],
        totals[5],
        totals[6],
        totals[7],
        totals[8],
        totals[9],
        totals[10],
        totals[11],
        totals[12],
        totals[13],
        totals[14],
        totals[15],
    )


MESH = pl.DeviceIdType.MESH
BF = jnp.bfloat16
F32 = jnp.float32
VMEM_BYTES = 63 << 20


def dot_nn(left, right):
    return lax.dot_general(left, right, (((1,), (0,)), ((), ())), preferred_element_type=F32)


def dot_nt(left, right):
    return lax.dot_general(left, right, (((1,), (1,)), ((), ())), preferred_element_type=F32)


def dot_tn(left, right):
    return lax.dot_general(left, right, (((0,), (0,)), ((), ())), preferred_element_type=F32)


class Move:
    def __init__(self, out, arrival):
        self.out, self.arrival = out, arrival

    def start(self):
        self.out.start()
        return self

    def sent(self):
        self.out.wait_send()

    def landed(self):
        self.arrival.wait_recv()


class Links:
    def __init__(self, send_sems, recv_sems):
        self.send_sems, self.recv_sems = send_sems, recv_sems
        self.used = 0
        self.moves = []

    def move(self, src, dst, device, lands):
        k = self.used
        self.used += 1
        out = pltpu.make_async_remote_copy(
            src_ref=src, dst_ref=dst, send_sem=self.send_sems.at[k], recv_sem=self.recv_sems.at[k],
            device_id=device, device_id_type=MESH,
        )
        arrival = pltpu.make_async_remote_copy(
            src_ref=lands, dst_ref=lands, send_sem=self.send_sems.at[k], recv_sem=self.recv_sems.at[k],
            device_id=device, device_id_type=MESH,
        )
        made = Move(out, arrival)
        self.moves.append(made)
        return made

    def finish(self):
        for made in self.moves:
            made.sent()

    def finish_rest(self, done):
        for made in self.moves:
            if made not in done:
                made.sent()


class Copies:
    def __init__(self, sems):
        self.sems, self.used, self.pending = sems, 0, []

    def start(self, src, dst):
        made = pltpu.make_async_copy(src, dst, self.sems.at[self.used])
        self.used += 1
        made.start()
        return made

    def save(self, src, dst):
        self.pending.append(self.start(src, dst))

    def finish(self):
        for made in self.pending:
            made.wait()


def greet(devices):
    barrier = pltpu.get_barrier_semaphore()
    for device in devices:
        pl.semaphore_signal(barrier, inc=1, device_id=device, device_id_type=MESH)
    pl.semaphore_wait(barrier, len(devices))


def position(count):
    g, w, t = lax.axis_index("grp"), lax.axis_index("wide"), lax.axis_index("tp")
    c = lax.rem(g, 2)
    left, right, far = (lax.rem(w + d, count) for d in (count - 1, 1, 2))
    return types.SimpleNamespace(
        count=count, g=g, w=w, t=t, c=c, yy=lax.div(g, 2), left=left, right=right, far=far,
        to_left={"wide": left}, to_right={"wide": right}, to_far={"wide": far},
        to_core={"grp": g + 1 - 2 * c}, to_y={"grp": lax.rem(g + 2, 4)}, to_tp={"tp": 1 - t},
    )


def rms_rows(values, gain):
    factor = lax.rsqrt(jnp.mean(values * values, axis=1, keepdims=True) + EPSILON)
    return (values * factor * gain).astype(BF)


def lane_masks():
    lane = lax.broadcasted_iota(jnp.int32, (1, 2 * HEAD_DIM), 1)
    low = jnp.where(lane < HEAD_DIM, 1.0, 0.0).astype(F32)
    return low.astype(BF), (1.0 - low).astype(BF)


def both_heads(pair):
    low, high = lane_masks()
    return jnp.concatenate([pair * low, pair * high], axis=0)


def pick_heads(stacked):
    rows = stacked.shape[0] // 2
    lane = lax.broadcasted_iota(jnp.int32, (rows, 2 * HEAD_DIM), 1)
    return jnp.where(lane < HEAD_DIM, stacked[:rows], stacked[rows:])


def pair_columns(p):
    return pl.ds(pl.multiple_of(p * 2 * HEAD_DIM, 2 * HEAD_DIM), 2 * HEAD_DIM)


def attention_forward(pairs, queries, keys, values, probs, context, allowed):
    factor = HEAD_DIM ** (-0.5)

    def step(p, carry):
        cols = pair_columns(p)
        scores = dot_nt(both_heads(queries[:, cols]), keys[:, cols]) * factor
        scores = jnp.where(allowed, scores, MASKED)
        exponent = jnp.exp(scores - jnp.max(scores, axis=1, keepdims=True))
        soft = (exponent / jnp.sum(exponent, axis=1, keepdims=True)).astype(BF)
        probs[p] = soft
        context[:, cols] = pick_heads(dot_nn(soft, values[:, cols])).astype(BF)
        return carry

    lax.fori_loop(0, pairs, step, 0)


def slot_choice(own_map, slots, count):
    rows = own_map.shape[1]
    capacity = slots // count
    reader_iota = lax.broadcasted_iota(jnp.int32, (max(8, count), rows), 0)
    matched = jnp.where(reader_iota == own_map, 1.0, 0.0).astype(F32)
    before = lax.broadcasted_iota(jnp.int32, (rows, rows), 0) < lax.broadcasted_iota(jnp.int32, (rows, rows), 1)
    ranks = dot_nn(matched.astype(BF), jnp.where(before, 1.0, 0.0).astype(BF))
    rank = jnp.sum(matched * ranks, axis=0, keepdims=True).astype(jnp.int32)
    slot_iota = lax.broadcasted_iota(jnp.int32, (slots, rows), 0)
    return jnp.where(slot_iota == own_map * capacity + rank, 1.0, 0.0).astype(BF)


class Gather:
    def __init__(self, here, links, buf, first, depth, placed):
        self.here, self.links, self.buf, self.placed = here, links, buf, placed
        self.mine, self.other = first + here.c, first + 1 - here.c
        self.depth = depth

    def rows(self, at, start, parts):
        size = self.depth // parts
        return pl.ds(pl.multiple_of(at * self.depth + start * size, 16), size)

    def y_half(self, at):
        return self.rows(at, self.here.yy, 2)

    def quarter(self, at, which):
        return self.rows(at, 2 * self.here.yy + which, 4)

    def send(self, where, device, lands, index=None):
        src = self.buf.at[self.mine, where]
        land = self.buf.at[self.mine if index is None else index, lands]
        return self.links.move(src, src, device, land).start()

    def issue(self):
        here = self.here
        for made in self.placed:
            made.wait()
        own = self.y_half(here.w)
        self.from_left = self.send(own, here.to_right, self.y_half(here.left))
        self.from_right = self.send(own, here.to_left, self.y_half(here.right))

    def to_y(self, at):
        return self.send(self.y_half(at), self.here.to_y, self.rows(at, 1 - self.here.yy, 2))

    def forward(self):
        here = self.here
        self.from_left.landed()
        self.far_top = self.send(self.quarter(here.left, 0), here.to_right, self.quarter(here.far, 0))
        self.over_y = [self.to_y(here.left)]
        self.from_right.landed()
        self.far_low = self.send(self.quarter(here.right, 1), here.to_left, self.quarter(here.far, 1))
        self.over_y.append(self.to_y(here.right))

    def complete(self):
        self.far_top.landed()
        self.far_low.landed()
        self.over_y.append(self.to_y(self.here.far))

    def share(self):
        here = self.here
        self.cores = []
        for made, at in zip(self.over_y, (here.left, here.right, here.far)):
            made.landed()
            whole = self.rows(at, 0, 1)
            self.cores.append(self.send(whole, here.to_core, whole, self.other))

    def ready(self):
        for made in self.cores:
            made.landed()


def forward_kernel(
    count, x_ref, mem_ref, map_ref, len_ref, gs_ref, gc_ref, gf_ref, ge_ref,
    q_in, k_in, v_in, so_in, cq_in, ck_in, cv_in, co_in, ga_in, up_in, dn_in,
    block_o, one_o, two_o, three_o, exit_o, q_o, k_o, v_o, cq_o, mk_o, mv_o, sc_o, cc_o, ps_o, pc_o,
    ga_o, up_o, sel_o, wa_o, wgu_o, wd_o, gain_o,
    wa, wgu, wd, gains, slots, packed, part_out, part_in, valid_slot,
    block, one, two, three, exit_rows, q, k, v, cq, mk, mv, sc, cc, ps, pc, ga, up, gain_sum,
    send_sems, recv_sems, copy_sems,
):
    here = position(count)
    g, w, t = here.g, here.w, here.t
    left, right, far = here.left, here.right, here.far
    to_left, to_right, to_far, to_tp = here.to_left, here.to_right, here.to_far, here.to_tp
    rows = x_ref.shape[0]
    links, copies = Links(send_sems, recv_sems), Copies(copy_sems)
    depth = q_in.shape[0]
    wide_cols = dn_in.shape[1] // 2

    own = pl.ds(pl.multiple_of(w * depth, 16), depth)
    order = (q_in, k_in, v_in, so_in, ck_in, cv_in, cq_in, co_in)
    weights = []
    for j in range(4):
        placed = [copies.start(order[2 * j + e], wa.at[2 * j + e, own]) for e in range(2)]
        weights.append(Gather(here, links, wa, 2 * j, depth, placed))
    placed = [copies.start(ref, wgu.at[e, own]) for e, ref in enumerate((ga_in, up_in))]
    weights.append(Gather(here, links, wgu, 0, depth, placed))
    placed = [copies.start(dn_in.at[:, pl.ds(e * wide_cols, wide_cols)], wd.at[e, own]) for e in range(2)]
    weights.append(Gather(here, links, wd, 0, depth, placed))

    gain_sum[...] = jnp.zeros_like(gain_sum)
    for n, ref in enumerate((gs_ref, gc_ref, gf_ref, ge_ref)):
        gain_sum[n : n + 1, 0:depth] = ref[...].astype(F32)
    gains[w] = pltpu.roll(gain_sum[...], w * depth, 1)
    greet([to_left, to_right, to_far, here.to_core, here.to_y, to_tp])
    gain_moves = [
        links.move(gains.at[w], gains.at[w], device, gains.at[at]).start()
        for device, at in ((to_left, right), (to_right, left), (to_far, far))
    ]
    weights[0].issue()
    weights[1].issue()

    capacity = slots.shape[0] // count
    choose = slot_choice(map_ref[:, pl.ds(pl.multiple_of(w * rows, rows), rows)], slots.shape[0], count)
    packed[...] = dot_nn(choose, mem_ref[...]).astype(BF)

    def slot_rows(at, which):
        return pl.ds(pl.multiple_of(at * capacity + which * (capacity // 2), 16), capacity // 2)

    slot_moves = [
        links.move(packed.at[slot_rows(to, t)], slots.at[slot_rows(w, t)], device, slots.at[slot_rows(at, t)]).start()
        for device, to, at in ((to_left, left, right), (to_right, right, left), (to_far, far, far))
    ]
    own_slots = pl.ds(pl.multiple_of(w * capacity, 16), capacity)
    slots[own_slots, :] = packed[own_slots, :]
    weights[0].forward()
    weights[2].issue()

    for made in gain_moves:
        made.landed()
    total_gain = gains[0]
    for at in range(1, count):
        total_gain = total_gain + gains[at]
    gain_sum[...] = total_gain
    hidden = x_ref[...].astype(F32)
    norm_self = rms_rows(hidden, gain_sum[0:1, :])
    weights[1].forward()
    weights[0].complete()
    weights[3].issue()
    weights[0].share()
    weights[1].complete()
    weights[2].forward()
    weights[1].share()
    weights[4].issue()
    weights[0].ready()
    q[...] = dot_nn(norm_self, wa[0]).astype(BF)
    k[...] = dot_nn(norm_self, wa[1]).astype(BF)
    weights[2].complete()
    weights[1].ready()
    v[...] = dot_nn(norm_self, wa[2]).astype(BF)
    slot_fills = []
    for made, at in zip(slot_moves, (right, left, far)):
        made.landed()
        src = slots.at[slot_rows(at, t)]
        slot_fills.append(links.move(src, src, to_tp, slots.at[slot_rows(at, 1 - t)]).start())
    weights[3].forward()
    length = len_ref[g * count + w]
    query_at = lax.broadcasted_iota(jnp.int32, (2 * rows, rows), 0)
    query_at = jnp.where(query_at >= rows, query_at - rows, query_at)
    key_at = lax.broadcasted_iota(jnp.int32, (2 * rows, rows), 1)
    allowed_self = (key_at <= query_at) & (key_at < length)
    pairs = q.shape[1] // (2 * HEAD_DIM)
    attention_forward(pairs, q, k, v, ps, sc, allowed_self)

    def exchange_start(n):
        return links.move(part_out.at[n], part_in.at[n], to_tp, part_in.at[n]).start()

    def exchanged(n, made):
        made.landed()
        return part_out[n].astype(F32) + part_in[n].astype(F32)

    part_out[0] = dot_nt(sc[...], wa[3]).astype(BF)
    swap = exchange_start(0)
    weights[2].share()
    weights[5].issue()
    weights[3].complete()
    for made in slot_fills:
        made.landed()
    weights[3].share()
    place = lax.broadcasted_iota(jnp.int32, (1, capacity), 1).astype(F32)
    for b in range(count):
        reads = jnp.sum(jnp.where(map_ref[:, b * rows : (b + 1) * rows] == w, 1.0, 0.0), axis=1, keepdims=True)
        valid_slot[0:1, b * capacity : (b + 1) * capacity] = jnp.where(place < reads, 1.0, 0.0)
    weights[2].ready()
    mk[...] = dot_nn(slots[...], wa[4]).astype(BF)
    mv[...] = dot_nn(slots[...], wa[5]).astype(BF)
    weights[4].forward()
    allowed_cross = jnp.broadcast_to(valid_slot[0:1, :], (2 * rows, slots.shape[0])) > 0.5
    one[...] = hidden + exchanged(0, swap)
    norm_cross = rms_rows(one[...], gain_sum[1:2, :])
    weights[3].ready()
    cq[...] = dot_nn(norm_cross, wa[6]).astype(BF)
    weights[4].complete()
    attention_forward(pairs, cq, mk, mv, pc, cc, allowed_cross)
    part_out[1] = dot_nt(cc[...], wa[7]).astype(BF)
    swap = exchange_start(1)
    weights[4].share()
    weights[5].forward()
    weights[5].complete()
    weights[5].share()
    copies.save(wa, wa_o)
    for src, dst in (
        (q, q_o), (k, k_o), (v, v_o), (sc, sc_o), (ps, ps_o), (mk, mk_o), (mv, mv_o), (cq, cq_o), (cc, cc_o), (pc, pc_o),
        (slots, sel_o), (one, one_o), (gain_sum, gain_o),
    ):
        copies.save(src, dst)
    two[...] = one[...] + exchanged(1, swap)
    copies.save(two, two_o)
    norm_ff = rms_rows(two[...], gain_sum[2:3, :])
    weights[4].ready()
    copies.save(wgu, wgu_o)
    ga[...] = dot_nn(norm_ff, wgu[0]).astype(BF)
    up[...] = dot_nn(norm_ff, wgu[1]).astype(BF)
    copies.save(ga, ga_o)
    copies.save(up, up_o)
    ff_hidden = (smooth_gate(ga[...].astype(F32)) * up[...].astype(F32)).astype(BF)
    weights[5].ready()
    copies.save(wd, wd_o)
    part_out[2] = (
        dot_nt(ff_hidden[:, :wide_cols], wd[0]) + dot_nt(ff_hidden[:, wide_cols:], wd[1])
    ).astype(BF)
    swap = exchange_start(2)
    three[...] = two[...] + exchanged(2, swap)
    block[...] = three[...].astype(BF)
    exit_rows[...] = rms_rows(three[...], gain_sum[3:4, :])
    copies.save(three, three_o)
    copies.save(block, block_o)
    copies.save(exit_rows, exit_o)
    links.finish()
    copies.finish()


def forward_layer(count, layer_input, memory, group_map, lengths, gain_parts, weights):
    rows, width = layer_input.shape
    heads = weights[0].shape[1]
    units = weights[8].shape[1]
    slots = count * max(2, 2 * rows // count)
    pairs = heads // (2 * HEAD_DIM)
    kept = [
        ((rows, width), BF), ((rows, width), F32), ((rows, width), F32), ((rows, width), F32), ((rows, width), BF),
        ((rows, heads), BF), ((rows, heads), BF), ((rows, heads), BF), ((rows, heads), BF),
        ((slots, heads), BF), ((slots, heads), BF), ((rows, heads), BF), ((rows, heads), BF),
        ((pairs, 2 * rows, rows), BF), ((pairs, 2 * rows, slots), BF),
        ((rows, units), BF), ((rows, units), BF), ((slots, width), BF),
        ((8, width, heads), BF), ((2, width, units), BF), ((2, width, units // 2), BF), ((8, width), F32),
    ]
    vmem, hbm = pl.BlockSpec(memory_space=pltpu.VMEM), pl.BlockSpec(memory_space=pl.ANY)
    scratch = [
        pltpu.VMEM((8, width, heads), BF), pltpu.VMEM((2, width, units), BF), pltpu.VMEM((2, width, units // 2), BF),
        pltpu.VMEM((count, 8, width), F32), pltpu.VMEM((slots, width), BF), pltpu.VMEM((slots, width), BF),
        pltpu.VMEM((3, rows, width), BF), pltpu.VMEM((3, rows, width), BF), pltpu.VMEM((8, slots), F32),
    ]
    scratch += [pltpu.VMEM(shape, kind) for shape, kind in kept[:17]]
    scratch += [pltpu.VMEM((8, width), F32)]
    scratch += [pltpu.SemaphoreType.DMA((80,)), pltpu.SemaphoreType.DMA((80,)), pltpu.SemaphoreType.DMA((40,))]
    return pl.pallas_call(
        functools.partial(forward_kernel, count),
        out_shape=[jax.ShapeDtypeStruct(shape, kind) for shape, kind in kept],
        in_specs=[vmem, vmem, vmem, pl.BlockSpec(memory_space=pltpu.SMEM)] + [vmem] * 4 + [hbm] * 11,
        out_specs=[hbm] * len(kept),
        scratch_shapes=scratch,
        compiler_params=pltpu.CompilerParams(
            collective_id=0, has_side_effects=True, vmem_limit_bytes=VMEM_BYTES
        ),
        name="forward_layer",
    )(layer_input, memory, group_map, lengths, *gain_parts, *weights)


CHUNK = 512


def tall(rows):
    return -(-rows // (2 * CHUNK)) * 2 * CHUNK


def span(at, size):
    return pl.ds(pl.multiple_of(at * size, size), size)


def exit_phase(here, links, rows_own, tab, tabt, gt, rb, ids, lens, high, total, stats, stats_tp, stats_wide, coef, weight, acc,
               dx, land_far, land_near, swap_out, swap_in, grad_out, vocab, fillers):
    count, g, w, t = here.count, here.g, here.w, here.t
    left, right, far = here.left, here.right, here.far
    to_left, to_right, to_far, to_tp = here.to_left, here.to_right, here.to_far, here.to_tp
    rows, width = rows_own.shape
    half = rows // 2
    chunks = tab.shape[0] // CHUNK
    scale = float(width) ** (-0.5)
    base = (w * 2 + t) * vocab
    tokens = count * rows

    def block(b):
        return span(b, rows)

    def halved(b, which):
        return pl.ds(pl.multiple_of(b * rows + which * half, half), half)

    rb[block(w), :] = rows_own[...]
    src = rb.at[block(w)]
    from_left = links.move(src, src, to_right, rb.at[block(left)]).start()
    from_right = links.move(src, src, to_left, rb.at[block(right)]).start()

    def target_row(cols):
        row = ids[:, cols] - base
        return jnp.where(row < vocab, row, -1)

    def flip(j, carry):
        tabt[:, span(j, CHUNK)] = tab[span(j, CHUNK), :].T
        return carry

    def score(b):
        cols = block(b)
        wanted = target_row(cols)
        block_rows = rb[cols, :]

        def step(j, pick):
            at = lax.broadcasted_iota(jnp.int32, (CHUNK, rows), 0) + j * CHUNK
            logits = dot_nt(tab[span(j, CHUNK), :], block_rows) * scale
            logits = jnp.where(at < vocab, logits, MASKED)
            top = jnp.max(logits, axis=0, keepdims=True)
            exponent = jnp.exp(logits - top)
            high[pl.ds(j, 1), cols] = top
            total[pl.ds(j, 1), cols] = jnp.sum(exponent, axis=0, keepdims=True)
            gt[span(j, CHUNK), cols] = exponent.astype(BF)
            return pick + jnp.sum(jnp.where(at == wanted, logits, 0.0), axis=0, keepdims=True)

        pick = lax.fori_loop(0, chunks, step, jnp.zeros((1, rows), F32), unroll=True)
        tops = high[:, cols]
        top = jnp.max(tops, axis=0, keepdims=True)
        stats[0:1, cols] = top
        stats[1:2, cols] = jnp.sum(total[:, cols] * jnp.exp(tops - top), axis=0, keepdims=True)
        stats[2:3, cols] = pick

    score(w)
    from_left.landed()
    src = rb.at[halved(left, 0)]
    far_top = links.move(src, src, to_right, rb.at[halved(far, 0)]).start()
    from_right.landed()
    src = rb.at[halved(right, 1)]
    far_low = links.move(src, src, to_left, rb.at[halved(far, 1)]).start()
    score(left)
    score(right)
    far_top.landed()
    far_low.landed()
    score(far)

    def merged_stats(parts):
        top = parts[0][0:1]
        for part in parts[1:]:
            top = jnp.maximum(top, part[0:1])
        mass = sum(part[1:2] * jnp.exp(part[0:1] - top) for part in parts)
        pick = sum(part[2:3] for part in parts)
        return top, mass, pick

    swap = links.move(stats, stats_tp, to_tp, stats_tp).start()
    lax.fori_loop(0, chunks, flip, 0)
    lengths = [lens[k] for k in range(lens.shape[0])]
    tokens_all = lengths[0]
    for length in lengths[1:]:
        tokens_all = tokens_all + length
    place = lax.broadcasted_iota(jnp.int32, (1, rows), 1)
    for b in range(count):
        inside = jnp.where(place < lens[g * count + b], 1.0, 0.0).astype(F32)
        weight[0:1, b * rows : (b + 1) * rows] = inside / tokens_all.astype(F32)
    swap.landed()
    mine, other = stats[...], stats_tp[...]
    top, mass, pick = merged_stats([mine, other])
    joint = stats_wide.at[w]
    joint[0:1, :] = top
    joint[1:2, :] = mass
    joint[2:3, :] = pick
    spreads = [
        links.move(joint, joint, device, stats_wide.at[at]).start()
        for device, at in ((to_left, right), (to_right, left), (to_far, far))
    ]
    for made in spreads:
        made.landed()
    top, mass, pick = merged_stats([stats_wide[b] for b in range(count)])
    log_total = top + jnp.log(mass)
    all_weight = weight[0:1, :]
    coef[...] = jnp.exp(high[...] - log_total) * all_weight
    stats_tp[3:4, :] = (log_total - pick) * all_weight
    loss = jnp.sum(stats_tp[3:4, block(w)], axis=1, keepdims=True)

    def row_grads(b):
        cols = block(b)
        wanted = target_row(cols)
        own_weight = weight[0:1, cols]
        acc[...] = jnp.zeros_like(acc)

        def step(j, carry):
            at = lax.broadcasted_iota(jnp.int32, (CHUNK, rows), 0) + j * CHUNK
            grad = gt[span(j, CHUNK), cols].astype(F32) * coef[pl.ds(j, 1), cols]
            grad = (grad - jnp.where(at == wanted, own_weight, 0.0)).astype(BF)
            gt[span(j, CHUNK), cols] = grad
            acc[...] += dot_nn(tabt[:, span(j, CHUNK)], grad)
            return carry

        lax.fori_loop(0, chunks, step, 0, unroll=True)
        return (acc[...] * scale).astype(BF).T

    dx[0] = row_grads(far)
    right_far = links.move(dx.at[0, pl.ds(0, half)], land_far.at[0], to_right, land_far.at[0]).start()
    left_far = links.move(dx.at[0, pl.ds(half, half)], land_far.at[1], to_left, land_far.at[1]).start()
    top_rows, low_rows = pl.ds(0, half), pl.ds(half, half)

    def near(slot, where, side, device):
        return links.move(dx.at[slot, where], land_near.at[side, where], device, land_near.at[side, where]).start()

    dx[1] = row_grads(right)
    right_low = near(1, low_rows, 0, to_right)
    dx[2] = row_grads(left)
    left_top = near(2, top_rows, 1, to_left)
    right_far.landed()
    dx[1, top_rows] = (dx[1, top_rows].astype(F32) + land_far[0].astype(F32)).astype(BF)
    right_top = near(1, top_rows, 0, to_right)
    left_far.landed()
    dx[2, low_rows] = (dx[2, low_rows].astype(F32) + land_far[1].astype(F32)).astype(BF)
    left_low = near(2, low_rows, 1, to_left)
    dx[3] = row_grads(w)
    fillers[0]()
    swaps = []
    for where, one_side, other_side in ((top_rows, left_top, right_top), (low_rows, right_low, left_low)):
        one_side.landed()
        other_side.landed()
        joined = dx[3, where].astype(F32) + land_near[0, where].astype(F32) + land_near[1, where].astype(F32)
        swap_out[where, :] = joined.astype(BF)
        swaps.append(links.move(swap_out.at[where], swap_in.at[where], to_tp, swap_in.at[where]).start())
    fillers[1]()
    for made in swaps:
        made.landed()
    grad_out[...] = swap_out[...].astype(F32) + swap_in[...].astype(F32)
    return loss


class TableGrad:
    def __init__(self, here, links, copies, tab, gt, rb, land_core, out):
        self.here, self.links, self.copies = here, links, copies
        self.tab, self.gt, self.rb, self.land_core, self.out = tab, gt, rb, land_core, out
        self.pieces = tab.shape[0] // (2 * CHUNK)
        self.scale = float(tab.shape[1]) ** (-0.5)
        self.cores = []

    def rows(self, owner, i):
        return pl.ds(pl.multiple_of((owner * self.pieces + i) * CHUNK, CHUNK), CHUNK)

    def product(self, where):
        return dot_nn(self.gt[where, :], self.rb[...]) * self.scale

    def first_half(self):
        c = self.here.c
        for i in range(self.pieces):
            where = self.rows(1 - c, i)
            self.tab[where, :] = self.product(where).astype(BF)
            land = self.land_core.at[pl.ds(i * CHUNK, CHUNK)]
            self.cores.append(self.links.move(self.tab.at[where], land, self.here.to_core, land).start())

    def second_half(self):
        c = self.here.c
        for i in range(self.pieces):
            where = self.rows(c, i)
            mine = self.product(where)
            self.cores[i].landed()
            self.tab[where, :] = (mine + self.land_core[i * CHUNK : (i + 1) * CHUNK, :].astype(F32)).astype(BF)
            self.copies.save(self.tab.at[where], self.out.at[pl.ds(i * CHUNK, CHUNK)])


def exit_kernel(
    count, vocab, rows_own, ids, lens, table, grad_o, loss_o, half_o,
    tab, tabt, gt, rb, high, total, stats, stats_tp, stats_wide, coef, weight, acc, dx, land_far, land_near, swap_out, swap_in,
    land_core, send_sems, recv_sems, copy_sems,
):
    here = position(count)
    links, copies = Links(send_sems, recv_sems), Copies(copy_sems)
    load = copies.start(table, tab.at[pl.ds(0, vocab)])
    greet([here.to_left, here.to_right, here.to_far, here.to_core, here.to_tp])
    tab[vocab:, :] = jnp.zeros((tab.shape[0] - vocab, tab.shape[1]), BF)
    load.wait()
    grads = TableGrad(here, links, copies, tab, gt, rb, land_core, half_o)
    loss = exit_phase(here, links, rows_own, tab, tabt, gt, rb, ids, lens, high, total, stats, stats_tp, stats_wide, coef, weight,
                      acc, dx, land_far, land_near, swap_out, swap_in, grad_o, vocab, (grads.first_half, grads.second_half))
    loss_o[...] = jnp.broadcast_to(loss, loss_o.shape)
    links.finish()
    copies.finish()


def exit_head(count, norm_exit, ids, lengths, table):
    vocab, width = table.shape
    rows = norm_exit.shape[0]
    high = tall(vocab)
    chunks = high // CHUNK
    tokens = rows * count
    vmem, hbm = pl.BlockSpec(memory_space=pltpu.VMEM), pl.BlockSpec(memory_space=pl.ANY)
    return pl.pallas_call(
        functools.partial(exit_kernel, count, vocab),
        out_shape=[
            jax.ShapeDtypeStruct((rows, width), F32), jax.ShapeDtypeStruct((8, 128), F32),
            jax.ShapeDtypeStruct((high // 2, width), BF),
        ],
        in_specs=[vmem, vmem, pl.BlockSpec(memory_space=pltpu.SMEM), hbm],
        out_specs=[vmem, vmem, hbm],
        scratch_shapes=[
            pltpu.VMEM((high, width), BF), pltpu.VMEM((width, high), BF), pltpu.VMEM((high, tokens), BF),
            pltpu.VMEM((tokens, width), BF), pltpu.VMEM((chunks, tokens), F32), pltpu.VMEM((chunks, tokens), F32),
            pltpu.VMEM((8, tokens), F32), pltpu.VMEM((8, tokens), F32), pltpu.VMEM((count, 8, tokens), F32),
            pltpu.VMEM((chunks, tokens), F32), pltpu.VMEM((8, tokens), F32), pltpu.VMEM((width, rows), F32),
            pltpu.VMEM((4, rows, width), BF), pltpu.VMEM((2, rows // 2, width), BF), pltpu.VMEM((2, rows, width), BF),
            pltpu.VMEM((rows, width), BF), pltpu.VMEM((rows, width), BF),
            pltpu.VMEM((high // 2, width), BF),
            pltpu.SemaphoreType.DMA((40,)), pltpu.SemaphoreType.DMA((40,)), pltpu.SemaphoreType.DMA((16,)),
        ],
        compiler_params=pltpu.CompilerParams(
            collective_id=1, has_side_effects=True, vmem_limit_bytes=VMEM_BYTES
        ),
        name="exit_head",
    )(norm_exit, ids, lengths, table)


GELU_SCALE = 0.7978845608028654
GELU_CUBE = 0.044715


def norm_back(values, gain, grad):
    factor = lax.rsqrt(jnp.mean(values * values, axis=1, keepdims=True) + EPSILON)
    unit = values * factor
    scaled = grad * gain
    inner = jnp.mean(scaled * values, axis=1, keepdims=True)
    return jnp.sum(grad * unit, axis=0, keepdims=True), factor * scaled - unit * (factor * factor * inner)


def attention_backward(pairs, queries, keys, values, probs, context_grad, query_grad, key_grad, value_grad):
    factor = HEAD_DIM ** (-0.5)

    def step(p, carry):
        cols = pair_columns(p)
        grad = both_heads(context_grad[:, cols])
        soft = probs[p]
        soft_float = soft.astype(F32)
        soft_grad = dot_nt(grad, values[:, cols])
        inner = jnp.sum(soft_float * soft_grad, axis=1, keepdims=True)
        score_grad = (soft_float * (soft_grad - inner)).astype(BF)
        query_grad[:, cols] = (pick_heads(dot_nn(score_grad, keys[:, cols])) * factor).astype(BF)
        key_grad[:, cols] = (dot_tn(score_grad, both_heads(queries[:, cols])) * factor).astype(BF)
        value_grad[:, cols] = dot_tn(soft, grad).astype(BF)
        return carry

    lax.fori_loop(0, pairs, step, 0)


class WeightGrad:
    def __init__(self, here, links, copies, grads, first, depth, land_core, land_far, land_near, land_y, mine_out, out):
        self.here, self.links, self.copies = here, links, copies
        self.grads, self.mine, self.other = grads, first + here.c, first + 1 - here.c
        self.depth, self.half = depth, depth // 2
        self.land_core, self.land_far, self.land_near, self.land_y = land_core, land_far, land_near, land_y
        self.mine_out, self.out = mine_out, out

    def whole(self, at):
        return pl.ds(pl.multiple_of(at * self.depth, 16), self.depth)

    def part(self, at, which):
        return pl.ds(pl.multiple_of(at * self.depth + which * self.half, 16), self.half)

    def pair(self):
        self.core = self.links.move(
            self.grads.at[self.other], self.land_core, self.here.to_core, self.land_core
        ).start()

    def near(self, where, side, which, device):
        rows = pl.ds(which * self.half, self.half)
        return self.links.move(
            self.grads.at[self.mine, where], self.land_near.at[side, rows], device, self.land_near.at[side, rows]
        ).start()

    def add_core(self, where):
        self.grads[self.mine, where] = (
            self.grads[self.mine, where].astype(F32) + self.land_core[where].astype(F32)
        ).astype(BF)

    def ring(self):
        here = self.here
        self.core.landed()
        for at in (here.far, here.right, here.left):
            self.add_core(self.whole(at))
            if at is here.far:
                self.far = [
                    self.links.move(
                        self.grads.at[self.mine, self.part(at, e)], self.land_far.at[e], way, self.land_far.at[e]
                    ).start()
                    for e, way in enumerate((here.to_right, here.to_left))
                ]
        self.early = [
            self.near(self.part(here.right, 1), 0, 1, here.to_right),
            self.near(self.part(here.left, 0), 1, 0, here.to_left),
        ]
        self.add_core(self.whole(here.w))

    def pass_on(self):
        here = self.here
        self.late = []
        for e, side, way in ((0, here.right, here.to_right), (1, here.left, here.to_left)):
            self.far[e].landed()
            where = self.part(side, e)
            self.grads[self.mine, where] = (
                self.grads[self.mine, where].astype(F32) + self.land_far[e].astype(F32)
            ).astype(BF)
            self.late.append(self.near(where, e, e, way))

    def across(self):
        for made in self.early + self.late:
            made.landed()
        where = self.whole(self.here.w)
        self.mine_out[0] = (
            self.grads[self.mine, where].astype(F32) + self.land_near[0].astype(F32) + self.land_near[1].astype(F32)
        ).astype(BF)
        self.y = self.links.move(self.mine_out.at[0], self.land_y, self.here.to_y, self.land_y).start()

    def settle(self):
        self.y.landed()
        self.mine_out[1] = (self.mine_out[0].astype(F32) + self.land_y[...].astype(F32)).astype(BF)
        src = self.mine_out.at[1]
        self.copies.save(src, self.out.at[self.mine])
        self.share = self.links.move(
            src, self.out.at[self.mine], self.here.to_core, self.out.at[self.other]
        ).start()

    def done(self):
        self.share.landed()


def backward_kernel(
    count,
    lens, map_ref, x_h, og_h, eg_h, loss_h, one_h, two_h, three_h, q_h, k_h, v_h, cq_h, mk_h, mv_h, sc_h, cc_h, ps_h, pc_h,
    ga_h, up_h, sel_h, wa_h, wgu_h, wd_h, gain_h, half_h,
    in_o, mem_o, small_o, ga8_o, ggu_o, gd_o, table_o,
    x, og, eg, loss, one, two, three, q, k, v, cq, mk, mv, sc, cc, ps, pc, ga, up, sel, wa, wgu, wd, gain, tab, land_t,
    part_out, part_in, grad, dq, dk, dv, dmk, dmv, dctx, gate_grad, up_grad, ff_hidden,
    g8, ggu, gd, lc8, lcg, lcd, lf8, lfg, lfd, ln8, lng, lnd, ly8, lyg, lyd, mo8, mog, mod,
    back_slots, got_slots, small, small_wide, small_land,
    send_sems, recv_sems, copy_sems,
):
    here = position(count)
    links, copies = Links(send_sems, recv_sems), Copies(copy_sems)
    g, w, c = here.g, here.w, here.c
    to_left, to_right, to_far, to_tp = (here.to_left, here.to_right, here.to_far, here.to_tp)
    loads = {}
    for src, dst in (
        (gain_h, gain), (three_h, three), (eg_h, eg), (og_h, og), (ga_h, ga), (up_h, up), (wd_h, wd), (half_h, tab), (wgu_h, wgu),
        (two_h, two), (wa_h, wa), (cc_h, cc), (pc_h, pc), (cq_h, cq), (mk_h, mk), (mv_h, mv), (sel_h, sel), (one_h, one),
        (sc_h, sc), (ps_h, ps), (q_h, q), (k_h, k), (v_h, v), (x_h, x), (loss_h, loss),
    ):
        loads[id(dst)] = copies.start(src, dst)

    def need(*refs):
        for ref in refs:
            loads.pop(id(ref)).wait()

    greet([to_left, to_right, to_far, here.to_core, here.to_y, to_tp])

    pieces = tab.shape[0] // CHUNK
    need(tab)
    crossing = [
        links.move(tab.at[pl.ds(i * CHUNK, CHUNK)], land_t.at[pl.ds(i * CHUNK, CHUNK)], here.to_y, land_t.at[pl.ds(i * CHUNK, CHUNK)]).start()
        for i in range(pieces)
    ]
    shares = []

    def settle_table(i):
        piece = pl.ds(i * CHUNK, CHUNK)
        crossing[i].landed()
        crossing[i].sent()
        tab[piece, :] = (tab[piece, :].astype(F32) + land_t[piece, :].astype(F32)).astype(BF)

        def rows(owner):
            return pl.ds(pl.multiple_of((owner * pieces + i) * CHUNK, CHUNK), CHUNK)

        copies.save(tab.at[piece], table_o.at[rows(c)])
        shares.append(
            links.move(tab.at[piece], table_o.at[rows(c)], here.to_core, table_o.at[rows(1 - c)]).start()
        )

    depth = g8.shape[1] // count

    def weight_pair(i):
        if i < 4:
            return WeightGrad(here, links, copies, g8, 2 * i, depth, lc8.at[i], lf8.at[i], ln8.at[i], ly8.at[i], mo8.at[i], ga8_o)
        if i == 4:
            return WeightGrad(here, links, copies, ggu, 0, depth, lcg, lfg, lng, lyg, mog, ggu_o)
        return WeightGrad(here, links, copies, gd, 0, depth, lcd, lfd, lnd, lyd, mod, gd_o)

    pair = [weight_pair(i) for i in range(6)]

    def exchange_start(n):
        return links.move(part_out.at[n], part_in.at[n], to_tp, part_in.at[n]).start()

    def exchanged(n, made):
        made.landed()
        return part_out[n].astype(F32) + part_in[n].astype(F32)

    small[...] = jnp.zeros_like(small)
    need(gain, three, eg, og)
    gain_row, back = norm_back(three[...], gain[3:4, :], eg[...])
    small[3:4, :] = gain_row
    grad[...] = og[...].astype(F32) + back
    branch = grad[...].astype(BF)
    need(ga, up, wd)
    units = wd.shape[2]
    for e in range(2):
        cols = slice(e * units, (e + 1) * units)
        act = ga[:, cols].astype(F32)
        up_act = up[:, cols].astype(F32)
        square = act * act
        bend = jnp.tanh(GELU_SCALE * (act + GELU_CUBE * act * square))
        gate = 0.5 * act * (1.0 + bend)
        slope = 0.5 * (1.0 + bend) + 0.5 * act * (1.0 - bend * bend) * (GELU_SCALE * (1.0 + 3.0 * GELU_CUBE * square))
        hidden_grad = dot_nn(branch, wd[e])
        gate_grad[:, cols] = (hidden_grad * up_act * slope).astype(BF)
        up_grad[:, cols] = (hidden_grad * gate).astype(BF)
        ff_hidden[:, cols] = (gate * up_act).astype(BF)
    need(wgu)
    part_out[0] = (dot_nt(gate_grad[...], wgu[0]) + dot_nt(up_grad[...], wgu[1])).astype(BF)
    swap = exchange_start(0)
    need(two)
    norm_t = rms_rows(two[...], gain[2:3, :]).T
    ggu[0] = dot_nn(norm_t, gate_grad[...]).astype(BF)
    ggu[1] = dot_nn(norm_t, up_grad[...]).astype(BF)
    pair[4].pair()
    branch_rows = branch.T
    for e in range(2):
        gd[e] = dot_nn(branch_rows, ff_hidden[:, e * units : (e + 1) * units]).astype(BF)
    pair[5].pair()
    pair[4].ring()
    gain_row, back = norm_back(two[...], gain[2:3, :], exchanged(0, swap))
    small[2:3, :] = gain_row
    grad[...] += back

    branch = grad[...].astype(BF)
    need(wa, cc, pc, cq, mk, mv, sel)
    dctx[...] = dot_nn(branch, wa[7]).astype(BF)
    pairs = dctx.shape[1] // (2 * HEAD_DIM)
    attention_backward(pairs, cq, mk, mv, pc, dctx, dq, dmk, dmv)
    part_out[1] = dot_nt(dq[...], wa[6]).astype(BF)
    swap = exchange_start(1)
    pair[5].ring()
    pair[4].pass_on()
    need(one)
    back_slots[...] = (dot_nt(dmk[...], wa[4]) + dot_nt(dmv[...], wa[5])).astype(BF)
    capacity = back_slots.shape[0] // count

    def slot_rows(at):
        return pl.ds(pl.multiple_of(at * capacity, 16), capacity)

    returns = [
        links.move(back_slots.at[slot_rows(to)], got_slots.at[slot_rows(w)], device, got_slots.at[slot_rows(at)]).start()
        for device, to, at in ((to_left, here.left, here.right), (to_right, here.right, here.left), (to_far, here.far, here.far))
    ]
    got_slots[slot_rows(w), :] = back_slots[slot_rows(w), :]
    g8[7] = dot_nn(branch.T, cc[...]).astype(BF)
    norm_t = rms_rows(one[...], gain[1:2, :]).T
    g8[6] = dot_nn(norm_t, dq[...]).astype(BF)
    pair[3].pair()
    slots_t = sel[...].T
    g8[4] = dot_nn(slots_t, dmk[...]).astype(BF)
    g8[5] = dot_nn(slots_t, dmv[...]).astype(BF)
    pair[2].pair()
    pair[4].across()
    pair[5].pass_on()
    pair[3].ring()
    pair[2].ring()
    gain_row, back = norm_back(one[...], gain[1:2, :], exchanged(1, swap))
    small[1:2, :] = gain_row
    grad[...] += back

    branch = grad[...].astype(BF)
    need(sc, ps, q, k, v, x)
    dctx[...] = dot_nn(branch, wa[3]).astype(BF)
    attention_backward(pairs, q, k, v, ps, dctx, dq, dk, dv)
    part_out[2] = (dot_nt(dq[...], wa[0]) + dot_nt(dk[...], wa[1]) + dot_nt(dv[...], wa[2])).astype(BF)
    swap = exchange_start(2)
    hidden = x[...].astype(F32)
    norm_t = rms_rows(hidden, gain[0:1, :]).T
    g8[0] = dot_nn(norm_t, dq[...]).astype(BF)
    g8[1] = dot_nn(norm_t, dk[...]).astype(BF)
    pair[0].pair()
    g8[2] = dot_nn(norm_t, dv[...]).astype(BF)
    g8[3] = dot_nn(branch.T, sc[...]).astype(BF)
    pair[1].pair()
    pair[3].pass_on()
    pair[2].pass_on()
    pair[5].across()
    pair[0].ring()
    pair[1].ring()
    for made in returns:
        made.landed()
    rows = x.shape[0]
    choose = slot_choice(map_ref[:, pl.ds(pl.multiple_of(w * rows, rows), rows)], got_slots.shape[0], count)
    part_out[3] = dot_tn(choose, got_slots[...]).astype(BF)
    memory_swap = exchange_start(3)
    gain_row, back = norm_back(hidden, gain[0:1, :], exchanged(2, swap))
    small[0:1, :] = gain_row
    grad[...] += back
    copies.save(grad, in_o)
    need(loss)
    small[4:5, 0:128] = loss[0:1, :]

    small_wide[w] = small[...]
    sums = [
        links.move(small, small_wide.at[w], device, small_wide.at[at]).start()
        for device, at in ((to_left, here.right), (to_right, here.left), (to_far, here.far))
    ]
    pair[0].pass_on()
    pair[1].pass_on()
    pair[3].across()
    pair[2].across()
    for made in sums:
        made.landed()
    total = small_wide[0]
    for b in range(1, count):
        total = total + small_wide[b]
    for n, way in enumerate((here.to_core, here.to_y)):
        small_land[2 * n] = total
        made = links.move(small_land.at[2 * n], small_land.at[2 * n + 1], way, small_land.at[2 * n + 1]).start()
        if n == 0:
            pair[0].across()
            pair[1].across()
        made.landed()
        total = total + small_land[2 * n + 1]
    small_o[...] = total
    mem_o[...] = exchanged(3, memory_swap)
    for i in range(pieces):
        settle_table(i)
    for i in (4, 5, 3, 2, 0, 1):
        pair[i].settle()
    for i in (4, 5, 3, 2, 0, 1):
        pair[i].done()
    for made in shares:
        made.landed()
    links.finish_rest(crossing)
    copies.finish()


def backward_layer(count, lengths, group_map, kept, table_half):
    (layer_input, out_grad, exit_rows_grad, loss_part, one, two, three, q, k, v, cq, mk, mv, sc, cc, ps, pc, ga, up, sel,
     wa, wgu, wd, gains) = kept
    rows, width = layer_input.shape
    heads, units = wa.shape[2], ga.shape[1]
    slots, depth = sel.shape[0], width // count
    half, narrow = depth // 2, units // 2
    piece_rows = table_half.shape[0]
    high = 2 * piece_rows
    vmem, hbm = pl.BlockSpec(memory_space=pltpu.VMEM), pl.BlockSpec(memory_space=pl.ANY)

    def three_kinds(rows_of, lead=()):
        return [
            pltpu.VMEM((4,) + lead + (rows_of, heads), BF), pltpu.VMEM(lead + (rows_of, units), BF),
            pltpu.VMEM(lead + (rows_of, narrow), BF),
        ]

    scratch = [pltpu.VMEM(value.shape, value.dtype) for value in kept]
    scratch += [pltpu.VMEM((piece_rows, width), BF), pltpu.VMEM((piece_rows, width), BF)]
    scratch += [
        pltpu.VMEM((4, rows, width), BF), pltpu.VMEM((4, rows, width), BF), pltpu.VMEM((rows, width), F32),
        pltpu.VMEM((rows, heads), BF), pltpu.VMEM((rows, heads), BF), pltpu.VMEM((rows, heads), BF),
        pltpu.VMEM((slots, heads), BF), pltpu.VMEM((slots, heads), BF), pltpu.VMEM((rows, heads), BF),
        pltpu.VMEM((rows, units), BF), pltpu.VMEM((rows, units), BF), pltpu.VMEM((rows, units), BF),
        pltpu.VMEM((8, width, heads), BF), pltpu.VMEM((2, width, units), BF), pltpu.VMEM((2, width, narrow), BF),
    ]
    scratch += three_kinds(width)
    scratch += three_kinds(half, (2,))
    scratch += three_kinds(depth, (2,))
    scratch += three_kinds(depth)
    scratch += three_kinds(depth, (2,))
    scratch += [
        pltpu.VMEM((slots, width), BF), pltpu.VMEM((slots, width), BF), pltpu.VMEM((8, width), F32),
        pltpu.VMEM((count, 8, width), F32), pltpu.VMEM((4, 8, width), F32),
        pltpu.SemaphoreType.DMA((80,)), pltpu.SemaphoreType.DMA((80,)), pltpu.SemaphoreType.DMA((48,)),
    ]
    return pl.pallas_call(
        functools.partial(backward_kernel, count),
        out_shape=[
            jax.ShapeDtypeStruct((rows, width), F32), jax.ShapeDtypeStruct((rows, width), F32),
            jax.ShapeDtypeStruct((8, width), F32), jax.ShapeDtypeStruct((8, depth, heads), BF),
            jax.ShapeDtypeStruct((2, depth, units), BF), jax.ShapeDtypeStruct((2, depth, narrow), BF),
            jax.ShapeDtypeStruct((high, width), BF),
        ],
        in_specs=[pl.BlockSpec(memory_space=pltpu.SMEM), vmem] + [hbm] * (len(kept) + 1),
        out_specs=[hbm, vmem, vmem, hbm, hbm, hbm, hbm],
        scratch_shapes=scratch,
        compiler_params=pltpu.CompilerParams(
            collective_id=2, has_side_effects=True, vmem_limit_bytes=VMEM_BYTES
        ),
        name="backward_layer",
    )(lengths, group_map, *kept, table_half)


def fused_body(
    layer_input,
    memory,
    reader_map,
    target_ids,
    target_lengths,
    out_grad,
    self_q,
    self_k,
    self_v,
    self_o,
    cross_q,
    cross_k,
    cross_v,
    cross_o,
    ff_gate,
    ff_up,
    ff_out,
    gain_self,
    gain_cross,
    gain_ff,
    gain_exit,
    exit_table,
):
    count = lax.axis_size("wide")
    wide_index = lax.axis_index("wide")
    depth = gain_self.shape[0]
    group_map = reader_map[None, :]
    (
        block_output, resid_one, resid_two, resid_three, norm_exit, queries, keys, values, cross_queries,
        keys_read, values_read, context_self, context_cross, probs_self, probs_cross, gate_act, up_act, slots,
        attn_weights, gate_weights, down_weights, gains,
    ) = forward_layer(
        count, layer_input, memory, group_map, target_lengths,
        tuple(gain[None, :] for gain in (gain_self, gain_cross, gain_ff, gain_exit)),
        (self_q, self_k, self_v, self_o, cross_q, cross_k, cross_v, cross_o, ff_gate, ff_up, ff_out),
    )
    exit_rows_grad, loss_part, table_half = exit_head(
        count, norm_exit, target_ids[None, :], target_lengths, exit_table
    )
    input_grad, memory_grad, small, attn_grads, gate_grads, down_grads, table_grad = backward_layer(
        count, target_lengths, group_map,
        (
            layer_input, out_grad, exit_rows_grad, loss_part, resid_one, resid_two, resid_three, queries, keys, values,
            cross_queries, keys_read, values_read, context_self, context_cross, probs_self, probs_cross, gate_act, up_act,
            slots, attn_weights, gate_weights, down_weights, gains,
        ),
        table_half,
    )
    own_gains = lax.dynamic_slice(small, (0, wide_index * depth), (4, depth))
    attn = attn_grads.astype(jnp.float32)
    gate = gate_grads.astype(jnp.float32)
    down = jnp.concatenate([down_grads[0], down_grads[1]], axis=1).astype(jnp.float32)
    return (
        block_output, small[4, 0], input_grad, memory_grad, attn[0], attn[1], attn[2], attn[3], attn[6], attn[4], attn[5],
        attn[7], gate[0], gate[1], down, own_gains[0], own_gains[1], own_gains[2], own_gains[3],
        table_grad[: exit_table.shape[0]].astype(jnp.float32),
    )


def fits(mesh):
    return mesh.shape["wide"] == 4 and mesh.shape["tp"] == 2 and mesh.shape["grp"] == 4


def solution(mesh):
    placed = (
        P(("grp", "wide"), None),
        P(("grp", "wide"), None),
        P("grp"),
        P("grp"),
        P(),
        P(("grp", "wide"), None),
        P("wide", "tp"),
        P("wide", "tp"),
        P("wide", "tp"),
        P("wide", "tp"),
        P("wide", "tp"),
        P("wide", "tp"),
        P("wide", "tp"),
        P("wide", "tp"),
        P("wide", "tp"),
        P("wide", "tp"),
        P("wide", "tp"),
        P("wide"),
        P("wide"),
        P("wide"),
        P("wide"),
        P(("wide", "tp"), None),
    )
    return jax.shard_map(
        fused_body if fits(mesh) else plain_body,
        mesh=mesh,
        in_specs=placed,
        out_specs=(
            P(("grp", "wide"), None),
            P(),
            P(("grp", "wide"), None),
            P(("grp", "wide"), None),
            P("wide", "tp"),
            P("wide", "tp"),
            P("wide", "tp"),
            P("wide", "tp"),
            P("wide", "tp"),
            P("wide", "tp"),
            P("wide", "tp"),
            P("wide", "tp"),
            P("wide", "tp"),
            P("wide", "tp"),
            P("wide", "tp"),
            P("wide"),
            P("wide"),
            P("wide"),
            P("wide"),
            P(("wide", "tp"), None),
        ),
        check_vma=False,
    )
```

```python
import functools
import types

import jax
import jax.numpy as jnp
from jax import lax
from jax.experimental import pallas as pl
from jax.experimental.pallas import tpu as pltpu
from jax.sharding import PartitionSpec as P

HEAD_DIM = 64


EPSILON = 1e-06
MASKED = -1e30


def merged(shard, axis, combine):
    everything = jax.tree.map(
        lambda part, kind: lax.all_gather(part.astype(kind), axis),
        shard,
        (jnp.bfloat16, jnp.bfloat16, jnp.bfloat16),
    )

    def take(k):
        return jax.tree.map(lambda part, own: part[k].astype(own.dtype), everything, shard)

    return lax.fori_loop(
        1, lax.axis_size(axis), lambda k, so_far: combine(so_far, take(k)), take(0)
    )


def project(left, right):
    return jnp.dot(left, right, preferred_element_type=jnp.float32)


def project_back(left, right):
    return lax.dot_general(
        left, right, (((1,), (1,)), ((), ())), preferred_element_type=jnp.float32
    )


def outer_rows(left, right):
    return lax.dot_general(
        left, right, (((0,), (0,)), ((), ())), preferred_element_type=jnp.float32
    )


def smooth_gate(values):
    return jax.nn.gelu(values, approximate=True)


def normalize(values, gain):
    factor = lax.rsqrt(jnp.mean(values * values, axis=1, keepdims=True) + EPSILON)
    unit_rows = values * factor
    return ((unit_rows * gain).astype(jnp.bfloat16), unit_rows, factor)


def normalize_back(values, unit_rows, factor, gain, grad_rows):
    gain_grad = jnp.sum(grad_rows * unit_rows, axis=0)
    scaled = grad_rows * gain
    inner = jnp.mean(scaled * values, axis=1, keepdims=True)
    return (gain_grad, factor * scaled - unit_rows * factor * factor * inner)


def split_heads(values):
    return values.reshape(values.shape[0], -1, HEAD_DIM).transpose(1, 0, 2)


def join_heads(values):
    return values.transpose(1, 0, 2).reshape(values.shape[1], -1)


def read_slots(group_map, reader, holders, rows_each, capacity):
    matched = (group_map.reshape(holders, rows_each) == reader).astype(jnp.int32)
    ranks = jnp.cumsum(matched, axis=1) - 1
    counts = jnp.sum(matched, axis=1)
    place = lax.iota(jnp.int32, holders * capacity)
    valid = place % capacity < jnp.repeat(counts, capacity, total_repeat_length=holders * capacity)
    anchor = lax.iota(jnp.int32, holders)[:, None] * capacity + ranks
    target = jnp.where(matched > 0, anchor, holders * capacity)
    return (valid, target.reshape(-1))


def attend_forward(queries, keys, values, allowed):
    factor = HEAD_DIM ** (-0.5)

    def one_head(parts):
        query, key_rows, value_rows = parts
        scores = jnp.where(allowed, project_back(query, key_rows) * factor, MASKED)
        highest = jnp.max(scores, axis=1, keepdims=True)
        exponent = jnp.exp(scores - highest)
        total = jnp.sum(exponent, axis=1, keepdims=True)
        soft_weights = (exponent / total).astype(jnp.bfloat16)
        return (project(soft_weights, value_rows), (highest + jnp.log(total))[:, 0])

    context, log_total = lax.map(
        one_head, (split_heads(queries), split_heads(keys), split_heads(values))
    )
    return (join_heads(context).astype(jnp.bfloat16), log_total)


def attend_backward(queries, keys, values, context_grad, log_total, allowed):
    factor = HEAD_DIM ** (-0.5)

    def one_head(parts):
        query, key_rows, value_rows, grad_rows, log_row = parts
        scores = jnp.where(allowed, project_back(query, key_rows) * factor, MASKED)
        soft = jnp.exp(scores - log_row[:, None])
        soft_grad = project_back(grad_rows, value_rows)
        score_grad = (soft * (soft_grad - jnp.sum(soft * soft_grad, axis=1, keepdims=True))).astype(
            jnp.bfloat16
        )
        query_grad = project(score_grad, key_rows) * factor
        key_grad = outer_rows(score_grad, query) * factor
        value_grad = outer_rows(soft.astype(jnp.bfloat16), grad_rows)
        return (query_grad, key_grad, value_grad)

    grads = lax.map(
        one_head,
        (
            split_heads(queries),
            split_heads(keys),
            split_heads(values),
            split_heads(context_grad),
            log_total,
        ),
    )
    return (join_heads(grads[0]), join_heads(grads[1]), join_heads(grads[2]))


def heads_total(partial_rows):
    return lax.psum(partial_rows, "tp")


def input_total(partial_rows):
    return lax.psum(partial_rows.astype(jnp.bfloat16), "tp").astype(jnp.float32)


def merge_softmax(first, second):
    highest = jnp.maximum(first[0], second[0])
    total = first[1] * jnp.exp(first[0] - highest) + second[1] * jnp.exp(second[0] - highest)
    return (highest, total, first[2] + second[2])


def plain_body(
    layer_input,
    memory,
    reader_map,
    target_ids,
    target_lengths,
    out_grad,
    self_q,
    self_k,
    self_v,
    self_o,
    cross_q,
    cross_k,
    cross_v,
    cross_o,
    ff_gate,
    ff_up,
    ff_out,
    gain_self,
    gain_cross,
    gain_ff,
    gain_exit,
    exit_table,
):
    (
        w_query,
        w_key,
        w_value,
        w_output,
        c_query,
        c_key,
        c_value,
        c_output,
        w_gate,
        w_up,
        w_down,
        full_gain_self,
        full_gain_cross,
        full_gain_ff,
        full_gain_exit,
    ) = (
        lax.all_gather(self_q, "wide", axis=0, tiled=True),
        lax.all_gather(self_k, "wide", axis=0, tiled=True),
        lax.all_gather(self_v, "wide", axis=0, tiled=True),
        lax.all_gather(self_o, "wide", axis=0, tiled=True),
        lax.all_gather(cross_q, "wide", axis=0, tiled=True),
        lax.all_gather(cross_k, "wide", axis=0, tiled=True),
        lax.all_gather(cross_v, "wide", axis=0, tiled=True),
        lax.all_gather(cross_o, "wide", axis=0, tiled=True),
        lax.all_gather(ff_gate, "wide", axis=0, tiled=True),
        lax.all_gather(ff_up, "wide", axis=0, tiled=True),
        lax.all_gather(ff_out, "wide", axis=0, tiled=True),
        lax.all_gather(gain_self, "wide", axis=0, tiled=True),
        lax.all_gather(gain_cross, "wide", axis=0, tiled=True),
        lax.all_gather(gain_ff, "wide", axis=0, tiled=True),
        lax.all_gather(gain_exit, "wide", axis=0, tiled=True),
    )
    gain_one = full_gain_self.astype(jnp.float32)
    gain_two = full_gain_cross.astype(jnp.float32)
    gain_three = full_gain_ff.astype(jnp.float32)
    gain_last = full_gain_exit.astype(jnp.float32)
    seq_rows = layer_input.shape[0]
    wide_count = lax.axis_size("wide")
    wide_index = lax.axis_index("wide")
    group_index = lax.axis_index("grp")
    group_lengths = lax.dynamic_slice_in_dim(target_lengths, group_index * wide_count, wide_count)
    own_length = lax.dynamic_index_in_dim(group_lengths, wide_index, keepdims=False)
    hidden = layer_input.astype(jnp.float32)
    norm_self, unit_self, factor_self = normalize(hidden, gain_one)
    queries = project(norm_self, w_query).astype(jnp.bfloat16)
    keys = project(norm_self, w_key).astype(jnp.bfloat16)
    values = project(norm_self, w_value).astype(jnp.bfloat16)
    position = lax.iota(jnp.int32, seq_rows)
    allowed_self = (position[None, :] <= position[:, None]) & (position[None, :] < own_length)
    context_self, log_self = attend_forward(queries, keys, values, allowed_self)
    resid_one = hidden + heads_total(project_back(context_self, w_output))
    norm_cross, unit_cross, factor_cross = normalize(resid_one, gain_two)
    cross_queries = project(norm_cross, c_query).astype(jnp.bfloat16)
    memory_keys = project(memory, c_key).astype(jnp.bfloat16)
    memory_values = project(memory, c_value).astype(jnp.bfloat16)
    rows_each = memory.shape[0]
    capacity = max(2, 2 * rows_each // wide_count)
    slot_count = wide_count * capacity
    slot_valid, slot_target = read_slots(reader_map, wide_index, wide_count, rows_each, capacity)
    keys_all, values_all = (
        lax.all_gather(memory_keys, "wide", axis=0, tiled=True),
        lax.all_gather(memory_values, "wide", axis=0, tiled=True),
    )
    read_table = (
        jnp.zeros((slot_count,), jnp.int32)
        .at[slot_target]
        .set(lax.iota(jnp.int32, wide_count * rows_each), mode="drop")
    )
    keys_read = jnp.take(keys_all, read_table, axis=0)
    values_read = jnp.take(values_all, read_table, axis=0)
    allowed_cross = slot_valid[None, :]
    context_cross, log_cross = attend_forward(cross_queries, keys_read, values_read, allowed_cross)
    resid_two = resid_one + heads_total(project_back(context_cross, c_output))
    norm_ff, unit_ff, factor_ff = normalize(resid_two, gain_three)
    gate_float = project(norm_ff, w_gate).astype(jnp.bfloat16).astype(jnp.float32)
    up_float = project(norm_ff, w_up).astype(jnp.bfloat16).astype(jnp.float32)
    gelu_value, gelu_pull = jax.vjp(smooth_gate, gate_float)
    ff_hidden = (gelu_value * up_float).astype(jnp.bfloat16)
    resid_three = resid_two + heads_total(project_back(ff_hidden, w_down))
    block_output = resid_three.astype(jnp.bfloat16)
    norm_exit, unit_exit, factor_exit = normalize(resid_three, gain_last)
    rows_all = lax.all_gather(norm_exit, "wide", axis=0, tiled=True)
    group_tokens = rows_all.shape[0]
    vocab_rows = exit_table.shape[0]
    scale_exit = float(rows_all.shape[1]) ** (-0.5)
    logits = project_back(rows_all, exit_table) * scale_exit
    vocab_ids = lax.axis_index(("wide", "tp")) * vocab_rows + lax.iota(jnp.int32, vocab_rows)
    is_target = target_ids[:, None] == vocab_ids[None, :]
    local_high = jnp.max(logits, axis=1)
    local_total = jnp.sum(jnp.exp(logits - local_high[:, None]), axis=1)
    local_pick = jnp.sum(jnp.where(is_target, logits, 0.0), axis=1)
    highest, total_exp, target_logit = merged(
        (local_high, local_total, local_pick), ("wide", "tp"), merge_softmax
    )
    log_total = highest + jnp.log(total_exp)
    token_place = lax.iota(jnp.int32, group_tokens)
    valid = token_place % seq_rows < jnp.repeat(
        group_lengths, seq_rows, total_repeat_length=group_tokens
    )
    token_count = jnp.sum(target_lengths).astype(jnp.float32)
    token_weight = jnp.where(valid, 1.0, 0.0).astype(jnp.float32) / token_count
    group_loss = jnp.sum(token_weight * (log_total - target_logit))
    logit_grad = (
        (jnp.exp(logits - log_total[:, None]) - jnp.where(is_target, 1.0, 0.0))
        * token_weight[:, None]
    ).astype(jnp.bfloat16)
    rows_grad_all = project(logit_grad, exit_table) * scale_exit
    exit_grad = outer_rows(logit_grad, rows_all) * scale_exit
    rows_part = lax.psum_scatter(
        rows_grad_all.astype(jnp.bfloat16), "wide", scatter_dimension=0, tiled=True
    )
    norm_exit_grad = lax.psum(rows_part, "tp").astype(jnp.float32)
    gain_exit_grad, back_exit = normalize_back(
        resid_three, unit_exit, factor_exit, gain_last, norm_exit_grad
    )
    resid_three_grad = out_grad.astype(jnp.float32) + back_exit
    ff_branch = resid_three_grad.astype(jnp.bfloat16)
    w_down_grad = outer_rows(ff_branch, ff_hidden)
    hidden_grad = project(ff_branch, w_down)
    gate_grad = gelu_pull(hidden_grad * up_float)[0].astype(jnp.bfloat16)
    up_grad = (hidden_grad * gelu_value).astype(jnp.bfloat16)
    w_gate_grad = outer_rows(norm_ff, gate_grad)
    w_up_grad = outer_rows(norm_ff, up_grad)
    norm_ff_grad = input_total(project_back(gate_grad, w_gate) + project_back(up_grad, w_up))
    gain_ff_grad, back_ff = normalize_back(resid_two, unit_ff, factor_ff, gain_three, norm_ff_grad)
    resid_two_grad = resid_three_grad + back_ff
    cross_branch = resid_two_grad.astype(jnp.bfloat16)
    c_output_grad = outer_rows(cross_branch, context_cross)
    cross_context_grad = project(cross_branch, c_output).astype(jnp.bfloat16)
    cross_query_grad, keys_grad_read, values_grad_read = attend_backward(
        cross_queries, keys_read, values_read, cross_context_grad, log_cross, allowed_cross
    )
    empty_grads = jnp.zeros((wide_count * rows_each, keys_grad_read.shape[1]), jnp.float32)
    keys_grad_all = empty_grads.at[read_table].add(keys_grad_read)
    values_grad_all = empty_grads.at[read_table].add(values_grad_read)
    keys_grad, values_grad = (
        lax.psum_scatter(
            keys_grad_all.astype(jnp.bfloat16), "wide", scatter_dimension=0, tiled=True
        ).astype(jnp.float32),
        lax.psum_scatter(
            values_grad_all.astype(jnp.bfloat16), "wide", scatter_dimension=0, tiled=True
        ).astype(jnp.float32),
    )
    keys_grad = keys_grad.astype(jnp.bfloat16)
    values_grad = values_grad.astype(jnp.bfloat16)
    cross_query_grad = cross_query_grad.astype(jnp.bfloat16)
    c_query_grad = outer_rows(norm_cross, cross_query_grad)
    c_key_grad = outer_rows(memory, keys_grad)
    c_value_grad = outer_rows(memory, values_grad)
    norm_cross_grad, memory_grad = (
        lax.psum(project_back(cross_query_grad, c_query).astype(jnp.bfloat16), "tp").astype(
            jnp.float32
        ),
        lax.psum(
            (project_back(keys_grad, c_key) + project_back(values_grad, c_value)).astype(
                jnp.bfloat16
            ),
            "tp",
        ).astype(jnp.float32),
    )
    gain_cross_grad, back_cross = normalize_back(
        resid_one, unit_cross, factor_cross, gain_two, norm_cross_grad
    )
    resid_one_grad = resid_two_grad + back_cross
    self_branch = resid_one_grad.astype(jnp.bfloat16)
    w_output_grad = outer_rows(self_branch, context_self)
    self_context_grad = project(self_branch, w_output).astype(jnp.bfloat16)
    query_grad, key_grad, value_grad = attend_backward(
        queries, keys, values, self_context_grad, log_self, allowed_self
    )
    query_grad = query_grad.astype(jnp.bfloat16)
    key_grad = key_grad.astype(jnp.bfloat16)
    value_grad = value_grad.astype(jnp.bfloat16)
    w_query_grad = outer_rows(norm_self, query_grad)
    w_key_grad = outer_rows(norm_self, key_grad)
    w_value_grad = outer_rows(norm_self, value_grad)
    norm_self_grad = input_total(
        project_back(query_grad, w_query)
        + project_back(key_grad, w_key)
        + project_back(value_grad, w_value)
    )
    gain_self_grad, back_self = normalize_back(
        hidden, unit_self, factor_self, gain_one, norm_self_grad
    )
    input_grad = resid_one_grad + back_self
    shards = (
        lax.psum_scatter(
            w_query_grad.astype(jnp.bfloat16), "wide", scatter_dimension=0, tiled=True
        ).astype(jnp.float32),
        lax.psum_scatter(
            w_key_grad.astype(jnp.bfloat16), "wide", scatter_dimension=0, tiled=True
        ).astype(jnp.float32),
        lax.psum_scatter(
            w_value_grad.astype(jnp.bfloat16), "wide", scatter_dimension=0, tiled=True
        ).astype(jnp.float32),
        lax.psum_scatter(
            w_output_grad.astype(jnp.bfloat16), "wide", scatter_dimension=0, tiled=True
        ).astype(jnp.float32),
        lax.psum_scatter(
            c_query_grad.astype(jnp.bfloat16), "wide", scatter_dimension=0, tiled=True
        ).astype(jnp.float32),
        lax.psum_scatter(
            c_key_grad.astype(jnp.bfloat16), "wide", scatter_dimension=0, tiled=True
        ).astype(jnp.float32),
        lax.psum_scatter(
            c_value_grad.astype(jnp.bfloat16), "wide", scatter_dimension=0, tiled=True
        ).astype(jnp.float32),
        lax.psum_scatter(
            c_output_grad.astype(jnp.bfloat16), "wide", scatter_dimension=0, tiled=True
        ).astype(jnp.float32),
        lax.psum_scatter(
            w_gate_grad.astype(jnp.bfloat16), "wide", scatter_dimension=0, tiled=True
        ).astype(jnp.float32),
        lax.psum_scatter(
            w_up_grad.astype(jnp.bfloat16), "wide", scatter_dimension=0, tiled=True
        ).astype(jnp.float32),
        lax.psum_scatter(
            w_down_grad.astype(jnp.bfloat16), "wide", scatter_dimension=0, tiled=True
        ).astype(jnp.float32),
        lax.psum_scatter(
            gain_self_grad.astype(jnp.bfloat16), "wide", scatter_dimension=0, tiled=True
        ).astype(jnp.float32),
        lax.psum_scatter(
            gain_cross_grad.astype(jnp.bfloat16), "wide", scatter_dimension=0, tiled=True
        ).astype(jnp.float32),
        lax.psum_scatter(
            gain_ff_grad.astype(jnp.bfloat16), "wide", scatter_dimension=0, tiled=True
        ).astype(jnp.float32),
        lax.psum_scatter(
            gain_exit_grad.astype(jnp.bfloat16), "wide", scatter_dimension=0, tiled=True
        ).astype(jnp.float32),
    )
    totals = (
        lax.psum(shards[0].astype(jnp.bfloat16), "grp").astype(jnp.float32),
        lax.psum(shards[1].astype(jnp.bfloat16), "grp").astype(jnp.float32),
        lax.psum(shards[2].astype(jnp.bfloat16), "grp").astype(jnp.float32),
        lax.psum(shards[3].astype(jnp.bfloat16), "grp").astype(jnp.float32),
        lax.psum(shards[4].astype(jnp.bfloat16), "grp").astype(jnp.float32),
        lax.psum(shards[5].astype(jnp.bfloat16), "grp").astype(jnp.float32),
        lax.psum(shards[6].astype(jnp.bfloat16), "grp").astype(jnp.float32),
        lax.psum(shards[7].astype(jnp.bfloat16), "grp").astype(jnp.float32),
        lax.psum(shards[8].astype(jnp.bfloat16), "grp").astype(jnp.float32),
        lax.psum(shards[9].astype(jnp.bfloat16), "grp").astype(jnp.float32),
        lax.psum(shards[10].astype(jnp.bfloat16), "grp").astype(jnp.float32),
        lax.psum(shards[11].astype(jnp.bfloat16), "grp").astype(jnp.float32),
        lax.psum(shards[12].astype(jnp.bfloat16), "grp").astype(jnp.float32),
        lax.psum(shards[13].astype(jnp.bfloat16), "grp").astype(jnp.float32),
        lax.psum(shards[14].astype(jnp.bfloat16), "grp").astype(jnp.float32),
        lax.psum(exit_grad.astype(jnp.bfloat16), "grp").astype(jnp.float32),
        lax.psum(group_loss.astype(jnp.bfloat16), "grp").astype(jnp.float32),
    )
    return (
        block_output,
        totals[16],
        input_grad,
        memory_grad,
        totals[0],
        totals[1],
        totals[2],
        totals[3],
        totals[4],
        totals[5],
        totals[6],
        totals[7],
        totals[8],
        totals[9],
        totals[10],
        totals[11],
        totals[12],
        totals[13],
        totals[14],
        totals[15],
    )


MESH = pl.DeviceIdType.MESH
BF = jnp.bfloat16
F32 = jnp.float32
VMEM_BYTES = 63 << 20


def dot_nn(left, right):
    return lax.dot_general(left, right, (((1,), (0,)), ((), ())), preferred_element_type=F32)


def dot_nt(left, right):
    return lax.dot_general(left, right, (((1,), (1,)), ((), ())), preferred_element_type=F32)


def dot_tn(left, right):
    return lax.dot_general(left, right, (((0,), (0,)), ((), ())), preferred_element_type=F32)


class Move:
    def __init__(self, out, arrival):
        self.out, self.arrival = out, arrival

    def start(self):
        self.out.start()
        return self

    def sent(self):
        self.out.wait_send()

    def landed(self):
        self.arrival.wait_recv()


class Links:
    def __init__(self, send_sems, recv_sems):
        self.send_sems, self.recv_sems = send_sems, recv_sems
        self.used = 0
        self.moves = []

    def move(self, src, dst, device, lands):
        k = self.used
        self.used += 1
        out = pltpu.make_async_remote_copy(
            src_ref=src, dst_ref=dst, send_sem=self.send_sems.at[k], recv_sem=self.recv_sems.at[k],
            device_id=device, device_id_type=MESH,
        )
        arrival = pltpu.make_async_remote_copy(
            src_ref=lands, dst_ref=lands, send_sem=self.send_sems.at[k], recv_sem=self.recv_sems.at[k],
            device_id=device, device_id_type=MESH,
        )
        made = Move(out, arrival)
        self.moves.append(made)
        return made

    def finish(self):
        for made in self.moves:
            made.sent()

    def finish_rest(self, done):
        for made in self.moves:
            if made not in done:
                made.sent()


class Copies:
    def __init__(self, sems):
        self.sems, self.used, self.pending = sems, 0, []

    def start(self, src, dst):
        made = pltpu.make_async_copy(src, dst, self.sems.at[self.used])
        self.used += 1
        made.start()
        return made

    def save(self, src, dst):
        self.pending.append(self.start(src, dst))

    def finish(self):
        for made in self.pending:
            made.wait()


def greet(devices):
    barrier = pltpu.get_barrier_semaphore()
    for device in devices:
        pl.semaphore_signal(barrier, inc=1, device_id=device, device_id_type=MESH)
    pl.semaphore_wait(barrier, len(devices))


def position(count):
    g, w, t = lax.axis_index("grp"), lax.axis_index("wide"), lax.axis_index("tp")
    c = lax.rem(g, 2)
    left, right, far = (lax.rem(w + d, count) for d in (count - 1, 1, 2))
    return types.SimpleNamespace(
        count=count, g=g, w=w, t=t, c=c, yy=lax.div(g, 2), left=left, right=right, far=far,
        to_left={"wide": left}, to_right={"wide": right}, to_far={"wide": far},
        to_core={"grp": g + 1 - 2 * c}, to_y={"grp": lax.rem(g + 2, 4)}, to_tp={"tp": 1 - t},
    )


def rms_rows(values, gain):
    factor = lax.rsqrt(jnp.mean(values * values, axis=1, keepdims=True) + EPSILON)
    return (values * factor * gain).astype(BF)


def lane_masks():
    lane = lax.broadcasted_iota(jnp.int32, (1, 2 * HEAD_DIM), 1)
    low = jnp.where(lane < HEAD_DIM, 1.0, 0.0).astype(F32)
    return low.astype(BF), (1.0 - low).astype(BF)


def both_heads(pair):
    low, high = lane_masks()
    return jnp.concatenate([pair * low, pair * high], axis=0)


def pick_heads(stacked):
    rows = stacked.shape[0] // 2
    lane = lax.broadcasted_iota(jnp.int32, (rows, 2 * HEAD_DIM), 1)
    return jnp.where(lane < HEAD_DIM, stacked[:rows], stacked[rows:])


def pair_columns(p):
    return pl.ds(pl.multiple_of(p * 2 * HEAD_DIM, 2 * HEAD_DIM), 2 * HEAD_DIM)


def attention_forward(pairs, queries, keys, values, probs, context, allowed):
    factor = HEAD_DIM ** (-0.5)

    def step(p, carry):
        cols = pair_columns(p)
        scores = dot_nt(both_heads(queries[:, cols]), keys[:, cols]) * factor
        scores = jnp.where(allowed, scores, MASKED)
        exponent = jnp.exp(scores - jnp.max(scores, axis=1, keepdims=True))
        soft = (exponent / jnp.sum(exponent, axis=1, keepdims=True)).astype(BF)
        probs[p] = soft
        context[:, cols] = pick_heads(dot_nn(soft, values[:, cols])).astype(BF)
        return carry

    lax.fori_loop(0, pairs, step, 0)


def slot_choice(own_map, slots, count, part=None):
    rows = own_map.shape[1]
    capacity = slots // count
    reader_iota = lax.broadcasted_iota(jnp.int32, (max(8, count), rows), 0)
    matched = jnp.where(reader_iota == own_map, 1.0, 0.0).astype(F32)
    before = lax.broadcasted_iota(jnp.int32, (rows, rows), 0) < lax.broadcasted_iota(jnp.int32, (rows, rows), 1)
    ranks = dot_nn(matched.astype(BF), jnp.where(before, 1.0, 0.0).astype(BF))
    rank = jnp.sum(matched * ranks, axis=0, keepdims=True).astype(jnp.int32)
    if part is None:
        slot_of = own_map * capacity + rank
    else:
        slots, capacity = slots // 2, capacity // 2
        rank = rank - part * capacity
        slot_of = jnp.where((rank >= 0) & (rank < capacity), own_map * capacity + rank, -1)
    slot_iota = lax.broadcasted_iota(jnp.int32, (slots, rows), 0)
    return jnp.where(slot_iota == slot_of, 1.0, 0.0).astype(BF)


class Gather:
    def __init__(self, here, links, buf, first, depth, placed):
        self.here, self.links, self.buf, self.placed = here, links, buf, placed
        self.mine, self.other = first + here.c, first + 1 - here.c
        self.depth = depth

    def rows(self, at, start, parts):
        size = self.depth // parts
        return pl.ds(pl.multiple_of(at * self.depth + start * size, 16), size)

    def y_half(self, at):
        return self.rows(at, self.here.yy, 2)

    def quarter(self, at, which):
        return self.rows(at, 2 * self.here.yy + which, 4)

    def send(self, where, device, lands, index=None):
        src = self.buf.at[self.mine, where]
        land = self.buf.at[self.mine if index is None else index, lands]
        return self.links.move(src, src, device, land).start()

    def issue(self):
        here = self.here
        for made in self.placed:
            made.wait()
        own = self.y_half(here.w)
        self.from_left = self.send(own, here.to_right, self.y_half(here.left))
        self.from_right = self.send(own, here.to_left, self.y_half(here.right))

    def to_y(self, at):
        return self.send(self.y_half(at), self.here.to_y, self.rows(at, 1 - self.here.yy, 2))

    def forward(self):
        here = self.here
        self.from_left.landed()
        self.far_top = self.send(self.quarter(here.left, 0), here.to_right, self.quarter(here.far, 0))
        self.over_y = [self.to_y(here.left)]
        self.from_right.landed()
        self.far_low = self.send(self.quarter(here.right, 1), here.to_left, self.quarter(here.far, 1))
        self.over_y.append(self.to_y(here.right))

    def complete(self):
        self.far_top.landed()
        self.far_low.landed()
        self.over_y.append(self.to_y(self.here.far))

    def share(self):
        here = self.here
        self.cores = []
        for made, at in zip(self.over_y, (here.left, here.right, here.far)):
            made.landed()
            whole = self.rows(at, 0, 1)
            self.cores.append(self.send(whole, here.to_core, whole, self.other))

    def ready(self):
        for made in self.cores:
            made.landed()


def forward_kernel(
    count, x_ref, mem_ref, map_ref, len_ref, gs_ref, gc_ref, gf_ref, ge_ref,
    q_in, k_in, v_in, so_in, cq_in, ck_in, cv_in, co_in, ga_in, up_in, dn_in,
    block_o, one_o, two_o, three_o, exit_o, q_o, k_o, v_o, cq_o, mk_o, mv_o, sc_o, cc_o, ps_o, pc_o,
    ga_o, up_o, sel_o, wa_o, wgu_o, wd_o, gain_o,
    wa, wgu, wd, gains, slots, packed, part_out, part_in, valid_slot,
    block, one, two, three, exit_rows, q, k, v, cq, mk, mv, sc, cc, ps, pc, ga, up, gain_sum,
    send_sems, recv_sems, copy_sems,
):
    here = position(count)
    g, w, t = here.g, here.w, here.t
    left, right, far = here.left, here.right, here.far
    to_left, to_right, to_far, to_tp = here.to_left, here.to_right, here.to_far, here.to_tp
    rows = x_ref.shape[0]
    links, copies = Links(send_sems, recv_sems), Copies(copy_sems)
    depth = q_in.shape[0]
    wide_cols = dn_in.shape[1] // 2

    own = pl.ds(pl.multiple_of(w * depth, 16), depth)
    order = (q_in, k_in, v_in, so_in, ck_in, cv_in, cq_in, co_in)
    weights = []
    for j in range(4):
        placed = [copies.start(order[2 * j + e], wa.at[2 * j + e, own]) for e in range(2)]
        weights.append(Gather(here, links, wa, 2 * j, depth, placed))
    placed = [copies.start(ref, wgu.at[e, own]) for e, ref in enumerate((ga_in, up_in))]
    weights.append(Gather(here, links, wgu, 0, depth, placed))
    placed = [copies.start(dn_in.at[:, pl.ds(e * wide_cols, wide_cols)], wd.at[e, own]) for e in range(2)]
    weights.append(Gather(here, links, wd, 0, depth, placed))

    gain_sum[...] = jnp.zeros_like(gain_sum)
    for n, ref in enumerate((gs_ref, gc_ref, gf_ref, ge_ref)):
        gain_sum[n : n + 1, 0:depth] = ref[...].astype(F32).reshape(1, depth)
    gains[w] = pltpu.roll(gain_sum[...], w * depth, 1)
    greet([to_left, to_right, to_far, here.to_core, here.to_y, to_tp])
    gain_moves = [
        links.move(gains.at[w], gains.at[w], device, gains.at[at]).start()
        for device, at in ((to_left, right), (to_right, left), (to_far, far))
    ]
    for first in weights[:3]:
        first.issue()

    capacity = slots.shape[0] // count
    choose = slot_choice(map_ref[:, pl.ds(pl.multiple_of(w * rows, rows), rows)], slots.shape[0], count)
    packed[...] = dot_nn(choose, mem_ref[...]).astype(BF)

    def slot_rows(at, which):
        return pl.ds(pl.multiple_of(at * capacity + which * (capacity // 2), 16), capacity // 2)

    own_slots = pl.ds(pl.multiple_of(w * capacity, 16), capacity)
    slots[own_slots, :] = packed[own_slots, :]
    weights[0].forward()
    weights[3].issue()
    for made in gain_moves:
        made.landed()
    total_gain = gains[0]
    for at in range(1, count):
        total_gain = total_gain + gains[at]
    gain_sum[...] = total_gain
    hidden = x_ref[...].astype(F32)
    norm_self = rms_rows(hidden, gain_sum[0:1, :])
    weights[1].forward()
    weights[0].complete()
    slot_moves = [
        links.move(packed.at[slot_rows(to, t)], slots.at[slot_rows(w, t)], device, slots.at[slot_rows(at, t)]).start()
        for device, to, at in ((to_left, left, right), (to_right, right, left), (to_far, far, far))
    ]
    weights[2].forward()
    weights[0].share()
    weights[1].complete()
    weights[1].share()
    weights[4].issue()
    weights[0].ready()
    q[...] = dot_nn(norm_self, wa[0]).astype(BF)
    k[...] = dot_nn(norm_self, wa[1]).astype(BF)
    weights[2].complete()
    weights[1].ready()
    v[...] = dot_nn(norm_self, wa[2]).astype(BF)
    weights[3].forward()
    weights[2].share()
    weights[5].issue()
    weights[3].complete()
    slot_fills = []
    for made, at in zip(slot_moves, (right, left, far)):
        made.landed()
        src = slots.at[slot_rows(at, t)]
        slot_fills.append(links.move(src, src, to_tp, slots.at[slot_rows(at, 1 - t)]).start())
    length = len_ref[g * count + w]
    query_at = lax.broadcasted_iota(jnp.int32, (2 * rows, rows), 0)
    query_at = jnp.where(query_at >= rows, query_at - rows, query_at)
    key_at = lax.broadcasted_iota(jnp.int32, (2 * rows, rows), 1)
    allowed_self = (key_at <= query_at) & (key_at < length)
    pairs = q.shape[1] // (2 * HEAD_DIM)
    attention_forward(pairs, q, k, v, ps, sc, allowed_self)

    def exchange_start(n):
        return links.move(part_out.at[n], part_in.at[n], to_tp, part_in.at[n]).start()

    def exchanged(n, made):
        made.landed()
        return part_out[n].astype(F32) + part_in[n].astype(F32)

    part_out[0] = dot_nt(sc[...], wa[3]).astype(BF)
    swap = exchange_start(0)
    weights[3].share()
    weights[4].forward()
    for made in slot_fills:
        made.landed()
    place = lax.broadcasted_iota(jnp.int32, (1, capacity), 1).astype(F32)
    for b in range(count):
        reads = jnp.sum(jnp.where(map_ref[:, b * rows : (b + 1) * rows] == w, 1.0, 0.0), axis=1, keepdims=True)
        valid_slot[0:1, b * capacity : (b + 1) * capacity] = jnp.where(place < reads, 1.0, 0.0)
    weights[2].ready()
    mk[...] = dot_nn(slots[...], wa[4]).astype(BF)
    mv[...] = dot_nn(slots[...], wa[5]).astype(BF)
    weights[4].complete()
    weights[5].forward()
    allowed_cross = jnp.broadcast_to(valid_slot[0:1, :], (2 * rows, slots.shape[0])) > 0.5
    one[...] = hidden + exchanged(0, swap)
    norm_cross = rms_rows(one[...], gain_sum[1:2, :])
    weights[3].ready()
    cq[...] = dot_nn(norm_cross, wa[6]).astype(BF)
    weights[4].share()
    weights[5].complete()
    attention_forward(pairs, cq, mk, mv, pc, cc, allowed_cross)
    part_out[1] = dot_nt(cc[...], wa[7]).astype(BF)
    swap = exchange_start(1)
    weights[5].share()
    copies.save(wa, wa_o)
    for src, dst in (
        (q, q_o), (k, k_o), (v, v_o), (sc, sc_o), (ps, ps_o), (mk, mk_o), (mv, mv_o), (cq, cq_o), (cc, cc_o), (pc, pc_o),
        (slots, sel_o), (one, one_o), (gain_sum, gain_o),
    ):
        copies.save(src, dst)
    two[...] = one[...] + exchanged(1, swap)
    copies.save(two, two_o)
    norm_ff = rms_rows(two[...], gain_sum[2:3, :])
    weights[4].ready()
    copies.save(wgu, wgu_o)
    ga[...] = dot_nn(norm_ff, wgu[0]).astype(BF)
    up[...] = dot_nn(norm_ff, wgu[1]).astype(BF)
    copies.save(ga, ga_o)
    copies.save(up, up_o)
    ff_hidden = (smooth_gate(ga[...].astype(F32)) * up[...].astype(F32)).astype(BF)
    weights[5].ready()
    copies.save(wd, wd_o)
    part_out[2] = (
        dot_nt(ff_hidden[:, :wide_cols], wd[0]) + dot_nt(ff_hidden[:, wide_cols:], wd[1])
    ).astype(BF)
    swap = exchange_start(2)
    three[...] = two[...] + exchanged(2, swap)
    block[...] = three[...].astype(BF)
    exit_rows[...] = rms_rows(three[...], gain_sum[3:4, :])
    copies.save(three, three_o)
    copies.save(block, block_o)
    copies.save(exit_rows, exit_o)
    links.finish()
    copies.finish()


def forward_layer(count, layer_input, memory, group_map, lengths, gain_parts, weights):
    rows, width = layer_input.shape
    heads = weights[0].shape[1]
    units = weights[8].shape[1]
    slots = count * max(2, 2 * rows // count)
    pairs = heads // (2 * HEAD_DIM)
    kept = [
        ((rows, width), BF), ((rows, width), F32), ((rows, width), F32), ((rows, width), F32), ((rows, width), BF),
        ((rows, heads), BF), ((rows, heads), BF), ((rows, heads), BF), ((rows, heads), BF),
        ((slots, heads), BF), ((slots, heads), BF), ((rows, heads), BF), ((rows, heads), BF),
        ((pairs, 2 * rows, rows), BF), ((pairs, 2 * rows, slots), BF),
        ((rows, units), BF), ((rows, units), BF), ((slots, width), BF),
        ((8, width, heads), BF), ((2, width, units), BF), ((2, width, units // 2), BF), ((8, width), F32),
    ]
    vmem, hbm = pl.BlockSpec(memory_space=pltpu.VMEM), pl.BlockSpec(memory_space=pl.ANY)
    scratch = [
        pltpu.VMEM((8, width, heads), BF), pltpu.VMEM((2, width, units), BF), pltpu.VMEM((2, width, units // 2), BF),
        pltpu.VMEM((count, 8, width), F32), pltpu.VMEM((slots, width), BF), pltpu.VMEM((slots, width), BF),
        pltpu.VMEM((3, rows, width), BF), pltpu.VMEM((3, rows, width), BF), pltpu.VMEM((8, slots), F32),
    ]
    scratch += [pltpu.VMEM(shape, kind) for shape, kind in kept[:17]]
    scratch += [pltpu.VMEM((8, width), F32)]
    scratch += [pltpu.SemaphoreType.DMA((80,)), pltpu.SemaphoreType.DMA((80,)), pltpu.SemaphoreType.DMA((40,))]
    return pl.pallas_call(
        functools.partial(forward_kernel, count),
        out_shape=[jax.ShapeDtypeStruct(shape, kind) for shape, kind in kept],
        in_specs=[vmem, vmem, vmem, pl.BlockSpec(memory_space=pltpu.SMEM)] + [vmem] * 4 + [hbm] * 11,
        out_specs=[hbm] * len(kept),
        scratch_shapes=scratch,
        compiler_params=pltpu.CompilerParams(
            collective_id=0, has_side_effects=True, vmem_limit_bytes=VMEM_BYTES
        ),
        name="forward_layer",
    )(layer_input, memory, group_map, lengths, *gain_parts, *weights)


CHUNK = 512
CROSSED = 0


def tall(rows):
    return -(-rows // (2 * CHUNK)) * 2 * CHUNK


def span(at, size):
    return pl.ds(pl.multiple_of(at * size, size), size)


def exit_phase(here, links, load, rows_own, tab, tabt, gt, rb, ids, lens, high, total, stats, stats_tp, stats_wide, coef, weight, acc,
               dx, joint, land_tp, land_far, land_near, swap_out, swap_in, grad_out, vocab, fillers):
    count, g, w, t = here.count, here.g, here.w, here.t
    left, right, far = here.left, here.right, here.far
    to_left, to_right, to_far, to_tp = here.to_left, here.to_right, here.to_far, here.to_tp
    rows, width = rows_own.shape
    half, quarter = rows // 2, rows // 4
    chunks = tab.shape[0] // CHUNK
    scale = float(width) ** (-0.5)
    base = (w * 2 + t) * vocab
    tokens = count * rows

    def block(b):
        return span(b, rows)

    def halved(b, which):
        return pl.ds(pl.multiple_of(b * rows + which * half, half), half)

    def quartered(b, which):
        return pl.ds(pl.multiple_of(b * rows + t * half + which * quarter, quarter), quarter)

    rb[block(w), :] = rows_own[...]
    src = rb.at[halved(w, t)]
    from_left = links.move(src, src, to_right, rb.at[halved(left, t)]).start()
    from_right = links.move(src, src, to_left, rb.at[halved(right, t)]).start()

    def to_other_half(b):
        src = rb.at[halved(b, t)]
        return links.move(src, src, to_tp, rb.at[halved(b, 1 - t)]).start()

    def target_row(cols):
        row = ids[:, cols] - base
        return jnp.where(row < vocab, row, -1)

    def flip(j, carry):
        tabt[:, span(j, CHUNK)] = tab[span(j, CHUNK), :].T
        return carry

    def score(b):
        cols = block(b)
        wanted = target_row(cols)
        block_rows = rb[cols, :]

        def step(j, pick):
            at = lax.broadcasted_iota(jnp.int32, (CHUNK, rows), 0) + j * CHUNK
            logits = dot_nt(tab[span(j, CHUNK), :], block_rows) * scale
            logits = jnp.where(at < vocab, logits, MASKED)
            top = jnp.max(logits, axis=0, keepdims=True)
            exponent = jnp.exp(logits - top)
            high[pl.ds(j, 1), cols] = top
            total[pl.ds(j, 1), cols] = jnp.sum(exponent, axis=0, keepdims=True)
            gt[span(j, CHUNK), cols] = exponent.astype(BF)
            return pick + jnp.sum(jnp.where(at == wanted, logits, 0.0), axis=0, keepdims=True)

        pick = lax.fori_loop(0, chunks, step, jnp.zeros((1, rows), F32), unroll=True)
        tops = high[:, cols]
        top = jnp.max(tops, axis=0, keepdims=True)
        stats[0:1, cols] = top
        stats[1:2, cols] = jnp.sum(total[:, cols] * jnp.exp(tops - top), axis=0, keepdims=True)
        stats[2:3, cols] = pick

    load.wait()
    score(w)
    from_left.landed()
    src = rb.at[quartered(left, 0)]
    far_top = links.move(src, src, to_right, rb.at[quartered(far, 0)]).start()
    left_rest = to_other_half(left)
    from_right.landed()
    src = rb.at[quartered(right, 1)]
    far_low = links.move(src, src, to_left, rb.at[quartered(far, 1)]).start()
    right_rest = to_other_half(right)
    lax.fori_loop(0, chunks, flip, 0)
    left_rest.landed()
    score(left)
    far_top.landed()
    far_low.landed()
    far_rest = to_other_half(far)
    right_rest.landed()
    score(right)
    far_rest.landed()
    score(far)

    def merged_stats(parts):
        top = parts[0][0:1]
        for part in parts[1:]:
            top = jnp.maximum(top, part[0:1])
        mass = sum(part[1:2] * jnp.exp(part[0:1] - top) for part in parts)
        pick = sum(part[2:3] for part in parts)
        return top, mass, pick

    swap = links.move(stats, stats_tp, to_tp, stats_tp).start()
    lengths = [lens[k] for k in range(lens.shape[0])]
    tokens_all = lengths[0]
    for length in lengths[1:]:
        tokens_all = tokens_all + length
    place = lax.broadcasted_iota(jnp.int32, (1, rows), 1)
    for b in range(count):
        inside = jnp.where(place < lens[g * count + b], 1.0, 0.0).astype(F32)
        weight[0:1, b * rows : (b + 1) * rows] = inside / tokens_all.astype(F32)
    swap.landed()
    mine, other = stats[...], stats_tp[...]
    top, mass, pick = merged_stats([mine, other])
    mine_wide = stats_wide.at[w]
    mine_wide[0:1, :] = top
    mine_wide[1:2, :] = mass
    mine_wide[2:3, :] = pick
    spreads = [
        links.move(mine_wide, mine_wide, device, stats_wide.at[at]).start()
        for device, at in ((to_left, right), (to_right, left), (to_far, far))
    ]
    for made in spreads:
        made.landed()
    top, mass, pick = merged_stats([stats_wide[b] for b in range(count)])
    log_total = top + jnp.log(mass)
    all_weight = weight[0:1, :]
    coef[...] = jnp.exp(high[...] - log_total) * all_weight
    stats_tp[3:4, :] = (log_total - pick) * all_weight
    loss = jnp.sum(stats_tp[3:4, block(w)], axis=1, keepdims=True)

    def row_grads(b):
        cols = block(b)
        wanted = target_row(cols)
        own_weight = weight[0:1, cols]
        acc[...] = jnp.zeros_like(acc)

        def step(j, carry):
            at = lax.broadcasted_iota(jnp.int32, (CHUNK, rows), 0) + j * CHUNK
            grad = gt[span(j, CHUNK), cols].astype(F32) * coef[pl.ds(j, 1), cols]
            grad = (grad - jnp.where(at == wanted, own_weight, 0.0)).astype(BF)
            gt[span(j, CHUNK), cols] = grad
            acc[...] += dot_nn(tabt[:, span(j, CHUNK)], grad)
            return carry

        lax.fori_loop(0, chunks, step, 0, unroll=True)
        return (acc[...] * scale).astype(BF).T

    own_half, other_half = (span(which, half) for which in (t, 1 - t))

    def start_block(slot, b):
        dx[slot] = row_grads(b)
        return links.move(dx.at[slot, other_half], land_tp.at[slot], to_tp, land_tp.at[slot]).start()

    def join_block(slot, made):
        made.landed()
        joint[slot] = (dx[slot, own_half].astype(F32) + land_tp[slot].astype(F32)).astype(BF)

    parts = [pl.ds(which * quarter, quarter) for which in range(2)]

    def near(slot, which, side, device):
        where = parts[which]
        return links.move(joint.at[slot, where], land_near.at[side, where], device, land_near.at[side, where]).start()

    made_far = start_block(0, far)
    made_right = start_block(1, right)
    join_block(0, made_far)
    far_moves = [
        links.move(joint.at[0, parts[which]], land_far.at[which], device, land_far.at[which]).start()
        for which, device in enumerate((to_right, to_left))
    ]
    made_left = start_block(2, left)
    join_block(1, made_right)
    right_low = near(1, 1, 0, to_right)
    made_own = start_block(3, w)
    fillers[0]()
    join_block(2, made_left)
    left_top = near(2, 0, 1, to_left)
    near_late = []
    for which, slot, device in ((0, 1, to_right), (1, 2, to_left)):
        far_moves[which].landed()
        where = parts[which]
        joint[slot, where] = (joint[slot, where].astype(F32) + land_far[which].astype(F32)).astype(BF)
        near_late.append(near(slot, which, which, device))
    fillers[1]()
    join_block(3, made_own)
    for made in [right_low, left_top] + near_late:
        made.landed()
    swap_out[...] = (joint[3].astype(F32) + land_near[0].astype(F32) + land_near[1].astype(F32)).astype(BF)
    swap = links.move(swap_out, swap_in, to_tp, swap_in).start()
    fillers[2]()
    grad_out[own_half, :] = swap_out[...].astype(F32)
    swap.landed()
    grad_out[other_half, :] = swap_in[...].astype(F32)
    return loss


class TableGrad:
    def __init__(self, here, links, copies, tab, gt, rb, land_core, land_y, out):
        self.here, self.links, self.copies = here, links, copies
        self.tab, self.gt, self.rb, self.land_core, self.land_y, self.out = tab, gt, rb, land_core, land_y, out
        self.pieces = tab.shape[0] // (2 * CHUNK)
        self.scale = float(tab.shape[1]) ** (-0.5)
        self.cores, self.ys = [], []

    def rows(self, owner, i):
        return pl.ds(pl.multiple_of((owner * self.pieces + i) * CHUNK, CHUNK), CHUNK)

    def product(self, where):
        return dot_nn(self.gt[where, :], self.rb[...]) * self.scale

    def first_half(self):
        c = self.here.c
        for i in range(self.pieces):
            where = self.rows(1 - c, i)
            self.tab[where, :] = self.product(where).astype(BF)
            land = self.land_core.at[pl.ds(i * CHUNK, CHUNK)]
            self.cores.append(self.links.move(self.tab.at[where], land, self.here.to_core, land).start())

    def second_half(self):
        c = self.here.c
        for i in range(self.pieces):
            where = self.rows(c, i)
            mine = self.product(where)
            self.cores[i].landed()
            self.tab[where, :] = (mine + self.land_core[i * CHUNK : (i + 1) * CHUNK, :].astype(F32)).astype(BF)
            if i < CROSSED:
                land = self.land_y.at[pl.ds(i * CHUNK, CHUNK)]
                self.ys.append(self.links.move(self.tab.at[where], land, self.here.to_y, land).start())
            else:
                self.copies.save(self.tab.at[where], self.out.at[pl.ds(i * CHUNK, CHUNK)])

    def settle(self):
        for i in range(CROSSED):
            where = self.rows(self.here.c, i)
            piece = pl.ds(i * CHUNK, CHUNK)
            self.ys[i].landed()
            self.ys[i].sent()
            self.tab[where, :] = (self.tab[where, :].astype(F32) + self.land_y[piece, :].astype(F32)).astype(BF)
            self.copies.save(self.tab.at[where], self.out.at[piece])


def exit_kernel(
    count, vocab, rows_own, ids, lens, table, grad_o, loss_o, half_o,
    tab, tabt, gt, rb, high, total, stats, stats_tp, stats_wide, coef, weight, acc, dx, joint, land_tp, land_far, land_near, swap_out, swap_in,
    land_core, land_y, send_sems, recv_sems, copy_sems,
):
    here = position(count)
    links, copies = Links(send_sems, recv_sems), Copies(copy_sems)
    load = copies.start(table, tab.at[pl.ds(0, vocab)])
    greet([here.to_left, here.to_right, here.to_far, here.to_core, here.to_y, here.to_tp])
    tab[vocab:, :] = jnp.zeros((tab.shape[0] - vocab, tab.shape[1]), BF)
    grads = TableGrad(here, links, copies, tab, gt, rb, land_core, land_y, half_o)
    loss = exit_phase(here, links, load, rows_own, tab, tabt, gt, rb, ids, lens, high, total, stats, stats_tp, stats_wide, coef, weight,
                      acc, dx, joint, land_tp, land_far, land_near, swap_out, swap_in, grad_o, vocab,
                      (grads.first_half, grads.second_half, grads.settle))
    loss_o[...] = jnp.broadcast_to(loss, loss_o.shape)
    links.finish_rest(grads.ys)
    copies.finish()


def exit_head(count, norm_exit, ids, lengths, table):
    vocab, width = table.shape
    rows = norm_exit.shape[0]
    high = tall(vocab)
    chunks = high // CHUNK
    tokens = rows * count
    vmem, hbm = pl.BlockSpec(memory_space=pltpu.VMEM), pl.BlockSpec(memory_space=pl.ANY)
    return pl.pallas_call(
        functools.partial(exit_kernel, count, vocab),
        out_shape=[
            jax.ShapeDtypeStruct((rows, width), F32), jax.ShapeDtypeStruct((8, 128), F32),
            jax.ShapeDtypeStruct((high // 2, width), BF),
        ],
        in_specs=[vmem, vmem, pl.BlockSpec(memory_space=pltpu.SMEM), hbm],
        out_specs=[vmem, vmem, hbm],
        scratch_shapes=[
            pltpu.VMEM((high, width), BF), pltpu.VMEM((width, high), BF), pltpu.VMEM((high, tokens), BF),
            pltpu.VMEM((tokens, width), BF), pltpu.VMEM((chunks, tokens), F32), pltpu.VMEM((chunks, tokens), F32),
            pltpu.VMEM((8, tokens), F32), pltpu.VMEM((8, tokens), F32), pltpu.VMEM((count, 8, tokens), F32),
            pltpu.VMEM((chunks, tokens), F32), pltpu.VMEM((8, tokens), F32), pltpu.VMEM((width, rows), F32),
            pltpu.VMEM((4, rows, width), BF), pltpu.VMEM((4, rows // 2, width), BF), pltpu.VMEM((4, rows // 2, width), BF),
            pltpu.VMEM((2, rows // 4, width), BF), pltpu.VMEM((2, rows // 2, width), BF),
            pltpu.VMEM((rows // 2, width), BF), pltpu.VMEM((rows // 2, width), BF),
            pltpu.VMEM((high // 2, width), BF), pltpu.VMEM((max(8, CROSSED * CHUNK), width), BF),
            pltpu.SemaphoreType.DMA((40,)), pltpu.SemaphoreType.DMA((40,)), pltpu.SemaphoreType.DMA((16,)),
        ],
        compiler_params=pltpu.CompilerParams(
            collective_id=1, has_side_effects=True, vmem_limit_bytes=VMEM_BYTES
        ),
        name="exit_head",
    )(norm_exit, ids, lengths, table)


GELU_SCALE = 0.7978845608028654
GELU_CUBE = 0.044715


def norm_back(values, gain, grad):
    factor = lax.rsqrt(jnp.mean(values * values, axis=1, keepdims=True) + EPSILON)
    unit = values * factor
    scaled = grad * gain
    inner = jnp.mean(scaled * values, axis=1, keepdims=True)
    return jnp.sum(grad * unit, axis=0, keepdims=True), factor * scaled - unit * (factor * factor * inner)


def attention_backward(pairs, queries, keys, values, probs, context_grad, query_grad, key_grad, value_grad):
    factor = HEAD_DIM ** (-0.5)

    def step(p, carry):
        cols = pair_columns(p)
        grad = both_heads(context_grad[:, cols])
        soft = probs[p]
        soft_float = soft.astype(F32)
        soft_grad = dot_nt(grad, values[:, cols])
        inner = jnp.sum(soft_float * soft_grad, axis=1, keepdims=True)
        score_grad = (soft_float * (soft_grad - inner)).astype(BF)
        query_grad[:, cols] = (pick_heads(dot_nn(score_grad, keys[:, cols])) * factor).astype(BF)
        key_grad[:, cols] = (dot_tn(score_grad, both_heads(queries[:, cols])) * factor).astype(BF)
        value_grad[:, cols] = dot_tn(soft, grad).astype(BF)
        return carry

    lax.fori_loop(0, pairs, step, 0)


class WeightGrad:
    def __init__(self, here, links, copies, grads, first, depth, land_core, land_far, land_near, land_y, mine_out, out):
        self.here, self.links, self.copies = here, links, copies
        self.grads, self.mine, self.other = grads, first + here.c, first + 1 - here.c
        self.depth, self.half = depth, depth // 2
        self.land_core, self.land_far, self.land_near, self.land_y = land_core, land_far, land_near, land_y
        self.mine_out, self.out = mine_out, out

    def whole(self, at):
        return pl.ds(pl.multiple_of(at * self.depth, 16), self.depth)

    def part(self, at, which):
        return pl.ds(pl.multiple_of(at * self.depth + which * self.half, 16), self.half)

    def pair(self):
        self.core = self.links.move(
            self.grads.at[self.other], self.land_core, self.here.to_core, self.land_core
        ).start()

    def near(self, where, side, which, device):
        rows = pl.ds(which * self.half, self.half)
        return self.links.move(
            self.grads.at[self.mine, where], self.land_near.at[side, rows], device, self.land_near.at[side, rows]
        ).start()

    def add_core(self, where):
        self.grads[self.mine, where] = (
            self.grads[self.mine, where].astype(F32) + self.land_core[where].astype(F32)
        ).astype(BF)

    def ring(self):
        here = self.here
        self.core.landed()
        for at in (here.far, here.right, here.left):
            self.add_core(self.whole(at))
            if at is here.far:
                self.far = [
                    self.links.move(
                        self.grads.at[self.mine, self.part(at, e)], self.land_far.at[e], way, self.land_far.at[e]
                    ).start()
                    for e, way in enumerate((here.to_right, here.to_left))
                ]
        self.early = [
            self.near(self.part(here.right, 1), 0, 1, here.to_right),
            self.near(self.part(here.left, 0), 1, 0, here.to_left),
        ]
        self.add_core(self.whole(here.w))

    def pass_on(self):
        here = self.here
        self.late = []
        for e, side, way in ((0, here.right, here.to_right), (1, here.left, here.to_left)):
            self.far[e].landed()
            where = self.part(side, e)
            self.grads[self.mine, where] = (
                self.grads[self.mine, where].astype(F32) + self.land_far[e].astype(F32)
            ).astype(BF)
            self.late.append(self.near(where, e, e, way))

    def across(self):
        for made in self.early + self.late:
            made.landed()
        where = self.whole(self.here.w)
        self.mine_out[0] = (
            self.grads[self.mine, where].astype(F32) + self.land_near[0].astype(F32) + self.land_near[1].astype(F32)
        ).astype(BF)
        self.y = self.links.move(self.mine_out.at[0], self.land_y, self.here.to_y, self.land_y).start()

    def settle(self):
        self.y.landed()
        self.mine_out[1] = (self.mine_out[0].astype(F32) + self.land_y[...].astype(F32)).astype(BF)
        src = self.mine_out.at[1]
        self.copies.save(src, self.out.at[self.mine])
        self.share = self.links.move(
            src, self.out.at[self.mine], self.here.to_core, self.out.at[self.other]
        ).start()

    def done(self):
        self.share.landed()


def backward_kernel(
    count,
    lens, map_ref, x_h, og_h, eg_h, loss_h, one_h, two_h, three_h, q_h, k_h, v_h, cq_h, mk_h, mv_h, sc_h, cc_h, ps_h, pc_h,
    ga_h, up_h, sel_h, wa_h, wgu_h, wd_h, gain_h, half_h,
    in_o, mem_o, small_o, ga8_o, ggu_o, gd_o, table_o,
    x, og, eg, loss, one, two, three, q, k, v, cq, mk, mv, sc, cc, ps, pc, ga, up, sel, wa, wgu, wd, gain, tab, land_t,
    part_out, part_in, grad, dq, dk, dv, dmk, dmv, dctx, gate_grad, up_grad, ff_hidden,
    g8, ggu, gd, lc8, lcg, lcd, lf8, lfg, lfd, ln8, lng, lnd, ly8, lyg, lyd, mo8, mog, mod,
    back_slots, land_slots, got_slots, small, small_wide, small_land,
    send_sems, recv_sems, copy_sems,
):
    here = position(count)
    links, copies = Links(send_sems, recv_sems), Copies(copy_sems)
    w, t, c = here.w, here.t, here.c
    to_left, to_right, to_far, to_tp = (here.to_left, here.to_right, here.to_far, here.to_tp)
    loads = {}
    for src, dst in (
        (gain_h, gain), (three_h, three), (eg_h, eg), (og_h, og), (ga_h, ga), (up_h, up), (wd_h, wd), (half_h, tab), (wgu_h, wgu),
        (two_h, two), (wa_h, wa), (cc_h, cc), (pc_h, pc), (cq_h, cq), (mk_h, mk), (mv_h, mv), (sel_h, sel), (one_h, one),
        (sc_h, sc), (ps_h, ps), (q_h, q), (k_h, k), (v_h, v), (x_h, x), (loss_h, loss),
    ):
        loads[id(dst)] = copies.start(src, dst)

    def need(*refs):
        for ref in refs:
            loads.pop(id(ref)).wait()

    greet([to_left, to_right, to_far, here.to_core, here.to_y, to_tp])

    pieces = tab.shape[0] // CHUNK
    need(tab)
    crossing = [
        links.move(tab.at[pl.ds(i * CHUNK, CHUNK)], land_t.at[pl.ds(i * CHUNK, CHUNK)], here.to_y, land_t.at[pl.ds(i * CHUNK, CHUNK)]).start()
        for i in range(CROSSED, pieces)
    ]
    shares = []

    def settle_table(i):
        piece = pl.ds(i * CHUNK, CHUNK)
        if i >= CROSSED:
            crossing[i - CROSSED].landed()
            crossing[i - CROSSED].sent()
            tab[piece, :] = (tab[piece, :].astype(F32) + land_t[piece, :].astype(F32)).astype(BF)

        def rows(owner):
            return pl.ds(pl.multiple_of((owner * pieces + i) * CHUNK, CHUNK), CHUNK)

        copies.save(tab.at[piece], table_o.at[rows(c)])
        shares.append(
            links.move(tab.at[piece], table_o.at[rows(c)], here.to_core, table_o.at[rows(1 - c)]).start()
        )

    depth = g8.shape[1] // count

    def weight_pair(i):
        if i < 4:
            return WeightGrad(here, links, copies, g8, 2 * i, depth, lc8.at[i], lf8.at[i], ln8.at[i], ly8.at[i], mo8.at[i], ga8_o)
        if i == 4:
            return WeightGrad(here, links, copies, ggu, 0, depth, lcg, lfg, lng, lyg, mog, ggu_o)
        return WeightGrad(here, links, copies, gd, 0, depth, lcd, lfd, lnd, lyd, mod, gd_o)

    pair = [weight_pair(i) for i in range(6)]

    def exchange_start(n):
        return links.move(part_out.at[n], part_in.at[n], to_tp, part_in.at[n]).start()

    def exchanged(n, made):
        made.landed()
        return part_out[n].astype(F32) + part_in[n].astype(F32)

    small[...] = jnp.zeros_like(small)
    need(gain, three, eg, og)
    gain_row, back = norm_back(three[...], gain[3:4, :], eg[...])
    small[3:4, :] = gain_row
    grad[...] = og[...].astype(F32) + back
    branch = grad[...].astype(BF)
    need(ga, up, wd)
    units = wd.shape[2]
    for e in range(2):
        cols = slice(e * units, (e + 1) * units)
        act = ga[:, cols].astype(F32)
        up_act = up[:, cols].astype(F32)
        square = act * act
        bend = jnp.tanh(GELU_SCALE * (act + GELU_CUBE * act * square))
        gate = 0.5 * act * (1.0 + bend)
        slope = 0.5 * (1.0 + bend) + 0.5 * act * (1.0 - bend * bend) * (GELU_SCALE * (1.0 + 3.0 * GELU_CUBE * square))
        hidden_grad = dot_nn(branch, wd[e])
        gate_grad[:, cols] = (hidden_grad * up_act * slope).astype(BF)
        up_grad[:, cols] = (hidden_grad * gate).astype(BF)
        ff_hidden[:, cols] = (gate * up_act).astype(BF)
    need(wgu)
    part_out[0] = (dot_nt(gate_grad[...], wgu[0]) + dot_nt(up_grad[...], wgu[1])).astype(BF)
    swap = exchange_start(0)
    need(two)
    norm_t = rms_rows(two[...], gain[2:3, :]).T
    ggu[0] = dot_nn(norm_t, gate_grad[...]).astype(BF)
    ggu[1] = dot_nn(norm_t, up_grad[...]).astype(BF)
    pair[4].pair()
    branch_rows = branch.T
    for e in range(2):
        gd[e] = dot_nn(branch_rows, ff_hidden[:, e * units : (e + 1) * units]).astype(BF)
    pair[5].pair()
    pair[4].ring()
    gain_row, back = norm_back(two[...], gain[2:3, :], exchanged(0, swap))
    small[2:3, :] = gain_row
    grad[...] += back

    branch = grad[...].astype(BF)
    need(wa, cc, pc, cq, mk, mv, sel)
    dctx[...] = dot_nn(branch, wa[7]).astype(BF)
    pairs = dctx.shape[1] // (2 * HEAD_DIM)
    attention_backward(pairs, cq, mk, mv, pc, dctx, dq, dmk, dmv)
    part_out[1] = dot_nt(dq[...], wa[6]).astype(BF)
    swap = exchange_start(1)
    pair[5].ring()
    pair[4].pass_on()
    need(one)
    slots_grad = (dot_nt(dmk[...], wa[4]) + dot_nt(dmv[...], wa[5])).astype(BF)
    capacity = slots_grad.shape[0] // count
    half_slots = capacity // 2
    for b in range(count):
        for e in range(2):
            start = b * capacity + e * half_slots
            back_slots[e, b * half_slots : (b + 1) * half_slots] = slots_grad[start : start + half_slots]
    mem_swap = links.move(back_slots.at[1 - t], land_slots, to_tp, land_slots).start()

    def slot_rows(at):
        return pl.ds(pl.multiple_of(at * half_slots, 16), half_slots)

    g8[7] = dot_nn(branch.T, cc[...]).astype(BF)
    norm_t = rms_rows(one[...], gain[1:2, :]).T
    g8[6] = dot_nn(norm_t, dq[...]).astype(BF)
    pair[3].pair()
    slots_t = sel[...].T
    g8[4] = dot_nn(slots_t, dmk[...]).astype(BF)
    g8[5] = dot_nn(slots_t, dmv[...]).astype(BF)
    pair[2].pair()
    pair[5].pass_on()
    pair[3].ring()
    pair[2].ring()
    mem_swap.landed()
    back_slots[t] = (back_slots[t].astype(F32) + land_slots[...].astype(F32)).astype(BF)
    returns = [
        links.move(back_slots.at[t, slot_rows(to)], got_slots.at[slot_rows(w)], device, got_slots.at[slot_rows(at)]).start()
        for device, to, at in ((to_left, here.left, here.right), (to_right, here.right, here.left), (to_far, here.far, here.far))
    ]
    got_slots[slot_rows(w), :] = back_slots[t, slot_rows(w), :]
    gain_row, back = norm_back(one[...], gain[1:2, :], exchanged(1, swap))
    small[1:2, :] = gain_row
    grad[...] += back

    branch = grad[...].astype(BF)
    need(sc, ps, q, k, v, x)
    dctx[...] = dot_nn(branch, wa[3]).astype(BF)
    attention_backward(pairs, q, k, v, ps, dctx, dq, dk, dv)
    part_out[2] = (dot_nt(dq[...], wa[0]) + dot_nt(dk[...], wa[1]) + dot_nt(dv[...], wa[2])).astype(BF)
    swap = exchange_start(2)
    hidden = x[...].astype(F32)
    norm_t = rms_rows(hidden, gain[0:1, :]).T
    g8[0] = dot_nn(norm_t, dq[...]).astype(BF)
    g8[1] = dot_nn(norm_t, dk[...]).astype(BF)
    pair[0].pair()
    g8[2] = dot_nn(norm_t, dv[...]).astype(BF)
    g8[3] = dot_nn(branch.T, sc[...]).astype(BF)
    pair[1].pair()
    pair[3].pass_on()
    pair[2].pass_on()
    pair[0].ring()
    pair[1].ring()
    pair[4].across()
    pair[5].across()
    for made in returns:
        made.landed()
    rows = x.shape[0]
    choose = slot_choice(map_ref[:, pl.ds(pl.multiple_of(w * rows, rows), rows)], slots_grad.shape[0], count, t)
    part_out[3] = dot_tn(choose, got_slots[...]).astype(BF)
    memory_swap = exchange_start(3)
    gain_row, back = norm_back(hidden, gain[0:1, :], exchanged(2, swap))
    small[0:1, :] = gain_row
    grad[...] += back
    copies.save(grad, in_o)
    need(loss)
    small[4:5, 0:128] = loss[0:1, :]

    small_wide[w] = small[...]
    sums = [
        links.move(small, small_wide.at[w], device, small_wide.at[at]).start()
        for device, at in ((to_left, here.right), (to_right, here.left), (to_far, here.far))
    ]
    pair[0].pass_on()
    pair[1].pass_on()
    pair[3].across()
    pair[2].across()
    for made in sums:
        made.landed()
    total = small_wide[0]
    for b in range(1, count):
        total = total + small_wide[b]
    for n, way in enumerate((here.to_core, here.to_y)):
        small_land[2 * n] = total
        made = links.move(small_land.at[2 * n], small_land.at[2 * n + 1], way, small_land.at[2 * n + 1]).start()
        if n == 0:
            pair[0].across()
            pair[1].across()
        made.landed()
        total = total + small_land[2 * n + 1]
    small_o[...] = total
    mem_o[...] = exchanged(3, memory_swap)
    for i in range(pieces):
        settle_table(i)
    for i in (4, 5, 3, 2, 0, 1):
        pair[i].settle()
    for i in (4, 5, 3, 2, 0, 1):
        pair[i].done()
    for made in shares:
        made.landed()
    links.finish_rest(crossing)
    copies.finish()


def backward_layer(count, lengths, group_map, kept, table_half):
    (layer_input, out_grad, exit_rows_grad, loss_part, one, two, three, q, k, v, cq, mk, mv, sc, cc, ps, pc, ga, up, sel,
     wa, wgu, wd, gains) = kept
    rows, width = layer_input.shape
    heads, units = wa.shape[2], ga.shape[1]
    slots, depth = sel.shape[0], width // count
    half, narrow = depth // 2, units // 2
    piece_rows = table_half.shape[0]
    high = 2 * piece_rows
    vmem, hbm = pl.BlockSpec(memory_space=pltpu.VMEM), pl.BlockSpec(memory_space=pl.ANY)

    def three_kinds(rows_of, lead=()):
        return [
            pltpu.VMEM((4,) + lead + (rows_of, heads), BF), pltpu.VMEM(lead + (rows_of, units), BF),
            pltpu.VMEM(lead + (rows_of, narrow), BF),
        ]

    scratch = [pltpu.VMEM(value.shape, value.dtype) for value in kept]
    scratch += [pltpu.VMEM((piece_rows, width), BF), pltpu.VMEM((piece_rows, width), BF)]
    scratch += [
        pltpu.VMEM((4, rows, width), BF), pltpu.VMEM((4, rows, width), BF), pltpu.VMEM((rows, width), F32),
        pltpu.VMEM((rows, heads), BF), pltpu.VMEM((rows, heads), BF), pltpu.VMEM((rows, heads), BF),
        pltpu.VMEM((slots, heads), BF), pltpu.VMEM((slots, heads), BF), pltpu.VMEM((rows, heads), BF),
        pltpu.VMEM((rows, units), BF), pltpu.VMEM((rows, units), BF), pltpu.VMEM((rows, units), BF),
        pltpu.VMEM((8, width, heads), BF), pltpu.VMEM((2, width, units), BF), pltpu.VMEM((2, width, narrow), BF),
    ]
    scratch += three_kinds(width)
    scratch += three_kinds(half, (2,))
    scratch += three_kinds(depth, (2,))
    scratch += three_kinds(depth)
    scratch += three_kinds(depth, (2,))
    scratch += [
        pltpu.VMEM((2, slots // 2, width), BF), pltpu.VMEM((slots // 2, width), BF), pltpu.VMEM((slots // 2, width), BF), pltpu.VMEM((8, width), F32),
        pltpu.VMEM((count, 8, width), F32), pltpu.VMEM((4, 8, width), F32),
        pltpu.SemaphoreType.DMA((80,)), pltpu.SemaphoreType.DMA((80,)), pltpu.SemaphoreType.DMA((48,)),
    ]
    return pl.pallas_call(
        functools.partial(backward_kernel, count),
        out_shape=[
            jax.ShapeDtypeStruct((rows, width), F32), jax.ShapeDtypeStruct((rows, width), F32),
            jax.ShapeDtypeStruct((8, width), F32), jax.ShapeDtypeStruct((8, depth, heads), BF),
            jax.ShapeDtypeStruct((2, depth, units), BF), jax.ShapeDtypeStruct((2, depth, narrow), BF),
            jax.ShapeDtypeStruct((high, width), BF),
        ],
        in_specs=[pl.BlockSpec(memory_space=pltpu.SMEM), vmem] + [hbm] * (len(kept) + 1),
        out_specs=[hbm, vmem, vmem, hbm, hbm, hbm, hbm],
        scratch_shapes=scratch,
        compiler_params=pltpu.CompilerParams(
            collective_id=2, has_side_effects=True, vmem_limit_bytes=VMEM_BYTES
        ),
        name="backward_layer",
    )(lengths, group_map, *kept, table_half)


def finish_kernel(
    vocab, attn_ref, gate_ref, down_ref, small_ref, small_scalar, table_h, in_h, mem_h, block_h, *refs
):
    attn_o, gate_o, down_o = refs[:8], refs[8:10], refs[10]
    gains_o, loss_o, in_o, mem_o, block_o, table_o = refs[11:15], refs[15], refs[16], refs[17], refs[18], refs[19]
    rounded, wide, in_v, mem_v, block_v, sems = refs[20:]
    copies = Copies(sems)
    rows = [pl.ds(i * CHUNK, min(CHUNK, vocab - i * CHUNK)) for i in range(rounded.shape[0] // CHUNK)]
    loads = [copies.start(table_h.at[where], rounded.at[where]) for where in rows]
    moved = [
        (copies.start(src, through), through, dst)
        for src, through, dst in ((in_h, in_v, in_o), (mem_h, mem_v, mem_o), (block_h, block_v, block_o))
    ]
    for where, load in zip(rows, loads):
        load.wait()
        wide[where, :] = rounded[where, :].astype(F32)
        copies.save(wide.at[where], table_o.at[where])
    for load, through, dst in moved:
        load.wait()
        copies.save(through, dst)
    for n, out in enumerate(attn_o):
        out[...] = attn_ref[n].astype(F32)
    for n, out in enumerate(gate_o):
        out[...] = gate_ref[n].astype(F32)
    narrow = down_ref.shape[2]
    for e in range(2):
        down_o[:, e * narrow : (e + 1) * narrow] = down_ref[e].astype(F32)
    depth = attn_ref.shape[1]
    width = small_ref.shape[1]
    turned = pltpu.roll(small_ref[...], width - lax.axis_index("wide") * depth, 1)
    for n, out in enumerate(gains_o):
        out[...] = turned[n : n + 1, 0:depth]
    loss_o[0, 0] = small_scalar[4, 0]
    copies.finish()


def finish(vocab, attn, gate, down, small, table, input_grad, memory_grad, block):
    depth, heads, units = attn.shape[1], attn.shape[2], gate.shape[2]
    vmem, hbm, smem = (pl.BlockSpec(memory_space=space) for space in (pltpu.VMEM, pl.ANY, pltpu.SMEM))
    high, width = table.shape

    def result(*shape):
        return jax.ShapeDtypeStruct(shape, F32)

    return pl.pallas_call(
        functools.partial(finish_kernel, vocab),
        out_shape=[result(depth, heads)] * 8 + [result(depth, units)] * 3 + [result(1, depth)] * 4 + [
            result(1, 1), result(*input_grad.shape), result(*memory_grad.shape),
            jax.ShapeDtypeStruct(block.shape, BF), result(vocab, width),
        ],
        in_specs=[vmem, vmem, vmem, vmem, smem] + [hbm] * 4,
        out_specs=[vmem] * 15 + [smem] + [hbm] * 4,
        scratch_shapes=[
            pltpu.VMEM((high, width), BF), pltpu.VMEM((high, width), F32), pltpu.VMEM(input_grad.shape, F32),
            pltpu.VMEM(memory_grad.shape, F32), pltpu.VMEM(block.shape, BF), pltpu.SemaphoreType.DMA((24,)),
        ],
        compiler_params=pltpu.CompilerParams(vmem_limit_bytes=VMEM_BYTES),
        name="finish",
    )(attn, gate, down, small, small, table, input_grad, memory_grad, block)


def fused_body(
    layer_input,
    memory,
    reader_map,
    target_ids,
    target_lengths,
    out_grad,
    self_q,
    self_k,
    self_v,
    self_o,
    cross_q,
    cross_k,
    cross_v,
    cross_o,
    ff_gate,
    ff_up,
    ff_out,
    gain_self,
    gain_cross,
    gain_ff,
    gain_exit,
    exit_table,
):
    count = lax.axis_size("wide")
    wide_index = lax.axis_index("wide")
    depth = gain_self.shape[0]
    group_map = reader_map[None, :]
    (
        block_output, resid_one, resid_two, resid_three, norm_exit, queries, keys, values, cross_queries,
        keys_read, values_read, context_self, context_cross, probs_self, probs_cross, gate_act, up_act, slots,
        attn_weights, gate_weights, down_weights, gains,
    ) = forward_layer(
        count, layer_input, memory, group_map, target_lengths,
        (gain_self, gain_cross, gain_ff, gain_exit),
        (self_q, self_k, self_v, self_o, cross_q, cross_k, cross_v, cross_o, ff_gate, ff_up, ff_out),
    )
    exit_rows_grad, loss_part, table_half = exit_head(
        count, norm_exit, target_ids[None, :], target_lengths, exit_table
    )
    input_grad, memory_grad, small, attn_grads, gate_grads, down_grads, table_grad = backward_layer(
        count, target_lengths, group_map,
        (
            layer_input, out_grad, exit_rows_grad, loss_part, resid_one, resid_two, resid_three, queries, keys, values,
            cross_queries, keys_read, values_read, context_self, context_cross, probs_self, probs_cross, gate_act, up_act,
            slots, attn_weights, gate_weights, down_weights, gains,
        ),
        table_half,
    )
    done = finish(
        exit_table.shape[0], attn_grads, gate_grads, down_grads, small, table_grad, input_grad, memory_grad, block_output
    )
    attn, gate, down, gains, loss = done[:8], done[8:10], done[10], done[11:15], done[15]
    input_grad, memory_grad, block_output, table_grad = done[16:]
    return (
        block_output, loss[0, 0], input_grad, memory_grad, attn[0], attn[1], attn[2], attn[3], attn[6], attn[4], attn[5],
        attn[7], gate[0], gate[1], down, gains[0][0], gains[1][0], gains[2][0], gains[3][0], table_grad,
    )


def fits(mesh):
    return mesh.shape["wide"] == 4 and mesh.shape["tp"] == 2 and mesh.shape["grp"] == 4


def solution(mesh):
    placed = (
        P(("grp", "wide"), None),
        P(("grp", "wide"), None),
        P("grp"),
        P("grp"),
        P(),
        P(("grp", "wide"), None),
        P("wide", "tp"),
        P("wide", "tp"),
        P("wide", "tp"),
        P("wide", "tp"),
        P("wide", "tp"),
        P("wide", "tp"),
        P("wide", "tp"),
        P("wide", "tp"),
        P("wide", "tp"),
        P("wide", "tp"),
        P("wide", "tp"),
        P("wide"),
        P("wide"),
        P("wide"),
        P("wide"),
        P(("wide", "tp"), None),
    )
    return jax.shard_map(
        fused_body if fits(mesh) else plain_body,
        mesh=mesh,
        in_specs=placed,
        out_specs=(
            P(("grp", "wide"), None),
            P(),
            P(("grp", "wide"), None),
            P(("grp", "wide"), None),
            P("wide", "tp"),
            P("wide", "tp"),
            P("wide", "tp"),
            P("wide", "tp"),
            P("wide", "tp"),
            P("wide", "tp"),
            P("wide", "tp"),
            P("wide", "tp"),
            P("wide", "tp"),
            P("wide", "tp"),
            P("wide", "tp"),
            P("wide"),
            P("wide"),
            P("wide"),
            P("wide"),
            P(("wide", "tp"), None),
        ),
        check_vma=False,
    )
```

```python
import functools
import types

import jax
import jax.numpy as jnp
from jax import lax
from jax.experimental import pallas as pl
from jax.experimental.pallas import tpu as pltpu
from jax.sharding import PartitionSpec as P

HEAD_DIM = 64


EPSILON = 1e-06
MASKED = -1e30


def merged(shard, axis, combine):
    everything = jax.tree.map(
        lambda part, kind: lax.all_gather(part.astype(kind), axis),
        shard,
        (jnp.bfloat16, jnp.bfloat16, jnp.bfloat16),
    )

    def take(k):
        return jax.tree.map(lambda part, own: part[k].astype(own.dtype), everything, shard)

    return lax.fori_loop(
        1, lax.axis_size(axis), lambda k, so_far: combine(so_far, take(k)), take(0)
    )


def project(left, right):
    return jnp.dot(left, right, preferred_element_type=jnp.float32)


def project_back(left, right):
    return lax.dot_general(
        left, right, (((1,), (1,)), ((), ())), preferred_element_type=jnp.float32
    )


def outer_rows(left, right):
    return lax.dot_general(
        left, right, (((0,), (0,)), ((), ())), preferred_element_type=jnp.float32
    )


def smooth_gate(values):
    return jax.nn.gelu(values, approximate=True)


def normalize(values, gain):
    factor = lax.rsqrt(jnp.mean(values * values, axis=1, keepdims=True) + EPSILON)
    unit_rows = values * factor
    return ((unit_rows * gain).astype(jnp.bfloat16), unit_rows, factor)


def normalize_back(values, unit_rows, factor, gain, grad_rows):
    gain_grad = jnp.sum(grad_rows * unit_rows, axis=0)
    scaled = grad_rows * gain
    inner = jnp.mean(scaled * values, axis=1, keepdims=True)
    return (gain_grad, factor * scaled - unit_rows * factor * factor * inner)


def split_heads(values):
    return values.reshape(values.shape[0], -1, HEAD_DIM).transpose(1, 0, 2)


def join_heads(values):
    return values.transpose(1, 0, 2).reshape(values.shape[1], -1)


def read_slots(group_map, reader, holders, rows_each, capacity):
    matched = (group_map.reshape(holders, rows_each) == reader).astype(jnp.int32)
    ranks = jnp.cumsum(matched, axis=1) - 1
    counts = jnp.sum(matched, axis=1)
    place = lax.iota(jnp.int32, holders * capacity)
    valid = place % capacity < jnp.repeat(counts, capacity, total_repeat_length=holders * capacity)
    anchor = lax.iota(jnp.int32, holders)[:, None] * capacity + ranks
    target = jnp.where(matched > 0, anchor, holders * capacity)
    return (valid, target.reshape(-1))


def attend_forward(queries, keys, values, allowed):
    factor = HEAD_DIM ** (-0.5)

    def one_head(parts):
        query, key_rows, value_rows = parts
        scores = jnp.where(allowed, project_back(query, key_rows) * factor, MASKED)
        highest = jnp.max(scores, axis=1, keepdims=True)
        exponent = jnp.exp(scores - highest)
        total = jnp.sum(exponent, axis=1, keepdims=True)
        soft_weights = (exponent / total).astype(jnp.bfloat16)
        return (project(soft_weights, value_rows), (highest + jnp.log(total))[:, 0])

    context, log_total = lax.map(
        one_head, (split_heads(queries), split_heads(keys), split_heads(values))
    )
    return (join_heads(context).astype(jnp.bfloat16), log_total)


def attend_backward(queries, keys, values, context_grad, log_total, allowed):
    factor = HEAD_DIM ** (-0.5)

    def one_head(parts):
        query, key_rows, value_rows, grad_rows, log_row = parts
        scores = jnp.where(allowed, project_back(query, key_rows) * factor, MASKED)
        soft = jnp.exp(scores - log_row[:, None])
        soft_grad = project_back(grad_rows, value_rows)
        score_grad = (soft * (soft_grad - jnp.sum(soft * soft_grad, axis=1, keepdims=True))).astype(
            jnp.bfloat16
        )
        query_grad = project(score_grad, key_rows) * factor
        key_grad = outer_rows(score_grad, query) * factor
        value_grad = outer_rows(soft.astype(jnp.bfloat16), grad_rows)
        return (query_grad, key_grad, value_grad)

    grads = lax.map(
        one_head,
        (
            split_heads(queries),
            split_heads(keys),
            split_heads(values),
            split_heads(context_grad),
            log_total,
        ),
    )
    return (join_heads(grads[0]), join_heads(grads[1]), join_heads(grads[2]))


def heads_total(partial_rows):
    return lax.psum(partial_rows, "tp")


def input_total(partial_rows):
    return lax.psum(partial_rows.astype(jnp.bfloat16), "tp").astype(jnp.float32)


def merge_softmax(first, second):
    highest = jnp.maximum(first[0], second[0])
    total = first[1] * jnp.exp(first[0] - highest) + second[1] * jnp.exp(second[0] - highest)
    return (highest, total, first[2] + second[2])


def plain_body(
    layer_input,
    memory,
    reader_map,
    target_ids,
    target_lengths,
    out_grad,
    self_q,
    self_k,
    self_v,
    self_o,
    cross_q,
    cross_k,
    cross_v,
    cross_o,
    ff_gate,
    ff_up,
    ff_out,
    gain_self,
    gain_cross,
    gain_ff,
    gain_exit,
    exit_table,
):
    (
        w_query,
        w_key,
        w_value,
        w_output,
        c_query,
        c_key,
        c_value,
        c_output,
        w_gate,
        w_up,
        w_down,
        full_gain_self,
        full_gain_cross,
        full_gain_ff,
        full_gain_exit,
    ) = (
        lax.all_gather(self_q, "wide", axis=0, tiled=True),
        lax.all_gather(self_k, "wide", axis=0, tiled=True),
        lax.all_gather(self_v, "wide", axis=0, tiled=True),
        lax.all_gather(self_o, "wide", axis=0, tiled=True),
        lax.all_gather(cross_q, "wide", axis=0, tiled=True),
        lax.all_gather(cross_k, "wide", axis=0, tiled=True),
        lax.all_gather(cross_v, "wide", axis=0, tiled=True),
        lax.all_gather(cross_o, "wide", axis=0, tiled=True),
        lax.all_gather(ff_gate, "wide", axis=0, tiled=True),
        lax.all_gather(ff_up, "wide", axis=0, tiled=True),
        lax.all_gather(ff_out, "wide", axis=0, tiled=True),
        lax.all_gather(gain_self, "wide", axis=0, tiled=True),
        lax.all_gather(gain_cross, "wide", axis=0, tiled=True),
        lax.all_gather(gain_ff, "wide", axis=0, tiled=True),
        lax.all_gather(gain_exit, "wide", axis=0, tiled=True),
    )
    gain_one = full_gain_self.astype(jnp.float32)
    gain_two = full_gain_cross.astype(jnp.float32)
    gain_three = full_gain_ff.astype(jnp.float32)
    gain_last = full_gain_exit.astype(jnp.float32)
    seq_rows = layer_input.shape[0]
    wide_count = lax.axis_size("wide")
    wide_index = lax.axis_index("wide")
    group_index = lax.axis_index("grp")
    group_lengths = lax.dynamic_slice_in_dim(target_lengths, group_index * wide_count, wide_count)
    own_length = lax.dynamic_index_in_dim(group_lengths, wide_index, keepdims=False)
    hidden = layer_input.astype(jnp.float32)
    norm_self, unit_self, factor_self = normalize(hidden, gain_one)
    queries = project(norm_self, w_query).astype(jnp.bfloat16)
    keys = project(norm_self, w_key).astype(jnp.bfloat16)
    values = project(norm_self, w_value).astype(jnp.bfloat16)
    position = lax.iota(jnp.int32, seq_rows)
    allowed_self = (position[None, :] <= position[:, None]) & (position[None, :] < own_length)
    context_self, log_self = attend_forward(queries, keys, values, allowed_self)
    resid_one = hidden + heads_total(project_back(context_self, w_output))
    norm_cross, unit_cross, factor_cross = normalize(resid_one, gain_two)
    cross_queries = project(norm_cross, c_query).astype(jnp.bfloat16)
    memory_keys = project(memory, c_key).astype(jnp.bfloat16)
    memory_values = project(memory, c_value).astype(jnp.bfloat16)
    rows_each = memory.shape[0]
    capacity = max(2, 2 * rows_each // wide_count)
    slot_count = wide_count * capacity
    slot_valid, slot_target = read_slots(reader_map, wide_index, wide_count, rows_each, capacity)
    keys_all, values_all = (
        lax.all_gather(memory_keys, "wide", axis=0, tiled=True),
        lax.all_gather(memory_values, "wide", axis=0, tiled=True),
    )
    read_table = (
        jnp.zeros((slot_count,), jnp.int32)
        .at[slot_target]
        .set(lax.iota(jnp.int32, wide_count * rows_each), mode="drop")
    )
    keys_read = jnp.take(keys_all, read_table, axis=0)
    values_read = jnp.take(values_all, read_table, axis=0)
    allowed_cross = slot_valid[None, :]
    context_cross, log_cross = attend_forward(cross_queries, keys_read, values_read, allowed_cross)
    resid_two = resid_one + heads_total(project_back(context_cross, c_output))
    norm_ff, unit_ff, factor_ff = normalize(resid_two, gain_three)
    gate_float = project(norm_ff, w_gate).astype(jnp.bfloat16).astype(jnp.float32)
    up_float = project(norm_ff, w_up).astype(jnp.bfloat16).astype(jnp.float32)
    gelu_value, gelu_pull = jax.vjp(smooth_gate, gate_float)
    ff_hidden = (gelu_value * up_float).astype(jnp.bfloat16)
    resid_three = resid_two + heads_total(project_back(ff_hidden, w_down))
    block_output = resid_three.astype(jnp.bfloat16)
    norm_exit, unit_exit, factor_exit = normalize(resid_three, gain_last)
    rows_all = lax.all_gather(norm_exit, "wide", axis=0, tiled=True)
    group_tokens = rows_all.shape[0]
    vocab_rows = exit_table.shape[0]
    scale_exit = float(rows_all.shape[1]) ** (-0.5)
    logits = project_back(rows_all, exit_table) * scale_exit
    vocab_ids = lax.axis_index(("wide", "tp")) * vocab_rows + lax.iota(jnp.int32, vocab_rows)
    is_target = target_ids[:, None] == vocab_ids[None, :]
    local_high = jnp.max(logits, axis=1)
    local_total = jnp.sum(jnp.exp(logits - local_high[:, None]), axis=1)
    local_pick = jnp.sum(jnp.where(is_target, logits, 0.0), axis=1)
    highest, total_exp, target_logit = merged(
        (local_high, local_total, local_pick), ("wide", "tp"), merge_softmax
    )
    log_total = highest + jnp.log(total_exp)
    token_place = lax.iota(jnp.int32, group_tokens)
    valid = token_place % seq_rows < jnp.repeat(
        group_lengths, seq_rows, total_repeat_length=group_tokens
    )
    token_count = jnp.sum(target_lengths).astype(jnp.float32)
    token_weight = jnp.where(valid, 1.0, 0.0).astype(jnp.float32) / token_count
    group_loss = jnp.sum(token_weight * (log_total - target_logit))
    logit_grad = (
        (jnp.exp(logits - log_total[:, None]) - jnp.where(is_target, 1.0, 0.0))
        * token_weight[:, None]
    ).astype(jnp.bfloat16)
    rows_grad_all = project(logit_grad, exit_table) * scale_exit
    exit_grad = outer_rows(logit_grad, rows_all) * scale_exit
    rows_part = lax.psum_scatter(
        rows_grad_all.astype(jnp.bfloat16), "wide", scatter_dimension=0, tiled=True
    )
    norm_exit_grad = lax.psum(rows_part, "tp").astype(jnp.float32)
    gain_exit_grad, back_exit = normalize_back(
        resid_three, unit_exit, factor_exit, gain_last, norm_exit_grad
    )
    resid_three_grad = out_grad.astype(jnp.float32) + back_exit
    ff_branch = resid_three_grad.astype(jnp.bfloat16)
    w_down_grad = outer_rows(ff_branch, ff_hidden)
    hidden_grad = project(ff_branch, w_down)
    gate_grad = gelu_pull(hidden_grad * up_float)[0].astype(jnp.bfloat16)
    up_grad = (hidden_grad * gelu_value).astype(jnp.bfloat16)
    w_gate_grad = outer_rows(norm_ff, gate_grad)
    w_up_grad = outer_rows(norm_ff, up_grad)
    norm_ff_grad = input_total(project_back(gate_grad, w_gate) + project_back(up_grad, w_up))
    gain_ff_grad, back_ff = normalize_back(resid_two, unit_ff, factor_ff, gain_three, norm_ff_grad)
    resid_two_grad = resid_three_grad + back_ff
    cross_branch = resid_two_grad.astype(jnp.bfloat16)
    c_output_grad = outer_rows(cross_branch, context_cross)
    cross_context_grad = project(cross_branch, c_output).astype(jnp.bfloat16)
    cross_query_grad, keys_grad_read, values_grad_read = attend_backward(
        cross_queries, keys_read, values_read, cross_context_grad, log_cross, allowed_cross
    )
    empty_grads = jnp.zeros((wide_count * rows_each, keys_grad_read.shape[1]), jnp.float32)
    keys_grad_all = empty_grads.at[read_table].add(keys_grad_read)
    values_grad_all = empty_grads.at[read_table].add(values_grad_read)
    keys_grad, values_grad = (
        lax.psum_scatter(
            keys_grad_all.astype(jnp.bfloat16), "wide", scatter_dimension=0, tiled=True
        ).astype(jnp.float32),
        lax.psum_scatter(
            values_grad_all.astype(jnp.bfloat16), "wide", scatter_dimension=0, tiled=True
        ).astype(jnp.float32),
    )
    keys_grad = keys_grad.astype(jnp.bfloat16)
    values_grad = values_grad.astype(jnp.bfloat16)
    cross_query_grad = cross_query_grad.astype(jnp.bfloat16)
    c_query_grad = outer_rows(norm_cross, cross_query_grad)
    c_key_grad = outer_rows(memory, keys_grad)
    c_value_grad = outer_rows(memory, values_grad)
    norm_cross_grad, memory_grad = (
        lax.psum(project_back(cross_query_grad, c_query).astype(jnp.bfloat16), "tp").astype(
            jnp.float32
        ),
        lax.psum(
            (project_back(keys_grad, c_key) + project_back(values_grad, c_value)).astype(
                jnp.bfloat16
            ),
            "tp",
        ).astype(jnp.float32),
    )
    gain_cross_grad, back_cross = normalize_back(
        resid_one, unit_cross, factor_cross, gain_two, norm_cross_grad
    )
    resid_one_grad = resid_two_grad + back_cross
    self_branch = resid_one_grad.astype(jnp.bfloat16)
    w_output_grad = outer_rows(self_branch, context_self)
    self_context_grad = project(self_branch, w_output).astype(jnp.bfloat16)
    query_grad, key_grad, value_grad = attend_backward(
        queries, keys, values, self_context_grad, log_self, allowed_self
    )
    query_grad = query_grad.astype(jnp.bfloat16)
    key_grad = key_grad.astype(jnp.bfloat16)
    value_grad = value_grad.astype(jnp.bfloat16)
    w_query_grad = outer_rows(norm_self, query_grad)
    w_key_grad = outer_rows(norm_self, key_grad)
    w_value_grad = outer_rows(norm_self, value_grad)
    norm_self_grad = input_total(
        project_back(query_grad, w_query)
        + project_back(key_grad, w_key)
        + project_back(value_grad, w_value)
    )
    gain_self_grad, back_self = normalize_back(
        hidden, unit_self, factor_self, gain_one, norm_self_grad
    )
    input_grad = resid_one_grad + back_self
    shards = (
        lax.psum_scatter(
            w_query_grad.astype(jnp.bfloat16), "wide", scatter_dimension=0, tiled=True
        ).astype(jnp.float32),
        lax.psum_scatter(
            w_key_grad.astype(jnp.bfloat16), "wide", scatter_dimension=0, tiled=True
        ).astype(jnp.float32),
        lax.psum_scatter(
            w_value_grad.astype(jnp.bfloat16), "wide", scatter_dimension=0, tiled=True
        ).astype(jnp.float32),
        lax.psum_scatter(
            w_output_grad.astype(jnp.bfloat16), "wide", scatter_dimension=0, tiled=True
        ).astype(jnp.float32),
        lax.psum_scatter(
            c_query_grad.astype(jnp.bfloat16), "wide", scatter_dimension=0, tiled=True
        ).astype(jnp.float32),
        lax.psum_scatter(
            c_key_grad.astype(jnp.bfloat16), "wide", scatter_dimension=0, tiled=True
        ).astype(jnp.float32),
        lax.psum_scatter(
            c_value_grad.astype(jnp.bfloat16), "wide", scatter_dimension=0, tiled=True
        ).astype(jnp.float32),
        lax.psum_scatter(
            c_output_grad.astype(jnp.bfloat16), "wide", scatter_dimension=0, tiled=True
        ).astype(jnp.float32),
        lax.psum_scatter(
            w_gate_grad.astype(jnp.bfloat16), "wide", scatter_dimension=0, tiled=True
        ).astype(jnp.float32),
        lax.psum_scatter(
            w_up_grad.astype(jnp.bfloat16), "wide", scatter_dimension=0, tiled=True
        ).astype(jnp.float32),
        lax.psum_scatter(
            w_down_grad.astype(jnp.bfloat16), "wide", scatter_dimension=0, tiled=True
        ).astype(jnp.float32),
        lax.psum_scatter(
            gain_self_grad.astype(jnp.bfloat16), "wide", scatter_dimension=0, tiled=True
        ).astype(jnp.float32),
        lax.psum_scatter(
            gain_cross_grad.astype(jnp.bfloat16), "wide", scatter_dimension=0, tiled=True
        ).astype(jnp.float32),
        lax.psum_scatter(
            gain_ff_grad.astype(jnp.bfloat16), "wide", scatter_dimension=0, tiled=True
        ).astype(jnp.float32),
        lax.psum_scatter(
            gain_exit_grad.astype(jnp.bfloat16), "wide", scatter_dimension=0, tiled=True
        ).astype(jnp.float32),
    )
    totals = (
        lax.psum(shards[0].astype(jnp.bfloat16), "grp").astype(jnp.float32),
        lax.psum(shards[1].astype(jnp.bfloat16), "grp").astype(jnp.float32),
        lax.psum(shards[2].astype(jnp.bfloat16), "grp").astype(jnp.float32),
        lax.psum(shards[3].astype(jnp.bfloat16), "grp").astype(jnp.float32),
        lax.psum(shards[4].astype(jnp.bfloat16), "grp").astype(jnp.float32),
        lax.psum(shards[5].astype(jnp.bfloat16), "grp").astype(jnp.float32),
        lax.psum(shards[6].astype(jnp.bfloat16), "grp").astype(jnp.float32),
        lax.psum(shards[7].astype(jnp.bfloat16), "grp").astype(jnp.float32),
        lax.psum(shards[8].astype(jnp.bfloat16), "grp").astype(jnp.float32),
        lax.psum(shards[9].astype(jnp.bfloat16), "grp").astype(jnp.float32),
        lax.psum(shards[10].astype(jnp.bfloat16), "grp").astype(jnp.float32),
        lax.psum(shards[11].astype(jnp.bfloat16), "grp").astype(jnp.float32),
        lax.psum(shards[12].astype(jnp.bfloat16), "grp").astype(jnp.float32),
        lax.psum(shards[13].astype(jnp.bfloat16), "grp").astype(jnp.float32),
        lax.psum(shards[14].astype(jnp.bfloat16), "grp").astype(jnp.float32),
        lax.psum(exit_grad.astype(jnp.bfloat16), "grp").astype(jnp.float32),
        lax.psum(group_loss.astype(jnp.bfloat16), "grp").astype(jnp.float32),
    )
    return (
        block_output,
        totals[16],
        input_grad,
        memory_grad,
        totals[0],
        totals[1],
        totals[2],
        totals[3],
        totals[4],
        totals[5],
        totals[6],
        totals[7],
        totals[8],
        totals[9],
        totals[10],
        totals[11],
        totals[12],
        totals[13],
        totals[14],
        totals[15],
    )


MESH = pl.DeviceIdType.MESH
BF = jnp.bfloat16
F32 = jnp.float32
VMEM_BYTES = 63 << 20


def dot_nn(left, right):
    return lax.dot_general(left, right, (((1,), (0,)), ((), ())), preferred_element_type=F32)


def dot_nt(left, right):
    return lax.dot_general(left, right, (((1,), (1,)), ((), ())), preferred_element_type=F32)


def dot_tn(left, right):
    return lax.dot_general(left, right, (((0,), (0,)), ((), ())), preferred_element_type=F32)


class Move:
    def __init__(self, out, arrival):
        self.out, self.arrival = out, arrival

    def start(self):
        self.out.start()
        return self

    def sent(self):
        self.out.wait_send()

    def landed(self):
        self.arrival.wait_recv()


class Links:
    def __init__(self, send_sems, recv_sems):
        self.send_sems, self.recv_sems = send_sems, recv_sems
        self.used = 0
        self.moves = []

    def move(self, src, dst, device, lands):
        k = self.used
        self.used += 1
        out = pltpu.make_async_remote_copy(
            src_ref=src, dst_ref=dst, send_sem=self.send_sems.at[k], recv_sem=self.recv_sems.at[k],
            device_id=device, device_id_type=MESH,
        )
        arrival = pltpu.make_async_remote_copy(
            src_ref=lands, dst_ref=lands, send_sem=self.send_sems.at[k], recv_sem=self.recv_sems.at[k],
            device_id=device, device_id_type=MESH,
        )
        made = Move(out, arrival)
        self.moves.append(made)
        return made

    def finish(self):
        for made in self.moves:
            made.sent()

    def finish_rest(self, done):
        for made in self.moves:
            if made not in done:
                made.sent()


class Copies:
    def __init__(self, sems):
        self.sems, self.used, self.pending = sems, 0, []

    def start(self, src, dst):
        made = pltpu.make_async_copy(src, dst, self.sems.at[self.used])
        self.used += 1
        made.start()
        return made

    def save(self, src, dst):
        self.pending.append(self.start(src, dst))

    def finish(self):
        for made in self.pending:
            made.wait()


def greet(devices):
    barrier = pltpu.get_barrier_semaphore()
    for device in devices:
        pl.semaphore_signal(barrier, inc=1, device_id=device, device_id_type=MESH)
    pl.semaphore_wait(barrier, len(devices))


def position(count):
    g, w, t = lax.axis_index("grp"), lax.axis_index("wide"), lax.axis_index("tp")
    c = lax.rem(g, 2)
    left, right, far = (lax.rem(w + d, count) for d in (count - 1, 1, 2))
    return types.SimpleNamespace(
        count=count, g=g, w=w, t=t, c=c, yy=lax.div(g, 2), left=left, right=right, far=far,
        to_left={"wide": left}, to_right={"wide": right}, to_far={"wide": far},
        to_core={"grp": g + 1 - 2 * c}, to_y={"grp": lax.rem(g + 2, 4)}, to_tp={"tp": 1 - t},
    )


def rms_rows(values, gain):
    factor = lax.rsqrt(jnp.mean(values * values, axis=1, keepdims=True) + EPSILON)
    return (values * factor * gain).astype(BF)


def lane_masks():
    lane = lax.broadcasted_iota(jnp.int32, (1, 2 * HEAD_DIM), 1)
    low = jnp.where(lane < HEAD_DIM, 1.0, 0.0).astype(F32)
    return low.astype(BF), (1.0 - low).astype(BF)


def both_heads(pair):
    low, high = lane_masks()
    return jnp.concatenate([pair * low, pair * high], axis=0)


def pick_heads(stacked):
    rows = stacked.shape[0] // 2
    lane = lax.broadcasted_iota(jnp.int32, (rows, 2 * HEAD_DIM), 1)
    return jnp.where(lane < HEAD_DIM, stacked[:rows], stacked[rows:])


def pair_columns(p):
    return pl.ds(pl.multiple_of(p * 2 * HEAD_DIM, 2 * HEAD_DIM), 2 * HEAD_DIM)


def attention_forward(pairs, queries, keys, values, probs, context, allowed):
    factor = HEAD_DIM ** (-0.5)

    def step(p, carry):
        cols = pair_columns(p)
        scores = dot_nt(both_heads(queries[:, cols]), keys[:, cols]) * factor
        scores = jnp.where(allowed, scores, MASKED)
        exponent = jnp.exp(scores - jnp.max(scores, axis=1, keepdims=True))
        soft = (exponent / jnp.sum(exponent, axis=1, keepdims=True)).astype(BF)
        probs[p] = soft
        context[:, cols] = pick_heads(dot_nn(soft, values[:, cols])).astype(BF)
        return carry

    lax.fori_loop(0, pairs, step, 0)


def slot_choice(own_map, slots, count, part=None):
    rows = own_map.shape[1]
    capacity = slots // count
    reader_iota = lax.broadcasted_iota(jnp.int32, (max(8, count), rows), 0)
    matched = jnp.where(reader_iota == own_map, 1.0, 0.0).astype(F32)
    before = lax.broadcasted_iota(jnp.int32, (rows, rows), 0) < lax.broadcasted_iota(jnp.int32, (rows, rows), 1)
    ranks = dot_nn(matched.astype(BF), jnp.where(before, 1.0, 0.0).astype(BF))
    rank = jnp.sum(matched * ranks, axis=0, keepdims=True).astype(jnp.int32)
    if part is None:
        slot_of = own_map * capacity + rank
    else:
        slots, capacity = slots // 2, capacity // 2
        rank = rank - part * capacity
        slot_of = jnp.where((rank >= 0) & (rank < capacity), own_map * capacity + rank, -1)
    slot_iota = lax.broadcasted_iota(jnp.int32, (slots, rows), 0)
    return jnp.where(slot_iota == slot_of, 1.0, 0.0).astype(BF)


class Gather:
    def __init__(self, here, links, buf, first, depth, placed):
        self.here, self.links, self.buf, self.placed = here, links, buf, placed
        self.mine, self.other = first + here.c, first + 1 - here.c
        self.depth = depth

    def rows(self, at, start, parts):
        size = self.depth // parts
        return pl.ds(pl.multiple_of(at * self.depth + start * size, 16), size)

    def y_half(self, at):
        return self.rows(at, self.here.yy, 2)

    def quarter(self, at, which):
        return self.rows(at, 2 * self.here.yy + which, 4)

    def send(self, where, device, lands, index=None):
        src = self.buf.at[self.mine, where]
        land = self.buf.at[self.mine if index is None else index, lands]
        return self.links.move(src, src, device, land).start()

    def issue(self):
        here = self.here
        for made in self.placed:
            made.wait()
        own = self.y_half(here.w)
        self.from_left = self.send(own, here.to_right, self.y_half(here.left))
        self.from_right = self.send(own, here.to_left, self.y_half(here.right))

    def to_y(self, at):
        return self.send(self.y_half(at), self.here.to_y, self.rows(at, 1 - self.here.yy, 2))

    def forward(self):
        here = self.here
        self.from_left.landed()
        self.far_top = self.send(self.quarter(here.left, 0), here.to_right, self.quarter(here.far, 0))
        self.over_y = [self.to_y(here.left)]
        self.from_right.landed()
        self.far_low = self.send(self.quarter(here.right, 1), here.to_left, self.quarter(here.far, 1))
        self.over_y.append(self.to_y(here.right))

    def complete(self):
        self.far_top.landed()
        self.far_low.landed()
        self.over_y.append(self.to_y(self.here.far))

    def share(self):
        here = self.here
        self.cores = []
        for made, at in zip(self.over_y, (here.left, here.right, here.far)):
            made.landed()
            whole = self.rows(at, 0, 1)
            self.cores.append(self.send(whole, here.to_core, whole, self.other))

    def ready(self):
        for made in self.cores:
            made.landed()


CHUNK = 512


def tall(rows):
    return -(-rows // (2 * CHUNK)) * 2 * CHUNK


def span(at, size):
    return pl.ds(pl.multiple_of(at * size, size), size)


def flip_table(tab, tabt):
    def step(j, carry):
        tabt[:, span(j, CHUNK)] = tab[span(j, CHUNK), :].T
        return carry

    lax.fori_loop(0, tab.shape[0] // CHUNK, step, 0)


def exit_phase(here, links, rows_own, tab, tabt, gt, rb, ids, lens, high, total, stats, stats_tp, stats_wide, coef, weight, acc,
               dx, joint, land_tp, land_far, land_near, swap_out, swap_in, grad_out, vocab, fillers):
    count, g, w, t = here.count, here.g, here.w, here.t
    left, right, far = here.left, here.right, here.far
    to_left, to_right, to_far, to_tp = here.to_left, here.to_right, here.to_far, here.to_tp
    rows, width = rows_own.shape
    half, quarter = rows // 2, rows // 4
    chunks = tab.shape[0] // CHUNK
    scale = float(width) ** (-0.5)
    base = (w * 2 + t) * vocab
    tokens = count * rows

    def block(b):
        return span(b, rows)

    def halved(b, which):
        return pl.ds(pl.multiple_of(b * rows + which * half, half), half)

    def quartered(b, which):
        return pl.ds(pl.multiple_of(b * rows + t * half + which * quarter, quarter), quarter)

    rb[block(w), :] = rows_own[...]
    src = rb.at[halved(w, t)]
    from_left = links.move(src, src, to_right, rb.at[halved(left, t)]).start()
    from_right = links.move(src, src, to_left, rb.at[halved(right, t)]).start()

    def to_other_half(b):
        src = rb.at[halved(b, t)]
        return links.move(src, src, to_tp, rb.at[halved(b, 1 - t)]).start()

    def target_row(cols):
        row = ids[:, cols] - base
        return jnp.where(row < vocab, row, -1)

    def score(b):
        cols = block(b)
        wanted = target_row(cols)
        block_rows = rb[cols, :]

        def step(j, pick):
            at = lax.broadcasted_iota(jnp.int32, (CHUNK, rows), 0) + j * CHUNK
            logits = dot_nt(tab[span(j, CHUNK), :], block_rows) * scale
            logits = jnp.where(at < vocab, logits, MASKED)
            top = jnp.max(logits, axis=0, keepdims=True)
            exponent = jnp.exp(logits - top)
            high[pl.ds(j, 1), cols] = top
            total[pl.ds(j, 1), cols] = jnp.sum(exponent, axis=0, keepdims=True)
            gt[span(j, CHUNK), cols] = exponent.astype(BF)
            return pick + jnp.sum(jnp.where(at == wanted, logits, 0.0), axis=0, keepdims=True)

        pick = lax.fori_loop(0, chunks, step, jnp.zeros((1, rows), F32), unroll=True)
        tops = high[:, cols]
        top = jnp.max(tops, axis=0, keepdims=True)
        stats[0:1, cols] = top
        stats[1:2, cols] = jnp.sum(total[:, cols] * jnp.exp(tops - top), axis=0, keepdims=True)
        stats[2:3, cols] = pick

    score(w)
    from_left.landed()
    src = rb.at[quartered(left, 0)]
    far_top = links.move(src, src, to_right, rb.at[quartered(far, 0)]).start()
    left_rest = to_other_half(left)
    from_right.landed()
    src = rb.at[quartered(right, 1)]
    far_low = links.move(src, src, to_left, rb.at[quartered(far, 1)]).start()
    right_rest = to_other_half(right)
    left_rest.landed()
    score(left)
    far_top.landed()
    far_low.landed()
    far_rest = to_other_half(far)
    right_rest.landed()
    score(right)
    far_rest.landed()
    score(far)

    def merged_stats(parts):
        top = parts[0][0:1]
        for part in parts[1:]:
            top = jnp.maximum(top, part[0:1])
        mass = sum(part[1:2] * jnp.exp(part[0:1] - top) for part in parts)
        pick = sum(part[2:3] for part in parts)
        return top, mass, pick

    swap = links.move(stats, stats_tp, to_tp, stats_tp).start()
    lengths = [lens[k] for k in range(lens.shape[0])]
    tokens_all = lengths[0]
    for length in lengths[1:]:
        tokens_all = tokens_all + length
    place = lax.broadcasted_iota(jnp.int32, (1, rows), 1)
    for b in range(count):
        inside = jnp.where(place < lens[g * count + b], 1.0, 0.0).astype(F32)
        weight[0:1, b * rows : (b + 1) * rows] = inside / tokens_all.astype(F32)
    swap.landed()
    mine, other = stats[...], stats_tp[...]
    top, mass, pick = merged_stats([mine, other])
    mine_wide = stats_wide.at[w]
    mine_wide[0:1, :] = top
    mine_wide[1:2, :] = mass
    mine_wide[2:3, :] = pick
    spreads = [
        links.move(mine_wide, mine_wide, device, stats_wide.at[at]).start()
        for device, at in ((to_left, right), (to_right, left), (to_far, far))
    ]
    for made in spreads:
        made.landed()
    top, mass, pick = merged_stats([stats_wide[b] for b in range(count)])
    log_total = top + jnp.log(mass)
    all_weight = weight[0:1, :]
    coef[...] = jnp.exp(high[...] - log_total) * all_weight
    stats_tp[3:4, :] = (log_total - pick) * all_weight
    loss = jnp.sum(stats_tp[3:4, block(w)], axis=1, keepdims=True)

    def row_grads(b):
        cols = block(b)
        wanted = target_row(cols)
        own_weight = weight[0:1, cols]
        acc[...] = jnp.zeros_like(acc)

        def step(j, carry):
            at = lax.broadcasted_iota(jnp.int32, (CHUNK, rows), 0) + j * CHUNK
            grad = gt[span(j, CHUNK), cols].astype(F32) * coef[pl.ds(j, 1), cols]
            grad = (grad - jnp.where(at == wanted, own_weight, 0.0)).astype(BF)
            gt[span(j, CHUNK), cols] = grad
            acc[...] += dot_nn(tabt[:, span(j, CHUNK)], grad)
            return carry

        lax.fori_loop(0, chunks, step, 0, unroll=True)
        return (acc[...] * scale).astype(BF).T

    own_half, other_half = (span(which, half) for which in (t, 1 - t))

    def start_block(slot, b):
        dx[slot] = row_grads(b)
        return links.move(dx.at[slot, other_half], land_tp.at[slot], to_tp, land_tp.at[slot]).start()

    def join_block(slot, made):
        made.landed()
        joint[slot] = (dx[slot, own_half].astype(F32) + land_tp[slot].astype(F32)).astype(BF)

    parts = [pl.ds(which * quarter, quarter) for which in range(2)]

    def near(slot, which, side, device):
        where = parts[which]
        return links.move(joint.at[slot, where], land_near.at[side, where], device, land_near.at[side, where]).start()

    made_far = start_block(0, far)
    made_right = start_block(1, right)
    join_block(0, made_far)
    far_moves = [
        links.move(joint.at[0, parts[which]], land_far.at[which], device, land_far.at[which]).start()
        for which, device in enumerate((to_right, to_left))
    ]
    made_left = start_block(2, left)
    join_block(1, made_right)
    right_low = near(1, 1, 0, to_right)
    made_own = start_block(3, w)
    fillers[0]()
    join_block(2, made_left)
    left_top = near(2, 0, 1, to_left)
    near_late = []
    for which, slot, device in ((0, 1, to_right), (1, 2, to_left)):
        far_moves[which].landed()
        where = parts[which]
        joint[slot, where] = (joint[slot, where].astype(F32) + land_far[which].astype(F32)).astype(BF)
        near_late.append(near(slot, which, which, device))
    fillers[1]()
    join_block(3, made_own)
    for made in [right_low, left_top] + near_late:
        made.landed()
    swap_out[...] = (joint[3].astype(F32) + land_near[0].astype(F32) + land_near[1].astype(F32)).astype(BF)
    swap = links.move(swap_out, swap_in, to_tp, swap_in).start()
    grad_out[own_half, :] = swap_out[...].astype(F32)
    swap.landed()
    grad_out[other_half, :] = swap_in[...].astype(F32)
    return loss


class TableGrad:
    def __init__(self, here, links, copies, tab, gt, rb, land_core, out):
        self.here, self.links, self.copies = here, links, copies
        self.tab, self.gt, self.rb, self.land_core, self.out = tab, gt, rb, land_core, out
        self.pieces = tab.shape[0] // (2 * CHUNK)
        self.scale = float(tab.shape[1]) ** (-0.5)
        self.cores = []

    def rows(self, owner, i):
        return pl.ds(pl.multiple_of((owner * self.pieces + i) * CHUNK, CHUNK), CHUNK)

    def product(self, where):
        return dot_nn(self.gt[where, :], self.rb[...]) * self.scale

    def first_half(self):
        c = self.here.c
        for i in range(self.pieces):
            where = self.rows(1 - c, i)
            self.tab[where, :] = self.product(where).astype(BF)
            land = self.land_core.at[pl.ds(i * CHUNK, CHUNK)]
            self.cores.append(self.links.move(self.tab.at[where], land, self.here.to_core, land).start())

    def second_half(self):
        c = self.here.c
        for i in range(self.pieces):
            where = self.rows(c, i)
            mine = self.product(where)
            self.cores[i].landed()
            self.tab[where, :] = (mine + self.land_core[i * CHUNK : (i + 1) * CHUNK, :].astype(F32)).astype(BF)
            self.copies.save(self.tab.at[where], self.out.at[pl.ds(i * CHUNK, CHUNK)])


def front_kernel(
    count, vocab, x_ref, mem_ref, map_ref, len_ref, gs_ref, gc_ref, gf_ref, ge_ref, ids,
    q_in, k_in, v_in, so_in, cq_in, ck_in, cv_in, co_in, ga_in, up_in, dn_in, table,
    block_o, one_o, two_o, three_o, q_o, k_o, v_o, cq_o, mk_o, mv_o, sc_o, cc_o, ps_o, pc_o,
    ga_o, up_o, sel_o, wa_o, wgu_o, wd_o, gain_o, grad_o, loss_o, half_o,
    wa, wgu, wd, gains, slots, packed, part_out, part_in, valid_slot,
    block, one, two, three, q, k, v, cq, mk, mv, sc, cc, ps, pc, ga, up, gain_sum, exit_rows,
    tab, tabt, gt, rb, high_v, total, stats, stats_tp, stats_wide, coef, weight, acc, dx, joint, land_tp, land_far, land_near,
    swap_out, swap_in, land_core,
    send_sems, recv_sems, copy_sems,
):
    here = position(count)
    g, w, t = here.g, here.w, here.t
    left, right, far = here.left, here.right, here.far
    to_left, to_right, to_far, to_tp = here.to_left, here.to_right, here.to_far, here.to_tp
    rows = x_ref.shape[0]
    links, copies = Links(send_sems, recv_sems), Copies(copy_sems)
    depth = q_in.shape[0]
    wide_cols = dn_in.shape[1] // 2

    own = pl.ds(pl.multiple_of(w * depth, 16), depth)
    order = (q_in, k_in, v_in, so_in, ck_in, cv_in, cq_in, co_in)
    weights = []
    for j in range(4):
        placed = [copies.start(order[2 * j + e], wa.at[2 * j + e, own]) for e in range(2)]
        weights.append(Gather(here, links, wa, 2 * j, depth, placed))
    for f in range(2):
        cols = pl.ds(f * wide_cols, wide_cols)
        placed = [copies.start(ref.at[:, cols], wgu.at[2 * f + e, own]) for e, ref in enumerate((ga_in, up_in))]
        weights.append(Gather(here, links, wgu, 2 * f, depth, placed))
    placed = [copies.start(dn_in.at[:, pl.ds(e * wide_cols, wide_cols)], wd.at[e, own]) for e in range(2)]
    weights.append(Gather(here, links, wd, 0, depth, placed))

    gain_sum[...] = jnp.zeros_like(gain_sum)
    for n, ref in enumerate((gs_ref, gc_ref, gf_ref, ge_ref)):
        gain_sum[n : n + 1, 0:depth] = ref[...].astype(F32).reshape(1, depth)
    gains[w] = pltpu.roll(gain_sum[...], w * depth, 1)
    table_load = copies.start(table, tab.at[pl.ds(0, vocab)])
    tab[vocab:, :] = jnp.zeros((tab.shape[0] - vocab, tab.shape[1]), BF)
    greet([to_left, to_right, to_far, here.to_core, here.to_y, to_tp])
    gain_moves = [
        links.move(gains.at[w], gains.at[w], device, gains.at[at]).start()
        for device, at in ((to_left, right), (to_right, left), (to_far, far))
    ]
    for first in weights[:3]:
        first.issue()

    capacity = slots.shape[0] // count
    choose = slot_choice(map_ref[:, pl.ds(pl.multiple_of(w * rows, rows), rows)], slots.shape[0], count)
    packed[...] = dot_nn(choose, mem_ref[...]).astype(BF)

    def slot_rows(at, which):
        return pl.ds(pl.multiple_of(at * capacity + which * (capacity // 2), 16), capacity // 2)

    own_slots = pl.ds(pl.multiple_of(w * capacity, 16), capacity)
    slots[own_slots, :] = packed[own_slots, :]
    weights[0].forward()
    weights[3].issue()
    for made in gain_moves:
        made.landed()
    total_gain = gains[0]
    for at in range(1, count):
        total_gain = total_gain + gains[at]
    gain_sum[...] = total_gain
    hidden = x_ref[...].astype(F32)
    norm_self = rms_rows(hidden, gain_sum[0:1, :])
    weights[1].forward()
    weights[0].complete()
    slot_moves = [
        links.move(packed.at[slot_rows(to, t)], slots.at[slot_rows(w, t)], device, slots.at[slot_rows(at, t)]).start()
        for device, to, at in ((to_left, left, right), (to_right, right, left), (to_far, far, far))
    ]
    weights[2].forward()
    weights[0].share()
    weights[1].complete()
    weights[1].share()
    weights[4].issue()
    weights[0].ready()
    q[...] = dot_nn(norm_self, wa[0]).astype(BF)
    k[...] = dot_nn(norm_self, wa[1]).astype(BF)
    weights[2].complete()
    weights[1].ready()
    v[...] = dot_nn(norm_self, wa[2]).astype(BF)
    weights[3].forward()
    weights[2].share()
    weights[5].issue()
    weights[3].complete()
    slot_fills = []
    for made, at in zip(slot_moves, (right, left, far)):
        made.landed()
        src = slots.at[slot_rows(at, t)]
        slot_fills.append(links.move(src, src, to_tp, slots.at[slot_rows(at, 1 - t)]).start())
    length = len_ref[g * count + w]
    query_at = lax.broadcasted_iota(jnp.int32, (2 * rows, rows), 0)
    query_at = jnp.where(query_at >= rows, query_at - rows, query_at)
    key_at = lax.broadcasted_iota(jnp.int32, (2 * rows, rows), 1)
    allowed_self = (key_at <= query_at) & (key_at < length)
    pairs = q.shape[1] // (2 * HEAD_DIM)
    attention_forward(pairs, q, k, v, ps, sc, allowed_self)

    def exchange_start(n):
        return links.move(part_out.at[n], part_in.at[n], to_tp, part_in.at[n]).start()

    def exchanged(n, made):
        made.landed()
        return part_out[n].astype(F32) + part_in[n].astype(F32)

    part_out[0] = dot_nt(sc[...], wa[3]).astype(BF)
    swap = exchange_start(0)
    weights[3].share()
    weights[4].forward()
    weights[6].issue()
    for made in slot_fills:
        made.landed()
    place = lax.broadcasted_iota(jnp.int32, (1, capacity), 1).astype(F32)
    for b in range(count):
        reads = jnp.sum(jnp.where(map_ref[:, b * rows : (b + 1) * rows] == w, 1.0, 0.0), axis=1, keepdims=True)
        valid_slot[0:1, b * capacity : (b + 1) * capacity] = jnp.where(place < reads, 1.0, 0.0)
    weights[2].ready()
    mk[...] = dot_nn(slots[...], wa[4]).astype(BF)
    mv[...] = dot_nn(slots[...], wa[5]).astype(BF)
    weights[4].complete()
    weights[5].forward()
    allowed_cross = jnp.broadcast_to(valid_slot[0:1, :], (2 * rows, slots.shape[0])) > 0.5
    one[...] = hidden + exchanged(0, swap)
    norm_cross = rms_rows(one[...], gain_sum[1:2, :])
    weights[3].ready()
    cq[...] = dot_nn(norm_cross, wa[6]).astype(BF)
    weights[4].share()
    weights[5].complete()
    weights[6].forward()
    attention_forward(pairs, cq, mk, mv, pc, cc, allowed_cross)
    part_out[1] = dot_nt(cc[...], wa[7]).astype(BF)
    swap = exchange_start(1)
    weights[5].share()
    weights[6].complete()
    weights[6].share()
    table_load.wait()
    flip_table(tab, tabt)
    copies.save(wa, wa_o)
    for src, dst in (
        (q, q_o), (k, k_o), (v, v_o), (sc, sc_o), (ps, ps_o), (mk, mk_o), (mv, mv_o), (cq, cq_o), (cc, cc_o), (pc, pc_o),
        (slots, sel_o), (one, one_o), (gain_sum, gain_o),
    ):
        copies.save(src, dst)
    two[...] = one[...] + exchanged(1, swap)
    copies.save(two, two_o)
    norm_ff = rms_rows(two[...], gain_sum[2:3, :])
    low, high = pl.ds(0, wide_cols), pl.ds(wide_cols, wide_cols)
    for f, cols in ((0, low), (1, high)):
        weights[4 + f].ready()
        ga[:, cols] = dot_nn(norm_ff, wgu[2 * f]).astype(BF)
        up[:, cols] = dot_nn(norm_ff, wgu[2 * f + 1]).astype(BF)
    copies.save(wgu, wgu_o)
    copies.save(ga, ga_o)
    copies.save(up, up_o)
    ff_hidden = (smooth_gate(ga[...].astype(F32)) * up[...].astype(F32)).astype(BF)
    weights[6].ready()
    copies.save(wd, wd_o)
    part_out[2] = (
        dot_nt(ff_hidden[:, :wide_cols], wd[0]) + dot_nt(ff_hidden[:, wide_cols:], wd[1])
    ).astype(BF)
    swap = exchange_start(2)
    three[...] = two[...] + exchanged(2, swap)
    block[...] = three[...].astype(BF)
    exit_rows[...] = rms_rows(three[...], gain_sum[3:4, :])
    copies.save(three, three_o)
    copies.save(block, block_o)
    grads = TableGrad(here, links, copies, tab, gt, rb, land_core, half_o)
    loss = exit_phase(
        here, links, exit_rows, tab, tabt, gt, rb, ids, len_ref, high_v, total, stats, stats_tp, stats_wide, coef, weight, acc,
        dx, joint, land_tp, land_far, land_near, swap_out, swap_in, grad_o, vocab, (grads.first_half, grads.second_half),
    )
    loss_o[...] = jnp.broadcast_to(loss, loss_o.shape)
    links.finish()
    copies.finish()


def front(count, layer_input, memory, group_map, lengths, gain_parts, ids, weights, table):
    rows, width = layer_input.shape
    vocab = table.shape[0]
    heads, units = weights[0].shape[1], weights[8].shape[1]
    slots = count * max(2, 2 * rows // count)
    pairs = heads // (2 * HEAD_DIM)
    kept = [
        ((rows, width), BF), ((rows, width), F32), ((rows, width), F32), ((rows, width), F32),
        ((rows, heads), BF), ((rows, heads), BF), ((rows, heads), BF), ((rows, heads), BF),
        ((slots, heads), BF), ((slots, heads), BF), ((rows, heads), BF), ((rows, heads), BF),
        ((pairs, 2 * rows, rows), BF), ((pairs, 2 * rows, slots), BF),
        ((rows, units), BF), ((rows, units), BF), ((slots, width), BF),
        ((8, width, heads), BF), ((4, width, units // 2), BF), ((2, width, units // 2), BF), ((8, width), F32),
    ]
    high = tall(vocab)
    chunks, tokens = high // CHUNK, rows * count
    vmem, hbm, smem = (pl.BlockSpec(memory_space=space) for space in (pltpu.VMEM, pl.ANY, pltpu.SMEM))
    scratch = [
        ((8, width, heads), BF), ((4, width, units // 2), BF), ((2, width, units // 2), BF), ((count, 8, width), F32),
        ((slots, width), BF), ((slots, width), BF), ((3, rows, width), BF), ((3, rows, width), BF), ((8, slots), F32),
    ]
    scratch += kept[:16]
    scratch += [
        ((8, width), F32), ((rows, width), BF),
        ((high, width), BF), ((width, high), BF), ((high, tokens), BF), ((tokens, width), BF), ((chunks, tokens), F32),
        ((chunks, tokens), F32), ((8, tokens), F32), ((8, tokens), F32), ((count, 8, tokens), F32), ((chunks, tokens), F32),
        ((8, tokens), F32), ((width, rows), F32), ((4, rows, width), BF), ((4, rows // 2, width), BF), ((4, rows // 2, width), BF),
        ((2, rows // 4, width), BF), ((2, rows // 2, width), BF), ((rows // 2, width), BF), ((rows // 2, width), BF),
        ((high // 2, width), BF),
    ]
    results = kept + [((rows, width), F32), ((8, 128), F32), ((high // 2, width), BF)]
    return pl.pallas_call(
        functools.partial(front_kernel, count, vocab),
        out_shape=[jax.ShapeDtypeStruct(shape, kind) for shape, kind in results],
        in_specs=[vmem, vmem, vmem, smem] + [vmem] * 5 + [hbm] * 12,
        out_specs=[hbm] * len(kept) + [vmem, vmem, hbm],
        scratch_shapes=[pltpu.VMEM(shape, kind) for shape, kind in scratch]
        + [pltpu.SemaphoreType.DMA((128,)), pltpu.SemaphoreType.DMA((128,)), pltpu.SemaphoreType.DMA((48,))],
        compiler_params=pltpu.CompilerParams(collective_id=0, has_side_effects=True, vmem_limit_bytes=VMEM_BYTES),
        name="forward_and_exit",
    )(layer_input, memory, group_map, lengths, *gain_parts, ids, *weights, table)


GELU_SCALE = 0.7978845608028654
GELU_CUBE = 0.044715


def norm_back(values, gain, grad):
    factor = lax.rsqrt(jnp.mean(values * values, axis=1, keepdims=True) + EPSILON)
    unit = values * factor
    scaled = grad * gain
    inner = jnp.mean(scaled * values, axis=1, keepdims=True)
    return jnp.sum(grad * unit, axis=0, keepdims=True), factor * scaled - unit * (factor * factor * inner)


def attention_backward(pairs, queries, keys, values, probs, context_grad, query_grad, key_grad, value_grad):
    factor = HEAD_DIM ** (-0.5)

    def step(p, carry):
        cols = pair_columns(p)
        grad = both_heads(context_grad[:, cols])
        soft = probs[p]
        soft_float = soft.astype(F32)
        soft_grad = dot_nt(grad, values[:, cols])
        inner = jnp.sum(soft_float * soft_grad, axis=1, keepdims=True)
        score_grad = (soft_float * (soft_grad - inner)).astype(BF)
        query_grad[:, cols] = (pick_heads(dot_nn(score_grad, keys[:, cols])) * factor).astype(BF)
        key_grad[:, cols] = (dot_tn(score_grad, both_heads(queries[:, cols])) * factor).astype(BF)
        value_grad[:, cols] = dot_tn(soft, grad).astype(BF)
        return carry

    lax.fori_loop(0, pairs, step, 0)


class WeightGrad:
    def __init__(self, here, links, copies, grads, first, depth, land_core, land_far, land_near, land_y, mine_out, out):
        self.here, self.links, self.copies = here, links, copies
        self.grads, self.mine, self.other = grads, first + here.c, first + 1 - here.c
        self.depth, self.half = depth, depth // 2
        self.land_core, self.land_far, self.land_near, self.land_y = land_core, land_far, land_near, land_y
        self.mine_out, self.out = mine_out, out

    def whole(self, at):
        return pl.ds(pl.multiple_of(at * self.depth, 16), self.depth)

    def part(self, at, which):
        return pl.ds(pl.multiple_of(at * self.depth + which * self.half, 16), self.half)

    def pair(self):
        self.core = self.links.move(
            self.grads.at[self.other], self.land_core, self.here.to_core, self.land_core
        ).start()

    def near(self, where, side, which, device):
        rows = pl.ds(which * self.half, self.half)
        return self.links.move(
            self.grads.at[self.mine, where], self.land_near.at[side, rows], device, self.land_near.at[side, rows]
        ).start()

    def add_core(self, where):
        self.grads[self.mine, where] = (
            self.grads[self.mine, where].astype(F32) + self.land_core[where].astype(F32)
        ).astype(BF)

    def ring(self):
        here = self.here
        self.core.landed()
        for at in (here.far, here.right, here.left):
            self.add_core(self.whole(at))
            if at is here.far:
                self.far = [
                    self.links.move(
                        self.grads.at[self.mine, self.part(at, e)], self.land_far.at[e], way, self.land_far.at[e]
                    ).start()
                    for e, way in enumerate((here.to_right, here.to_left))
                ]
        self.early = [
            self.near(self.part(here.right, 1), 0, 1, here.to_right),
            self.near(self.part(here.left, 0), 1, 0, here.to_left),
        ]
        self.add_core(self.whole(here.w))

    def pass_on(self):
        here = self.here
        self.late = []
        for e, side, way in ((0, here.right, here.to_right), (1, here.left, here.to_left)):
            self.far[e].landed()
            where = self.part(side, e)
            self.grads[self.mine, where] = (
                self.grads[self.mine, where].astype(F32) + self.land_far[e].astype(F32)
            ).astype(BF)
            self.late.append(self.near(where, e, e, way))

    def across(self):
        for made in self.early + self.late:
            made.landed()
        where = self.whole(self.here.w)
        self.mine_out[0] = (
            self.grads[self.mine, where].astype(F32) + self.land_near[0].astype(F32) + self.land_near[1].astype(F32)
        ).astype(BF)
        self.y = self.links.move(self.mine_out.at[0], self.land_y, self.here.to_y, self.land_y).start()

    def settle(self):
        self.y.landed()
        self.mine_out[1] = (self.mine_out[0].astype(F32) + self.land_y[...].astype(F32)).astype(BF)
        src = self.mine_out.at[1]
        self.copies.save(src, self.out.at[self.mine])
        self.share = self.links.move(
            src, self.out.at[self.mine], self.here.to_core, self.out.at[self.other]
        ).start()

    def done(self):
        self.share.landed()


def backward_kernel(
    count,
    lens, map_ref, x_h, og_h, eg_h, loss_h, one_h, two_h, three_h, q_h, k_h, v_h, cq_h, mk_h, mv_h, sc_h, cc_h, ps_h, pc_h,
    ga_h, up_h, sel_h, wa_h, wgu_h, wd_h, gain_h, half_h,
    in_o, mem_o, small_o, ga8_o, ggu_o, gd_o, table_o,
    x, og, eg, loss, one, two, three, q, k, v, cq, mk, mv, sc, cc, ps, pc, ga, up, sel, wa, wgu, wd, gain, tab, land_t,
    part_out, part_in, grad, dq, dk, dv, dmk, dmv, dctx, gate_grad, up_grad, ff_hidden,
    g8, ggu, gd, lc8, lcg, lcd, lf8, lfg, lfd, ln8, lng, lnd, ly8, lyg, lyd, mo8, mog, mod,
    back_slots, land_slots, got_slots, small, small_wide, small_land,
    send_sems, recv_sems, copy_sems,
):
    here = position(count)
    links, copies = Links(send_sems, recv_sems), Copies(copy_sems)
    w, t, c = here.w, here.t, here.c
    to_left, to_right, to_far, to_tp = (here.to_left, here.to_right, here.to_far, here.to_tp)
    loads = {}
    for src, dst in (
        (gain_h, gain), (three_h, three), (eg_h, eg), (og_h, og), (ga_h, ga), (up_h, up), (wd_h, wd), (half_h, tab), (wgu_h, wgu),
        (two_h, two), (wa_h, wa), (cc_h, cc), (pc_h, pc), (cq_h, cq), (mk_h, mk), (mv_h, mv), (sel_h, sel), (one_h, one),
        (sc_h, sc), (ps_h, ps), (q_h, q), (k_h, k), (v_h, v), (x_h, x), (loss_h, loss),
    ):
        loads[id(dst)] = copies.start(src, dst)

    def need(*refs):
        for ref in refs:
            loads.pop(id(ref)).wait()

    greet([to_left, to_right, to_far, here.to_core, here.to_y, to_tp])

    pieces = tab.shape[0] // CHUNK
    need(tab)
    crossing = [
        links.move(tab.at[pl.ds(i * CHUNK, CHUNK)], land_t.at[pl.ds(i * CHUNK, CHUNK)], here.to_y, land_t.at[pl.ds(i * CHUNK, CHUNK)]).start()
        for i in range(pieces)
    ]
    shares = []

    def settle_table(i):
        piece = pl.ds(i * CHUNK, CHUNK)
        crossing[i].landed()
        crossing[i].sent()
        tab[piece, :] = (tab[piece, :].astype(F32) + land_t[piece, :].astype(F32)).astype(BF)

        def rows(owner):
            return pl.ds(pl.multiple_of((owner * pieces + i) * CHUNK, CHUNK), CHUNK)

        copies.save(tab.at[piece], table_o.at[rows(c)])
        shares.append(
            links.move(tab.at[piece], table_o.at[rows(c)], here.to_core, table_o.at[rows(1 - c)]).start()
        )

    depth = g8.shape[1] // count

    def weight_pair(i):
        if i < 4:
            return WeightGrad(here, links, copies, g8, 2 * i, depth, lc8.at[i], lf8.at[i], ln8.at[i], ly8.at[i], mo8.at[i], ga8_o)
        if i == 4:
            return WeightGrad(here, links, copies, ggu, 0, depth, lcg, lfg, lng, lyg, mog, ggu_o)
        return WeightGrad(here, links, copies, gd, 0, depth, lcd, lfd, lnd, lyd, mod, gd_o)

    pair = [weight_pair(i) for i in range(6)]

    def exchange_start(n):
        return links.move(part_out.at[n], part_in.at[n], to_tp, part_in.at[n]).start()

    def exchanged(n, made):
        made.landed()
        return part_out[n].astype(F32) + part_in[n].astype(F32)

    small[...] = jnp.zeros_like(small)
    need(gain, three, eg, og)
    gain_row, back = norm_back(three[...], gain[3:4, :], eg[...])
    small[3:4, :] = gain_row
    grad[...] = og[...].astype(F32) + back
    branch = grad[...].astype(BF)
    need(ga, up, wd)
    units = wd.shape[2]
    for e in range(2):
        cols = slice(e * units, (e + 1) * units)
        act = ga[:, cols].astype(F32)
        up_act = up[:, cols].astype(F32)
        square = act * act
        bend = jnp.tanh(GELU_SCALE * (act + GELU_CUBE * act * square))
        gate = 0.5 * act * (1.0 + bend)
        slope = 0.5 * (1.0 + bend) + 0.5 * act * (1.0 - bend * bend) * (GELU_SCALE * (1.0 + 3.0 * GELU_CUBE * square))
        hidden_grad = dot_nn(branch, wd[e])
        gate_grad[:, cols] = (hidden_grad * up_act * slope).astype(BF)
        up_grad[:, cols] = (hidden_grad * gate).astype(BF)
        ff_hidden[:, cols] = (gate * up_act).astype(BF)
    need(wgu)
    total = dot_nt(gate_grad[:, :units], wgu[0]) + dot_nt(up_grad[:, :units], wgu[1])
    total += dot_nt(gate_grad[:, units:], wgu[2]) + dot_nt(up_grad[:, units:], wgu[3])
    part_out[0] = total.astype(BF)
    swap = exchange_start(0)
    need(two)
    norm_t = rms_rows(two[...], gain[2:3, :]).T
    ggu[0] = dot_nn(norm_t, gate_grad[...]).astype(BF)
    ggu[1] = dot_nn(norm_t, up_grad[...]).astype(BF)
    pair[4].pair()
    branch_rows = branch.T
    for e in range(2):
        gd[e] = dot_nn(branch_rows, ff_hidden[:, e * units : (e + 1) * units]).astype(BF)
    pair[5].pair()
    pair[4].ring()
    gain_row, back = norm_back(two[...], gain[2:3, :], exchanged(0, swap))
    small[2:3, :] = gain_row
    grad[...] += back

    branch = grad[...].astype(BF)
    need(wa, cc, pc, cq, mk, mv, sel)
    dctx[...] = dot_nn(branch, wa[7]).astype(BF)
    pairs = dctx.shape[1] // (2 * HEAD_DIM)
    attention_backward(pairs, cq, mk, mv, pc, dctx, dq, dmk, dmv)
    part_out[1] = dot_nt(dq[...], wa[6]).astype(BF)
    swap = exchange_start(1)
    pair[5].ring()
    pair[4].pass_on()
    need(one)
    slots_grad = (dot_nt(dmk[...], wa[4]) + dot_nt(dmv[...], wa[5])).astype(BF)
    capacity = slots_grad.shape[0] // count
    half_slots = capacity // 2
    for b in range(count):
        for e in range(2):
            start = b * capacity + e * half_slots
            back_slots[e, b * half_slots : (b + 1) * half_slots] = slots_grad[start : start + half_slots]
    mem_swap = links.move(back_slots.at[1 - t], land_slots, to_tp, land_slots).start()

    def slot_rows(at):
        return pl.ds(pl.multiple_of(at * half_slots, 16), half_slots)

    g8[7] = dot_nn(branch.T, cc[...]).astype(BF)
    norm_t = rms_rows(one[...], gain[1:2, :]).T
    g8[6] = dot_nn(norm_t, dq[...]).astype(BF)
    pair[3].pair()
    slots_t = sel[...].T
    g8[4] = dot_nn(slots_t, dmk[...]).astype(BF)
    g8[5] = dot_nn(slots_t, dmv[...]).astype(BF)
    pair[2].pair()
    pair[5].pass_on()
    pair[3].ring()
    pair[2].ring()
    mem_swap.landed()
    back_slots[t] = (back_slots[t].astype(F32) + land_slots[...].astype(F32)).astype(BF)
    returns = [
        links.move(back_slots.at[t, slot_rows(to)], got_slots.at[slot_rows(w)], device, got_slots.at[slot_rows(at)]).start()
        for device, to, at in ((to_left, here.left, here.right), (to_right, here.right, here.left), (to_far, here.far, here.far))
    ]
    got_slots[slot_rows(w), :] = back_slots[t, slot_rows(w), :]
    gain_row, back = norm_back(one[...], gain[1:2, :], exchanged(1, swap))
    small[1:2, :] = gain_row
    grad[...] += back

    branch = grad[...].astype(BF)
    need(sc, ps, q, k, v, x)
    dctx[...] = dot_nn(branch, wa[3]).astype(BF)
    attention_backward(pairs, q, k, v, ps, dctx, dq, dk, dv)
    part_out[2] = (dot_nt(dq[...], wa[0]) + dot_nt(dk[...], wa[1]) + dot_nt(dv[...], wa[2])).astype(BF)
    swap = exchange_start(2)
    hidden = x[...].astype(F32)
    norm_t = rms_rows(hidden, gain[0:1, :]).T
    g8[0] = dot_nn(norm_t, dq[...]).astype(BF)
    g8[1] = dot_nn(norm_t, dk[...]).astype(BF)
    pair[0].pair()
    g8[2] = dot_nn(norm_t, dv[...]).astype(BF)
    g8[3] = dot_nn(branch.T, sc[...]).astype(BF)
    pair[1].pair()
    pair[3].pass_on()
    pair[2].pass_on()
    pair[0].ring()
    pair[1].ring()
    pair[4].across()
    pair[5].across()
    for made in returns:
        made.landed()
    rows = x.shape[0]
    choose = slot_choice(map_ref[:, pl.ds(pl.multiple_of(w * rows, rows), rows)], slots_grad.shape[0], count, t)
    part_out[3] = dot_tn(choose, got_slots[...]).astype(BF)
    memory_swap = exchange_start(3)
    gain_row, back = norm_back(hidden, gain[0:1, :], exchanged(2, swap))
    small[0:1, :] = gain_row
    grad[...] += back
    copies.save(grad, in_o)
    need(loss)
    small[4:5, 0:128] = loss[0:1, :]

    small_wide[w] = small[...]
    sums = [
        links.move(small, small_wide.at[w], device, small_wide.at[at]).start()
        for device, at in ((to_left, here.right), (to_right, here.left), (to_far, here.far))
    ]
    pair[0].pass_on()
    pair[1].pass_on()
    pair[3].across()
    pair[2].across()
    for made in sums:
        made.landed()
    total = small_wide[0]
    for b in range(1, count):
        total = total + small_wide[b]
    for n, way in enumerate((here.to_core, here.to_y)):
        small_land[2 * n] = total
        made = links.move(small_land.at[2 * n], small_land.at[2 * n + 1], way, small_land.at[2 * n + 1]).start()
        if n == 0:
            pair[0].across()
            pair[1].across()
        made.landed()
        total = total + small_land[2 * n + 1]
    small_o[...] = total
    mem_o[...] = exchanged(3, memory_swap)
    for i in range(pieces):
        settle_table(i)
    for i in (4, 5, 3, 2, 0, 1):
        pair[i].settle()
    for i in (4, 5, 3, 2, 0, 1):
        pair[i].done()
    for made in shares:
        made.landed()
    links.finish_rest(crossing)
    copies.finish()


def backward_layer(count, lengths, group_map, kept, table_half):
    (layer_input, out_grad, exit_rows_grad, loss_part, one, two, three, q, k, v, cq, mk, mv, sc, cc, ps, pc, ga, up, sel,
     wa, wgu, wd, gains) = kept
    rows, width = layer_input.shape
    heads, units = wa.shape[2], ga.shape[1]
    slots, depth = sel.shape[0], width // count
    half, narrow = depth // 2, units // 2
    piece_rows = table_half.shape[0]
    high = 2 * piece_rows
    vmem, hbm = pl.BlockSpec(memory_space=pltpu.VMEM), pl.BlockSpec(memory_space=pl.ANY)

    def three_kinds(rows_of, lead=()):
        return [
            pltpu.VMEM((4,) + lead + (rows_of, heads), BF), pltpu.VMEM(lead + (rows_of, units), BF),
            pltpu.VMEM(lead + (rows_of, narrow), BF),
        ]

    scratch = [pltpu.VMEM(value.shape, value.dtype) for value in kept]
    scratch += [pltpu.VMEM((piece_rows, width), BF), pltpu.VMEM((piece_rows, width), BF)]
    scratch += [
        pltpu.VMEM((4, rows, width), BF), pltpu.VMEM((4, rows, width), BF), pltpu.VMEM((rows, width), F32),
        pltpu.VMEM((rows, heads), BF), pltpu.VMEM((rows, heads), BF), pltpu.VMEM((rows, heads), BF),
        pltpu.VMEM((slots, heads), BF), pltpu.VMEM((slots, heads), BF), pltpu.VMEM((rows, heads), BF),
        pltpu.VMEM((rows, units), BF), pltpu.VMEM((rows, units), BF), pltpu.VMEM((rows, units), BF),
        pltpu.VMEM((8, width, heads), BF), pltpu.VMEM((2, width, units), BF), pltpu.VMEM((2, width, narrow), BF),
    ]
    scratch += three_kinds(width)
    scratch += three_kinds(half, (2,))
    scratch += three_kinds(depth, (2,))
    scratch += three_kinds(depth)
    scratch += three_kinds(depth, (2,))
    scratch += [
        pltpu.VMEM((2, slots // 2, width), BF), pltpu.VMEM((slots // 2, width), BF), pltpu.VMEM((slots // 2, width), BF), pltpu.VMEM((8, width), F32),
        pltpu.VMEM((count, 8, width), F32), pltpu.VMEM((4, 8, width), F32),
        pltpu.SemaphoreType.DMA((80,)), pltpu.SemaphoreType.DMA((80,)), pltpu.SemaphoreType.DMA((48,)),
    ]
    return pl.pallas_call(
        functools.partial(backward_kernel, count),
        out_shape=[
            jax.ShapeDtypeStruct((rows, width), F32), jax.ShapeDtypeStruct((rows, width), F32),
            jax.ShapeDtypeStruct((8, width), F32), jax.ShapeDtypeStruct((8, depth, heads), BF),
            jax.ShapeDtypeStruct((2, depth, units), BF), jax.ShapeDtypeStruct((2, depth, narrow), BF),
            jax.ShapeDtypeStruct((high, width), BF),
        ],
        in_specs=[pl.BlockSpec(memory_space=pltpu.SMEM), vmem] + [hbm] * (len(kept) + 1),
        out_specs=[hbm, vmem, vmem, hbm, hbm, hbm, hbm],
        scratch_shapes=scratch,
        compiler_params=pltpu.CompilerParams(
            collective_id=2, has_side_effects=True, vmem_limit_bytes=VMEM_BYTES
        ),
        name="backward_layer",
    )(lengths, group_map, *kept, table_half)


def finish_kernel(
    vocab, attn_ref, gate_ref, down_ref, small_ref, small_scalar, table_h, in_h, mem_h, block_h, *refs
):
    attn_o, gate_o, down_o = refs[:8], refs[8:10], refs[10]
    gains_o, loss_o, in_o, mem_o, block_o, table_o = refs[11:15], refs[15], refs[16], refs[17], refs[18], refs[19]
    rounded, wide, in_v, mem_v, block_v, sems = refs[20:]
    copies = Copies(sems)
    rows = [pl.ds(i * CHUNK, min(CHUNK, vocab - i * CHUNK)) for i in range(rounded.shape[0] // CHUNK)]
    loads = [copies.start(table_h.at[where], rounded.at[where]) for where in rows]
    moved = [
        (copies.start(src, through), through, dst)
        for src, through, dst in ((in_h, in_v, in_o), (mem_h, mem_v, mem_o), (block_h, block_v, block_o))
    ]
    for where, load in zip(rows, loads):
        load.wait()
        wide[where, :] = rounded[where, :].astype(F32)
        copies.save(wide.at[where], table_o.at[where])
    for load, through, dst in moved:
        load.wait()
        copies.save(through, dst)
    for n, out in enumerate(attn_o):
        out[...] = attn_ref[n].astype(F32)
    for n, out in enumerate(gate_o):
        out[...] = gate_ref[n].astype(F32)
    narrow = down_ref.shape[2]
    for e in range(2):
        down_o[:, e * narrow : (e + 1) * narrow] = down_ref[e].astype(F32)
    depth = attn_ref.shape[1]
    width = small_ref.shape[1]
    turned = pltpu.roll(small_ref[...], width - lax.axis_index("wide") * depth, 1)
    for n, out in enumerate(gains_o):
        out[...] = turned[n : n + 1, 0:depth]
    loss_o[0, 0] = small_scalar[4, 0]
    copies.finish()


def finish(vocab, attn, gate, down, small, table, input_grad, memory_grad, block):
    depth, heads, units = attn.shape[1], attn.shape[2], gate.shape[2]
    vmem, hbm, smem = (pl.BlockSpec(memory_space=space) for space in (pltpu.VMEM, pl.ANY, pltpu.SMEM))
    high, width = table.shape

    def result(*shape):
        return jax.ShapeDtypeStruct(shape, F32)

    return pl.pallas_call(
        functools.partial(finish_kernel, vocab),
        out_shape=[result(depth, heads)] * 8 + [result(depth, units)] * 3 + [result(1, depth)] * 4 + [
            result(1, 1), result(*input_grad.shape), result(*memory_grad.shape),
            jax.ShapeDtypeStruct(block.shape, BF), result(vocab, width),
        ],
        in_specs=[vmem, vmem, vmem, vmem, smem] + [hbm] * 4,
        out_specs=[vmem] * 15 + [smem] + [hbm] * 4,
        scratch_shapes=[
            pltpu.VMEM((high, width), BF), pltpu.VMEM((high, width), F32), pltpu.VMEM(input_grad.shape, F32),
            pltpu.VMEM(memory_grad.shape, F32), pltpu.VMEM(block.shape, BF), pltpu.SemaphoreType.DMA((24,)),
        ],
        compiler_params=pltpu.CompilerParams(vmem_limit_bytes=VMEM_BYTES),
        name="finish",
    )(attn, gate, down, small, small, table, input_grad, memory_grad, block)


def fused_body(
    layer_input,
    memory,
    reader_map,
    target_ids,
    target_lengths,
    out_grad,
    self_q,
    self_k,
    self_v,
    self_o,
    cross_q,
    cross_k,
    cross_v,
    cross_o,
    ff_gate,
    ff_up,
    ff_out,
    gain_self,
    gain_cross,
    gain_ff,
    gain_exit,
    exit_table,
):
    count = lax.axis_size("wide")
    wide_index = lax.axis_index("wide")
    depth = gain_self.shape[0]
    group_map = reader_map[None, :]
    (
        block_output, resid_one, resid_two, resid_three, queries, keys, values, cross_queries, keys_read, values_read,
        context_self, context_cross, probs_self, probs_cross, gate_act, up_act, slots, attn_weights, gate_weights, down_weights,
        gains, exit_rows_grad, loss_part, table_half,
    ) = front(
        count, layer_input, memory, group_map, target_lengths, (gain_self, gain_cross, gain_ff, gain_exit), target_ids[None, :],
        (self_q, self_k, self_v, self_o, cross_q, cross_k, cross_v, cross_o, ff_gate, ff_up, ff_out), exit_table,
    )
    input_grad, memory_grad, small, attn_grads, gate_grads, down_grads, table_grad = backward_layer(
        count, target_lengths, group_map,
        (
            layer_input, out_grad, exit_rows_grad, loss_part, resid_one, resid_two, resid_three, queries, keys, values,
            cross_queries, keys_read, values_read, context_self, context_cross, probs_self, probs_cross, gate_act, up_act,
            slots, attn_weights, gate_weights, down_weights, gains,
        ),
        table_half,
    )
    done = finish(
        exit_table.shape[0], attn_grads, gate_grads, down_grads, small, table_grad, input_grad, memory_grad, block_output
    )
    attn, gate, down, gains, loss = done[:8], done[8:10], done[10], done[11:15], done[15]
    input_grad, memory_grad, block_output, table_grad = done[16:]
    return (
        block_output, loss[0, 0], input_grad, memory_grad, attn[0], attn[1], attn[2], attn[3], attn[6], attn[4], attn[5],
        attn[7], gate[0], gate[1], down, gains[0][0], gains[1][0], gains[2][0], gains[3][0], table_grad,
    )


def fits(mesh):
    return mesh.shape["wide"] == 4 and mesh.shape["tp"] == 2 and mesh.shape["grp"] == 4


def solution(mesh):
    placed = (
        P(("grp", "wide"), None),
        P(("grp", "wide"), None),
        P("grp"),
        P("grp"),
        P(),
        P(("grp", "wide"), None),
        P("wide", "tp"),
        P("wide", "tp"),
        P("wide", "tp"),
        P("wide", "tp"),
        P("wide", "tp"),
        P("wide", "tp"),
        P("wide", "tp"),
        P("wide", "tp"),
        P("wide", "tp"),
        P("wide", "tp"),
        P("wide", "tp"),
        P("wide"),
        P("wide"),
        P("wide"),
        P("wide"),
        P(("wide", "tp"), None),
    )
    return jax.shard_map(
        fused_body if fits(mesh) else plain_body,
        mesh=mesh,
        in_specs=placed,
        out_specs=(
            P(("grp", "wide"), None),
            P(),
            P(("grp", "wide"), None),
            P(("grp", "wide"), None),
            P("wide", "tp"),
            P("wide", "tp"),
            P("wide", "tp"),
            P("wide", "tp"),
            P("wide", "tp"),
            P("wide", "tp"),
            P("wide", "tp"),
            P("wide", "tp"),
            P("wide", "tp"),
            P("wide", "tp"),
            P("wide", "tp"),
            P("wide"),
            P("wide"),
            P("wide"),
            P("wide"),
            P(("wide", "tp"), None),
        ),
        check_vma=False,
    )
```

```python
import functools
import types

import jax
import jax.numpy as jnp
from jax import lax
from jax.experimental import pallas as pl
from jax.experimental.pallas import tpu as pltpu
from jax.sharding import PartitionSpec as P

HEAD_DIM = 64


EPSILON = 1e-06
MASKED = -1e30


def merged(shard, axis, combine):
    everything = jax.tree.map(
        lambda part, kind: lax.all_gather(part.astype(kind), axis),
        shard,
        (jnp.bfloat16, jnp.bfloat16, jnp.bfloat16),
    )

    def take(k):
        return jax.tree.map(lambda part, own: part[k].astype(own.dtype), everything, shard)

    return lax.fori_loop(
        1, lax.axis_size(axis), lambda k, so_far: combine(so_far, take(k)), take(0)
    )


def project(left, right):
    return jnp.dot(left, right, preferred_element_type=jnp.float32)


def project_back(left, right):
    return lax.dot_general(
        left, right, (((1,), (1,)), ((), ())), preferred_element_type=jnp.float32
    )


def outer_rows(left, right):
    return lax.dot_general(
        left, right, (((0,), (0,)), ((), ())), preferred_element_type=jnp.float32
    )


def smooth_gate(values):
    return jax.nn.gelu(values, approximate=True)


def normalize(values, gain):
    factor = lax.rsqrt(jnp.mean(values * values, axis=1, keepdims=True) + EPSILON)
    unit_rows = values * factor
    return ((unit_rows * gain).astype(jnp.bfloat16), unit_rows, factor)


def normalize_back(values, unit_rows, factor, gain, grad_rows):
    gain_grad = jnp.sum(grad_rows * unit_rows, axis=0)
    scaled = grad_rows * gain
    inner = jnp.mean(scaled * values, axis=1, keepdims=True)
    return (gain_grad, factor * scaled - unit_rows * factor * factor * inner)


def split_heads(values):
    return values.reshape(values.shape[0], -1, HEAD_DIM).transpose(1, 0, 2)


def join_heads(values):
    return values.transpose(1, 0, 2).reshape(values.shape[1], -1)


def read_slots(group_map, reader, holders, rows_each, capacity):
    matched = (group_map.reshape(holders, rows_each) == reader).astype(jnp.int32)
    ranks = jnp.cumsum(matched, axis=1) - 1
    counts = jnp.sum(matched, axis=1)
    place = lax.iota(jnp.int32, holders * capacity)
    valid = place % capacity < jnp.repeat(counts, capacity, total_repeat_length=holders * capacity)
    anchor = lax.iota(jnp.int32, holders)[:, None] * capacity + ranks
    target = jnp.where(matched > 0, anchor, holders * capacity)
    return (valid, target.reshape(-1))


def attend_forward(queries, keys, values, allowed):
    factor = HEAD_DIM ** (-0.5)

    def one_head(parts):
        query, key_rows, value_rows = parts
        scores = jnp.where(allowed, project_back(query, key_rows) * factor, MASKED)
        highest = jnp.max(scores, axis=1, keepdims=True)
        exponent = jnp.exp(scores - highest)
        total = jnp.sum(exponent, axis=1, keepdims=True)
        soft_weights = (exponent / total).astype(jnp.bfloat16)
        return (project(soft_weights, value_rows), (highest + jnp.log(total))[:, 0])

    context, log_total = lax.map(
        one_head, (split_heads(queries), split_heads(keys), split_heads(values))
    )
    return (join_heads(context).astype(jnp.bfloat16), log_total)


def attend_backward(queries, keys, values, context_grad, log_total, allowed):
    factor = HEAD_DIM ** (-0.5)

    def one_head(parts):
        query, key_rows, value_rows, grad_rows, log_row = parts
        scores = jnp.where(allowed, project_back(query, key_rows) * factor, MASKED)
        soft = jnp.exp(scores - log_row[:, None])
        soft_grad = project_back(grad_rows, value_rows)
        score_grad = (soft * (soft_grad - jnp.sum(soft * soft_grad, axis=1, keepdims=True))).astype(
            jnp.bfloat16
        )
        query_grad = project(score_grad, key_rows) * factor
        key_grad = outer_rows(score_grad, query) * factor
        value_grad = outer_rows(soft.astype(jnp.bfloat16), grad_rows)
        return (query_grad, key_grad, value_grad)

    grads = lax.map(
        one_head,
        (
            split_heads(queries),
            split_heads(keys),
            split_heads(values),
            split_heads(context_grad),
            log_total,
        ),
    )
    return (join_heads(grads[0]), join_heads(grads[1]), join_heads(grads[2]))


def heads_total(partial_rows):
    return lax.psum(partial_rows, "tp")


def input_total(partial_rows):
    return lax.psum(partial_rows.astype(jnp.bfloat16), "tp").astype(jnp.float32)


def merge_softmax(first, second):
    highest = jnp.maximum(first[0], second[0])
    total = first[1] * jnp.exp(first[0] - highest) + second[1] * jnp.exp(second[0] - highest)
    return (highest, total, first[2] + second[2])


def plain_body(
    layer_input,
    memory,
    reader_map,
    target_ids,
    target_lengths,
    out_grad,
    self_q,
    self_k,
    self_v,
    self_o,
    cross_q,
    cross_k,
    cross_v,
    cross_o,
    ff_gate,
    ff_up,
    ff_out,
    gain_self,
    gain_cross,
    gain_ff,
    gain_exit,
    exit_table,
):
    (
        w_query,
        w_key,
        w_value,
        w_output,
        c_query,
        c_key,
        c_value,
        c_output,
        w_gate,
        w_up,
        w_down,
        full_gain_self,
        full_gain_cross,
        full_gain_ff,
        full_gain_exit,
    ) = (
        lax.all_gather(self_q, "wide", axis=0, tiled=True),
        lax.all_gather(self_k, "wide", axis=0, tiled=True),
        lax.all_gather(self_v, "wide", axis=0, tiled=True),
        lax.all_gather(self_o, "wide", axis=0, tiled=True),
        lax.all_gather(cross_q, "wide", axis=0, tiled=True),
        lax.all_gather(cross_k, "wide", axis=0, tiled=True),
        lax.all_gather(cross_v, "wide", axis=0, tiled=True),
        lax.all_gather(cross_o, "wide", axis=0, tiled=True),
        lax.all_gather(ff_gate, "wide", axis=0, tiled=True),
        lax.all_gather(ff_up, "wide", axis=0, tiled=True),
        lax.all_gather(ff_out, "wide", axis=0, tiled=True),
        lax.all_gather(gain_self, "wide", axis=0, tiled=True),
        lax.all_gather(gain_cross, "wide", axis=0, tiled=True),
        lax.all_gather(gain_ff, "wide", axis=0, tiled=True),
        lax.all_gather(gain_exit, "wide", axis=0, tiled=True),
    )
    gain_one = full_gain_self.astype(jnp.float32)
    gain_two = full_gain_cross.astype(jnp.float32)
    gain_three = full_gain_ff.astype(jnp.float32)
    gain_last = full_gain_exit.astype(jnp.float32)
    seq_rows = layer_input.shape[0]
    wide_count = lax.axis_size("wide")
    wide_index = lax.axis_index("wide")
    group_index = lax.axis_index("grp")
    group_lengths = lax.dynamic_slice_in_dim(target_lengths, group_index * wide_count, wide_count)
    own_length = lax.dynamic_index_in_dim(group_lengths, wide_index, keepdims=False)
    hidden = layer_input.astype(jnp.float32)
    norm_self, unit_self, factor_self = normalize(hidden, gain_one)
    queries = project(norm_self, w_query).astype(jnp.bfloat16)
    keys = project(norm_self, w_key).astype(jnp.bfloat16)
    values = project(norm_self, w_value).astype(jnp.bfloat16)
    position = lax.iota(jnp.int32, seq_rows)
    allowed_self = (position[None, :] <= position[:, None]) & (position[None, :] < own_length)
    context_self, log_self = attend_forward(queries, keys, values, allowed_self)
    resid_one = hidden + heads_total(project_back(context_self, w_output))
    norm_cross, unit_cross, factor_cross = normalize(resid_one, gain_two)
    cross_queries = project(norm_cross, c_query).astype(jnp.bfloat16)
    memory_keys = project(memory, c_key).astype(jnp.bfloat16)
    memory_values = project(memory, c_value).astype(jnp.bfloat16)
    rows_each = memory.shape[0]
    capacity = max(2, 2 * rows_each // wide_count)
    slot_count = wide_count * capacity
    slot_valid, slot_target = read_slots(reader_map, wide_index, wide_count, rows_each, capacity)
    keys_all, values_all = (
        lax.all_gather(memory_keys, "wide", axis=0, tiled=True),
        lax.all_gather(memory_values, "wide", axis=0, tiled=True),
    )
    read_table = (
        jnp.zeros((slot_count,), jnp.int32)
        .at[slot_target]
        .set(lax.iota(jnp.int32, wide_count * rows_each), mode="drop")
    )
    keys_read = jnp.take(keys_all, read_table, axis=0)
    values_read = jnp.take(values_all, read_table, axis=0)
    allowed_cross = slot_valid[None, :]
    context_cross, log_cross = attend_forward(cross_queries, keys_read, values_read, allowed_cross)
    resid_two = resid_one + heads_total(project_back(context_cross, c_output))
    norm_ff, unit_ff, factor_ff = normalize(resid_two, gain_three)
    gate_float = project(norm_ff, w_gate).astype(jnp.bfloat16).astype(jnp.float32)
    up_float = project(norm_ff, w_up).astype(jnp.bfloat16).astype(jnp.float32)
    gelu_value, gelu_pull = jax.vjp(smooth_gate, gate_float)
    ff_hidden = (gelu_value * up_float).astype(jnp.bfloat16)
    resid_three = resid_two + heads_total(project_back(ff_hidden, w_down))
    block_output = resid_three.astype(jnp.bfloat16)
    norm_exit, unit_exit, factor_exit = normalize(resid_three, gain_last)
    rows_all = lax.all_gather(norm_exit, "wide", axis=0, tiled=True)
    group_tokens = rows_all.shape[0]
    vocab_rows = exit_table.shape[0]
    scale_exit = float(rows_all.shape[1]) ** (-0.5)
    logits = project_back(rows_all, exit_table) * scale_exit
    vocab_ids = lax.axis_index(("wide", "tp")) * vocab_rows + lax.iota(jnp.int32, vocab_rows)
    is_target = target_ids[:, None] == vocab_ids[None, :]
    local_high = jnp.max(logits, axis=1)
    local_total = jnp.sum(jnp.exp(logits - local_high[:, None]), axis=1)
    local_pick = jnp.sum(jnp.where(is_target, logits, 0.0), axis=1)
    highest, total_exp, target_logit = merged(
        (local_high, local_total, local_pick), ("wide", "tp"), merge_softmax
    )
    log_total = highest + jnp.log(total_exp)
    token_place = lax.iota(jnp.int32, group_tokens)
    valid = token_place % seq_rows < jnp.repeat(
        group_lengths, seq_rows, total_repeat_length=group_tokens
    )
    token_count = jnp.sum(target_lengths).astype(jnp.float32)
    token_weight = jnp.where(valid, 1.0, 0.0).astype(jnp.float32) / token_count
    group_loss = jnp.sum(token_weight * (log_total - target_logit))
    logit_grad = (
        (jnp.exp(logits - log_total[:, None]) - jnp.where(is_target, 1.0, 0.0))
        * token_weight[:, None]
    ).astype(jnp.bfloat16)
    rows_grad_all = project(logit_grad, exit_table) * scale_exit
    exit_grad = outer_rows(logit_grad, rows_all) * scale_exit
    rows_part = lax.psum_scatter(
        rows_grad_all.astype(jnp.bfloat16), "wide", scatter_dimension=0, tiled=True
    )
    norm_exit_grad = lax.psum(rows_part, "tp").astype(jnp.float32)
    gain_exit_grad, back_exit = normalize_back(
        resid_three, unit_exit, factor_exit, gain_last, norm_exit_grad
    )
    resid_three_grad = out_grad.astype(jnp.float32) + back_exit
    ff_branch = resid_three_grad.astype(jnp.bfloat16)
    w_down_grad = outer_rows(ff_branch, ff_hidden)
    hidden_grad = project(ff_branch, w_down)
    gate_grad = gelu_pull(hidden_grad * up_float)[0].astype(jnp.bfloat16)
    up_grad = (hidden_grad * gelu_value).astype(jnp.bfloat16)
    w_gate_grad = outer_rows(norm_ff, gate_grad)
    w_up_grad = outer_rows(norm_ff, up_grad)
    norm_ff_grad = input_total(project_back(gate_grad, w_gate) + project_back(up_grad, w_up))
    gain_ff_grad, back_ff = normalize_back(resid_two, unit_ff, factor_ff, gain_three, norm_ff_grad)
    resid_two_grad = resid_three_grad + back_ff
    cross_branch = resid_two_grad.astype(jnp.bfloat16)
    c_output_grad = outer_rows(cross_branch, context_cross)
    cross_context_grad = project(cross_branch, c_output).astype(jnp.bfloat16)
    cross_query_grad, keys_grad_read, values_grad_read = attend_backward(
        cross_queries, keys_read, values_read, cross_context_grad, log_cross, allowed_cross
    )
    empty_grads = jnp.zeros((wide_count * rows_each, keys_grad_read.shape[1]), jnp.float32)
    keys_grad_all = empty_grads.at[read_table].add(keys_grad_read)
    values_grad_all = empty_grads.at[read_table].add(values_grad_read)
    keys_grad, values_grad = (
        lax.psum_scatter(
            keys_grad_all.astype(jnp.bfloat16), "wide", scatter_dimension=0, tiled=True
        ).astype(jnp.float32),
        lax.psum_scatter(
            values_grad_all.astype(jnp.bfloat16), "wide", scatter_dimension=0, tiled=True
        ).astype(jnp.float32),
    )
    keys_grad = keys_grad.astype(jnp.bfloat16)
    values_grad = values_grad.astype(jnp.bfloat16)
    cross_query_grad = cross_query_grad.astype(jnp.bfloat16)
    c_query_grad = outer_rows(norm_cross, cross_query_grad)
    c_key_grad = outer_rows(memory, keys_grad)
    c_value_grad = outer_rows(memory, values_grad)
    norm_cross_grad, memory_grad = (
        lax.psum(project_back(cross_query_grad, c_query).astype(jnp.bfloat16), "tp").astype(
            jnp.float32
        ),
        lax.psum(
            (project_back(keys_grad, c_key) + project_back(values_grad, c_value)).astype(
                jnp.bfloat16
            ),
            "tp",
        ).astype(jnp.float32),
    )
    gain_cross_grad, back_cross = normalize_back(
        resid_one, unit_cross, factor_cross, gain_two, norm_cross_grad
    )
    resid_one_grad = resid_two_grad + back_cross
    self_branch = resid_one_grad.astype(jnp.bfloat16)
    w_output_grad = outer_rows(self_branch, context_self)
    self_context_grad = project(self_branch, w_output).astype(jnp.bfloat16)
    query_grad, key_grad, value_grad = attend_backward(
        queries, keys, values, self_context_grad, log_self, allowed_self
    )
    query_grad = query_grad.astype(jnp.bfloat16)
    key_grad = key_grad.astype(jnp.bfloat16)
    value_grad = value_grad.astype(jnp.bfloat16)
    w_query_grad = outer_rows(norm_self, query_grad)
    w_key_grad = outer_rows(norm_self, key_grad)
    w_value_grad = outer_rows(norm_self, value_grad)
    norm_self_grad = input_total(
        project_back(query_grad, w_query)
        + project_back(key_grad, w_key)
        + project_back(value_grad, w_value)
    )
    gain_self_grad, back_self = normalize_back(
        hidden, unit_self, factor_self, gain_one, norm_self_grad
    )
    input_grad = resid_one_grad + back_self
    shards = (
        lax.psum_scatter(
            w_query_grad.astype(jnp.bfloat16), "wide", scatter_dimension=0, tiled=True
        ).astype(jnp.float32),
        lax.psum_scatter(
            w_key_grad.astype(jnp.bfloat16), "wide", scatter_dimension=0, tiled=True
        ).astype(jnp.float32),
        lax.psum_scatter(
            w_value_grad.astype(jnp.bfloat16), "wide", scatter_dimension=0, tiled=True
        ).astype(jnp.float32),
        lax.psum_scatter(
            w_output_grad.astype(jnp.bfloat16), "wide", scatter_dimension=0, tiled=True
        ).astype(jnp.float32),
        lax.psum_scatter(
            c_query_grad.astype(jnp.bfloat16), "wide", scatter_dimension=0, tiled=True
        ).astype(jnp.float32),
        lax.psum_scatter(
            c_key_grad.astype(jnp.bfloat16), "wide", scatter_dimension=0, tiled=True
        ).astype(jnp.float32),
        lax.psum_scatter(
            c_value_grad.astype(jnp.bfloat16), "wide", scatter_dimension=0, tiled=True
        ).astype(jnp.float32),
        lax.psum_scatter(
            c_output_grad.astype(jnp.bfloat16), "wide", scatter_dimension=0, tiled=True
        ).astype(jnp.float32),
        lax.psum_scatter(
            w_gate_grad.astype(jnp.bfloat16), "wide", scatter_dimension=0, tiled=True
        ).astype(jnp.float32),
        lax.psum_scatter(
            w_up_grad.astype(jnp.bfloat16), "wide", scatter_dimension=0, tiled=True
        ).astype(jnp.float32),
        lax.psum_scatter(
            w_down_grad.astype(jnp.bfloat16), "wide", scatter_dimension=0, tiled=True
        ).astype(jnp.float32),
        lax.psum_scatter(
            gain_self_grad.astype(jnp.bfloat16), "wide", scatter_dimension=0, tiled=True
        ).astype(jnp.float32),
        lax.psum_scatter(
            gain_cross_grad.astype(jnp.bfloat16), "wide", scatter_dimension=0, tiled=True
        ).astype(jnp.float32),
        lax.psum_scatter(
            gain_ff_grad.astype(jnp.bfloat16), "wide", scatter_dimension=0, tiled=True
        ).astype(jnp.float32),
        lax.psum_scatter(
            gain_exit_grad.astype(jnp.bfloat16), "wide", scatter_dimension=0, tiled=True
        ).astype(jnp.float32),
    )
    totals = (
        lax.psum(shards[0].astype(jnp.bfloat16), "grp").astype(jnp.float32),
        lax.psum(shards[1].astype(jnp.bfloat16), "grp").astype(jnp.float32),
        lax.psum(shards[2].astype(jnp.bfloat16), "grp").astype(jnp.float32),
        lax.psum(shards[3].astype(jnp.bfloat16), "grp").astype(jnp.float32),
        lax.psum(shards[4].astype(jnp.bfloat16), "grp").astype(jnp.float32),
        lax.psum(shards[5].astype(jnp.bfloat16), "grp").astype(jnp.float32),
        lax.psum(shards[6].astype(jnp.bfloat16), "grp").astype(jnp.float32),
        lax.psum(shards[7].astype(jnp.bfloat16), "grp").astype(jnp.float32),
        lax.psum(shards[8].astype(jnp.bfloat16), "grp").astype(jnp.float32),
        lax.psum(shards[9].astype(jnp.bfloat16), "grp").astype(jnp.float32),
        lax.psum(shards[10].astype(jnp.bfloat16), "grp").astype(jnp.float32),
        lax.psum(shards[11].astype(jnp.bfloat16), "grp").astype(jnp.float32),
        lax.psum(shards[12].astype(jnp.bfloat16), "grp").astype(jnp.float32),
        lax.psum(shards[13].astype(jnp.bfloat16), "grp").astype(jnp.float32),
        lax.psum(shards[14].astype(jnp.bfloat16), "grp").astype(jnp.float32),
        lax.psum(exit_grad.astype(jnp.bfloat16), "grp").astype(jnp.float32),
        lax.psum(group_loss.astype(jnp.bfloat16), "grp").astype(jnp.float32),
    )
    return (
        block_output,
        totals[16],
        input_grad,
        memory_grad,
        totals[0],
        totals[1],
        totals[2],
        totals[3],
        totals[4],
        totals[5],
        totals[6],
        totals[7],
        totals[8],
        totals[9],
        totals[10],
        totals[11],
        totals[12],
        totals[13],
        totals[14],
        totals[15],
    )


MESH = pl.DeviceIdType.MESH
BF = jnp.bfloat16
F32 = jnp.float32
VMEM_BYTES = 63 << 20


def dot_nn(left, right):
    return lax.dot_general(left, right, (((1,), (0,)), ((), ())), preferred_element_type=F32)


def dot_nt(left, right):
    return lax.dot_general(left, right, (((1,), (1,)), ((), ())), preferred_element_type=F32)


def dot_tn(left, right):
    return lax.dot_general(left, right, (((0,), (0,)), ((), ())), preferred_element_type=F32)


class Move:
    def __init__(self, out, arrival):
        self.out, self.arrival = out, arrival

    def start(self):
        self.out.start()
        return self

    def sent(self):
        self.out.wait_send()

    def landed(self):
        self.arrival.wait_recv()


class Links:
    def __init__(self, send_sems, recv_sems):
        self.send_sems, self.recv_sems = send_sems, recv_sems
        self.used = 0
        self.moves = []

    def move(self, src, dst, device, lands):
        k = self.used
        assert k < self.send_sems.shape[0]
        self.used += 1
        out = pltpu.make_async_remote_copy(
            src_ref=src, dst_ref=dst, send_sem=self.send_sems.at[k], recv_sem=self.recv_sems.at[k],
            device_id=device, device_id_type=MESH,
        )
        arrival = pltpu.make_async_remote_copy(
            src_ref=lands, dst_ref=lands, send_sem=self.send_sems.at[k], recv_sem=self.recv_sems.at[k],
            device_id=device, device_id_type=MESH,
        )
        made = Move(out, arrival)
        self.moves.append(made)
        return made

    def finish(self):
        for made in self.moves:
            made.sent()

    def finish_rest(self, done):
        for made in self.moves:
            if made not in done:
                made.sent()


class Copies:
    def __init__(self, sems):
        self.sems, self.used, self.pending = sems, 0, []

    def start(self, src, dst):
        assert self.used < self.sems.shape[0]
        made = pltpu.make_async_copy(src, dst, self.sems.at[self.used])
        self.used += 1
        made.start()
        return made

    def save(self, src, dst):
        self.pending.append(self.start(src, dst))

    def finish(self):
        for made in self.pending:
            made.wait()


def greet(devices):
    barrier = pltpu.get_barrier_semaphore()
    for device in devices:
        pl.semaphore_signal(barrier, inc=1, device_id=device, device_id_type=MESH)
    pl.semaphore_wait(barrier, len(devices))


def position(count):
    g, w, t = lax.axis_index("grp"), lax.axis_index("wide"), lax.axis_index("tp")
    c = lax.rem(g, 2)
    left, right, far = (lax.rem(w + d, count) for d in (count - 1, 1, 2))
    return types.SimpleNamespace(
        count=count, g=g, w=w, t=t, c=c, yy=lax.div(g, 2), left=left, right=right, far=far,
        to_left={"wide": left}, to_right={"wide": right}, to_far={"wide": far},
        to_core={"grp": g + 1 - 2 * c}, to_y={"grp": lax.rem(g + 2, 4)}, to_tp={"tp": 1 - t},
    )


def rms_rows(values, gain):
    factor = lax.rsqrt(jnp.mean(values * values, axis=1, keepdims=True) + EPSILON)
    return (values * factor * gain).astype(BF)


def lane_masks():
    lane = lax.broadcasted_iota(jnp.int32, (1, 2 * HEAD_DIM), 1)
    low = jnp.where(lane < HEAD_DIM, 1.0, 0.0).astype(F32)
    return low.astype(BF), (1.0 - low).astype(BF)


def both_heads(pair):
    low, high = lane_masks()
    return jnp.concatenate([pair * low, pair * high], axis=0)


def pick_heads(stacked):
    rows = stacked.shape[0] // 2
    lane = lax.broadcasted_iota(jnp.int32, (rows, 2 * HEAD_DIM), 1)
    return jnp.where(lane < HEAD_DIM, stacked[:rows], stacked[rows:])


def pair_columns(p):
    return pl.ds(pl.multiple_of(p * 2 * HEAD_DIM, 2 * HEAD_DIM), 2 * HEAD_DIM)


def attention_forward(pairs, queries, keys, values, probs, context, allowed):
    factor = HEAD_DIM ** (-0.5)

    def step(p, carry):
        cols = pair_columns(p)
        scores = dot_nt(both_heads(queries[:, cols]), keys[:, cols]) * factor
        scores = jnp.where(allowed, scores, MASKED)
        exponent = jnp.exp(scores - jnp.max(scores, axis=1, keepdims=True))
        soft = (exponent / jnp.sum(exponent, axis=1, keepdims=True)).astype(BF)
        probs[p] = soft
        context[:, cols] = pick_heads(dot_nn(soft, values[:, cols])).astype(BF)
        return carry

    lax.fori_loop(0, pairs, step, 0)


def slot_choice(own_map, slots, count, part=None):
    rows = own_map.shape[1]
    capacity = slots // count
    reader_iota = lax.broadcasted_iota(jnp.int32, (max(8, count), rows), 0)
    matched = jnp.where(reader_iota == own_map, 1.0, 0.0).astype(F32)
    before = lax.broadcasted_iota(jnp.int32, (rows, rows), 0) < lax.broadcasted_iota(jnp.int32, (rows, rows), 1)
    ranks = dot_nn(matched.astype(BF), jnp.where(before, 1.0, 0.0).astype(BF))
    rank = jnp.sum(matched * ranks, axis=0, keepdims=True).astype(jnp.int32)
    if part is None:
        slot_of = own_map * capacity + rank
    else:
        slots, capacity = slots // 2, capacity // 2
        rank = rank - part * capacity
        slot_of = jnp.where((rank >= 0) & (rank < capacity), own_map * capacity + rank, -1)
    slot_iota = lax.broadcasted_iota(jnp.int32, (slots, rows), 0)
    return jnp.where(slot_iota == slot_of, 1.0, 0.0).astype(BF)


class Gather:
    def __init__(self, here, links, buf, first, depth, placed):
        self.here, self.links, self.buf, self.placed = here, links, buf, placed
        self.mine, self.other = first + here.c, first + 1 - here.c
        self.depth = depth

    def rows(self, at, start, parts):
        size = self.depth // parts
        return pl.ds(pl.multiple_of(at * self.depth + start * size, 16), size)

    def y_half(self, at):
        return self.rows(at, self.here.yy, 2)

    def quarter(self, at, which):
        return self.rows(at, 2 * self.here.yy + which, 4)

    def send(self, where, device, lands, index=None):
        src = self.buf.at[self.mine, where]
        land = self.buf.at[self.mine if index is None else index, lands]
        return self.links.move(src, src, device, land).start()

    def issue(self):
        here = self.here
        for made in self.placed:
            made.wait()
        own = self.y_half(here.w)
        self.from_left = self.send(own, here.to_right, self.y_half(here.left))
        self.from_right = self.send(own, here.to_left, self.y_half(here.right))

    def to_y(self, at):
        return self.send(self.y_half(at), self.here.to_y, self.rows(at, 1 - self.here.yy, 2))

    def forward(self):
        here = self.here
        self.from_left.landed()
        self.far_top = self.send(self.quarter(here.left, 0), here.to_right, self.quarter(here.far, 0))
        self.over_y = [self.to_y(here.left)]
        self.from_right.landed()
        self.far_low = self.send(self.quarter(here.right, 1), here.to_left, self.quarter(here.far, 1))
        self.over_y.append(self.to_y(here.right))

    def complete(self):
        self.far_top.landed()
        self.far_low.landed()
        self.over_y.append(self.to_y(self.here.far))

    def share(self):
        here = self.here
        self.cores = []
        for made, at in zip(self.over_y, (here.left, here.right, here.far)):
            made.landed()
            whole = self.rows(at, 0, 1)
            self.cores.append(self.send(whole, here.to_core, whole, self.other))

    def ready(self):
        for made in self.cores:
            made.landed()


CHUNK = 512
CROSSED = 1


def tall(rows):
    return -(-rows // (2 * CHUNK)) * 2 * CHUNK


def span(at, size):
    return pl.ds(pl.multiple_of(at * size, size), size)


def flip_table(tab, tabt):
    def step(j, carry):
        tabt[:, span(j, CHUNK)] = tab[span(j, CHUNK), :].T
        return carry

    lax.fori_loop(0, tab.shape[0] // CHUNK, step, 0)


def exit_phase(here, links, rows_own, tab, tabt, gt, rb, ids, lens, high, total, stats, packed_stats, stats_tp, stats_wide, coef, weight, acc,
               dx, joint, land_tp, land_far, land_near, swap_out, swap_in, grad_out, vocab, fillers):
    count, g, w, t = here.count, here.g, here.w, here.t
    left, right, far = here.left, here.right, here.far
    to_left, to_right, to_far, to_tp = here.to_left, here.to_right, here.to_far, here.to_tp
    rows, width = rows_own.shape
    half, quarter = rows // 2, rows // 4
    chunks = tab.shape[0] // CHUNK
    scale = float(width) ** (-0.5)
    base = (w * 2 + t) * vocab
    tokens = count * rows

    def block(b):
        return span(b, rows)

    def halved(b, which):
        return pl.ds(pl.multiple_of(b * rows + which * half, half), half)

    def quartered(b, which):
        return pl.ds(pl.multiple_of(b * rows + t * half + which * quarter, quarter), quarter)

    rb[block(w), :] = rows_own[...]
    src = rb.at[halved(w, t)]
    from_left = links.move(src, src, to_right, rb.at[halved(left, t)]).start()
    from_right = links.move(src, src, to_left, rb.at[halved(right, t)]).start()

    def to_other_half(b):
        src = rb.at[halved(b, t)]
        return links.move(src, src, to_tp, rb.at[halved(b, 1 - t)]).start()

    def target_row(cols):
        row = ids[:, cols] - base
        return jnp.where(row < vocab, row, -1)

    def score(b):
        cols = block(b)
        wanted = target_row(cols)
        block_rows = rb[cols, :]

        def step(j, pick):
            at = lax.broadcasted_iota(jnp.int32, (CHUNK, rows), 0) + j * CHUNK
            logits = dot_nt(tab[span(j, CHUNK), :], block_rows) * scale
            logits = jnp.where(at < vocab, logits, MASKED)
            top = jnp.max(logits, axis=0, keepdims=True)
            exponent = jnp.exp(logits - top)
            high[pl.ds(j, 1), cols] = top
            total[pl.ds(j, 1), cols] = jnp.sum(exponent, axis=0, keepdims=True)
            gt[span(j, CHUNK), cols] = exponent.astype(BF)
            return pick + jnp.sum(jnp.where(at == wanted, logits, 0.0), axis=0, keepdims=True)

        pick = lax.fori_loop(0, chunks, step, jnp.zeros((1, rows), F32), unroll=True)
        tops = high[:, cols]
        top = jnp.max(tops, axis=0, keepdims=True)
        stats[0:1, cols] = top
        stats[1:2, cols] = jnp.sum(total[:, cols] * jnp.exp(tops - top), axis=0, keepdims=True)
        stats[2:3, cols] = pick

    score(w)
    from_left.landed()
    src = rb.at[quartered(left, 0)]
    far_top = links.move(src, src, to_right, rb.at[quartered(far, 0)]).start()
    left_rest = to_other_half(left)
    from_right.landed()
    src = rb.at[quartered(right, 1)]
    far_low = links.move(src, src, to_left, rb.at[quartered(far, 1)]).start()
    right_rest = to_other_half(right)
    left_rest.landed()
    score(left)
    far_top.landed()
    far_low.landed()
    far_rest = to_other_half(far)
    right_rest.landed()
    score(right)
    far_rest.landed()
    score(far)

    lines = tokens // 128

    def merged_stats(parts):
        top = parts[0][0:lines]
        for part in parts[1:]:
            top = jnp.maximum(top, part[0:lines])
        mass = sum(part[lines : 2 * lines] * jnp.exp(part[0:lines] - top) for part in parts)
        pick = sum(part[2 * lines :] for part in parts)
        return top, mass, pick

    for n in range(3):
        for line in range(lines):
            packed_stats[n * lines + line : n * lines + line + 1, :] = stats[n : n + 1, line * 128 : (line + 1) * 128]
    swap = links.move(packed_stats, stats_tp, to_tp, stats_tp).start()
    lengths = [lens[k] for k in range(lens.shape[0])]
    tokens_all = lengths[0]
    for length in lengths[1:]:
        tokens_all = tokens_all + length
    place = lax.broadcasted_iota(jnp.int32, (1, rows), 1)
    for b in range(count):
        inside = jnp.where(place < lens[g * count + b], 1.0, 0.0).astype(F32)
        weight[0:1, b * rows : (b + 1) * rows] = inside / tokens_all.astype(F32)
    swap.landed()
    top, mass, pick = merged_stats([packed_stats[...], stats_tp[...]])
    mine_wide = stats_wide.at[w]
    mine_wide[0:lines, :] = top
    mine_wide[lines : 2 * lines, :] = mass
    mine_wide[2 * lines :, :] = pick
    spreads = [
        links.move(mine_wide, mine_wide, device, stats_wide.at[at]).start()
        for device, at in ((to_left, right), (to_right, left), (to_far, far))
    ]
    for made in spreads:
        made.landed()
    top, mass, pick = merged_stats([stats_wide[b] for b in range(count)])
    log_total = top + jnp.log(mass)
    token_loss = log_total - pick
    for line in range(lines):
        cols = slice(line * 128, (line + 1) * 128)
        stats[3:4, cols] = log_total[line : line + 1]
        stats[4:5, cols] = token_loss[line : line + 1]
    all_weight = weight[0:1, :]
    coef[...] = jnp.exp(high[...] - stats[3:4, :]) * all_weight
    stats[5:6, :] = stats[4:5, :] * all_weight
    loss = jnp.sum(stats[5:6, block(w)], axis=1, keepdims=True)

    def row_grads(b):
        cols = block(b)
        wanted = target_row(cols)
        own_weight = weight[0:1, cols]
        acc[...] = jnp.zeros_like(acc)

        def step(j, carry):
            at = lax.broadcasted_iota(jnp.int32, (CHUNK, rows), 0) + j * CHUNK
            grad = gt[span(j, CHUNK), cols].astype(F32) * coef[pl.ds(j, 1), cols]
            grad = (grad - jnp.where(at == wanted, own_weight, 0.0)).astype(BF)
            gt[span(j, CHUNK), cols] = grad
            acc[...] += dot_nn(tabt[:, span(j, CHUNK)], grad)
            return carry

        lax.fori_loop(0, chunks, step, 0, unroll=True)
        return (acc[...] * scale).astype(BF).T

    own_half, other_half = (span(which, half) for which in (t, 1 - t))

    def start_block(slot, b):
        dx[slot] = row_grads(b)
        return links.move(dx.at[slot, other_half], land_tp.at[slot], to_tp, land_tp.at[slot]).start()

    def join_block(slot, made):
        made.landed()
        joint[slot] = (dx[slot, own_half].astype(F32) + land_tp[slot].astype(F32)).astype(BF)

    parts = [pl.ds(which * quarter, quarter) for which in range(2)]

    def near(slot, which, side, device):
        where = parts[which]
        return links.move(joint.at[slot, where], land_near.at[side, where], device, land_near.at[side, where]).start()

    made_far = start_block(0, far)
    made_right = start_block(1, right)
    join_block(0, made_far)
    far_moves = [
        links.move(joint.at[0, parts[which]], land_far.at[which], device, land_far.at[which]).start()
        for which, device in enumerate((to_right, to_left))
    ]
    made_left = start_block(2, left)
    join_block(1, made_right)
    right_low = near(1, 1, 0, to_right)
    made_own = start_block(3, w)
    fillers[0]()
    join_block(2, made_left)
    left_top = near(2, 0, 1, to_left)
    near_late = []
    for which, slot, device in ((0, 1, to_right), (1, 2, to_left)):
        far_moves[which].landed()
        where = parts[which]
        joint[slot, where] = (joint[slot, where].astype(F32) + land_far[which].astype(F32)).astype(BF)
        near_late.append(near(slot, which, which, device))
    fillers[1]()
    join_block(3, made_own)
    for made in [right_low, left_top] + near_late:
        made.landed()
    swap_out[...] = (joint[3].astype(F32) + land_near[0].astype(F32) + land_near[1].astype(F32)).astype(BF)
    swap = links.move(swap_out, swap_in, to_tp, swap_in).start()
    grad_out[own_half, :] = swap_out[...].astype(F32)
    swap.landed()
    grad_out[other_half, :] = swap_in[...].astype(F32)
    return loss


class TableGrad:
    def __init__(self, here, links, copies, tab, gt, rb, land_core, land_y, out):
        self.here, self.links, self.copies = here, links, copies
        self.tab, self.gt, self.rb, self.land_core, self.land_y, self.out = tab, gt, rb, land_core, land_y, out
        self.pieces = tab.shape[0] // (2 * CHUNK)
        self.scale = float(tab.shape[1]) ** (-0.5)
        self.cores, self.ys = [], []

    def rows(self, owner, i):
        return pl.ds(pl.multiple_of((owner * self.pieces + i) * CHUNK, CHUNK), CHUNK)

    def product(self, where):
        return dot_nn(self.gt[where, :], self.rb[...]) * self.scale

    def give(self, i):
        where = self.rows(1 - self.here.c, i)
        self.tab[where, :] = self.product(where).astype(BF)
        land = self.land_core.at[pl.ds(i * CHUNK, CHUNK)]
        self.cores.append(self.links.move(self.tab.at[where], land, self.here.to_core, land).start())

    def take(self, i):
        where = self.rows(self.here.c, i)
        mine = self.product(where)
        self.cores[i].landed()
        self.tab[where, :] = (mine + self.land_core[i * CHUNK : (i + 1) * CHUNK, :].astype(F32)).astype(BF)
        if i < CROSSED:
            land = self.land_y.at[pl.ds(i * CHUNK, CHUNK)]
            self.ys.append(self.links.move(self.tab.at[where], land, self.here.to_y, land).start())
        else:
            self.copies.save(self.tab.at[where], self.out.at[pl.ds(i * CHUNK, CHUNK)])

    def first(self):
        for i in range(self.pieces):
            self.give(i)
        for i in range(CROSSED):
            self.take(i)

    def second(self):
        for i in range(CROSSED, self.pieces):
            self.take(i)

    def settle(self):
        for i in range(CROSSED):
            where = self.rows(self.here.c, i)
            piece = pl.ds(i * CHUNK, CHUNK)
            self.ys[i].landed()
            self.ys[i].sent()
            self.tab[where, :] = (self.tab[where, :].astype(F32) + self.land_y[piece, :].astype(F32)).astype(BF)
            self.copies.save(self.tab.at[where], self.out.at[piece])


def front_kernel(
    count, vocab, x_ref, mem_ref, map_ref, len_ref, gs_ref, gc_ref, gf_ref, ge_ref, ids,
    q_in, k_in, v_in, so_in, cq_in, ck_in, cv_in, co_in, ga_in, up_in, dn_in, table,
    block_o, one_o, two_o, three_o, q_o, k_o, v_o, cq_o, mk_o, mv_o, sc_o, cc_o, ps_o, pc_o,
    ga_o, up_o, sel_o, wa_o, wgu_o, wd_o, gain_o, grad_o, loss_o, half_o,
    wa, wgu, wd, gains, slots, packed, part_out, part_in, valid_slot,
    block, one, two, three, q, k, v, cq, mk, mv, sc, cc, ps, pc, ga, up, gain_sum, exit_rows,
    tab, tabt, gt, rb, high_v, total, stats, packed_stats, stats_tp, stats_wide, coef, weight, acc, dx, joint, land_tp, land_far, land_near,
    swap_out, swap_in, land_core, land_y,
    send_sems, recv_sems, copy_sems,
):
    here = position(count)
    g, w, t = here.g, here.w, here.t
    left, right, far = here.left, here.right, here.far
    to_left, to_right, to_far, to_tp = here.to_left, here.to_right, here.to_far, here.to_tp
    rows = x_ref.shape[0]
    links, copies = Links(send_sems, recv_sems), Copies(copy_sems)
    depth = q_in.shape[0]
    wide_cols = dn_in.shape[1] // 2

    own = pl.ds(pl.multiple_of(w * depth, 16), depth)
    order = (q_in, k_in, v_in, so_in, ck_in, cv_in, cq_in, co_in)
    weights = []
    for j in range(4):
        placed = [copies.start(order[2 * j + e], wa.at[2 * j + e, own]) for e in range(2)]
        weights.append(Gather(here, links, wa, 2 * j, depth, placed))
    for f in range(2):
        cols = pl.ds(f * wide_cols, wide_cols)
        placed = [copies.start(ref.at[:, cols], wgu.at[2 * f + e, own]) for e, ref in enumerate((ga_in, up_in))]
        weights.append(Gather(here, links, wgu, 2 * f, depth, placed))
    placed = [copies.start(dn_in.at[:, pl.ds(e * wide_cols, wide_cols)], wd.at[e, own]) for e in range(2)]
    weights.append(Gather(here, links, wd, 0, depth, placed))

    gain_sum[...] = jnp.zeros_like(gain_sum)
    for n, ref in enumerate((gs_ref, gc_ref, gf_ref, ge_ref)):
        gain_sum[n : n + 1, 0:depth] = ref[...].astype(F32).reshape(1, depth)
    gains[w] = pltpu.roll(gain_sum[...], w * depth, 1)
    table_load = copies.start(table, tab.at[pl.ds(0, vocab)])
    tab[vocab:, :] = jnp.zeros((tab.shape[0] - vocab, tab.shape[1]), BF)
    greet([to_left, to_right, to_far, here.to_core, here.to_y, to_tp])
    gain_moves = [
        links.move(gains.at[w], gains.at[w], device, gains.at[at]).start()
        for device, at in ((to_left, right), (to_right, left), (to_far, far))
    ]
    for first in weights[:2]:
        first.issue()

    capacity = slots.shape[0] // count
    choose = slot_choice(map_ref[:, pl.ds(pl.multiple_of(w * rows, rows), rows)], slots.shape[0], count)
    packed[...] = dot_nn(choose, mem_ref[...]).astype(BF)

    def slot_rows(at, which):
        return pl.ds(pl.multiple_of(at * capacity + which * (capacity // 2), 16), capacity // 2)

    own_slots = pl.ds(pl.multiple_of(w * capacity, 16), capacity)
    slots[own_slots, :] = packed[own_slots, :]
    weights[0].forward()
    weights[2].issue()
    for made in gain_moves:
        made.landed()
    total_gain = gains[0]
    for at in range(1, count):
        total_gain = total_gain + gains[at]
    gain_sum[...] = total_gain
    hidden = x_ref[...].astype(F32)
    norm_self = rms_rows(hidden, gain_sum[0:1, :])
    weights[1].forward()
    weights[0].complete()
    weights[3].issue()
    weights[2].forward()
    weights[0].share()
    weights[1].complete()
    weights[1].share()
    slot_moves = [
        links.move(packed.at[slot_rows(to, t)], slots.at[slot_rows(w, t)], device, slots.at[slot_rows(at, t)]).start()
        for device, to, at in ((to_left, left, right), (to_right, right, left), (to_far, far, far))
    ]
    weights[4].issue()
    weights[0].ready()
    q[...] = dot_nn(norm_self, wa[0]).astype(BF)
    k[...] = dot_nn(norm_self, wa[1]).astype(BF)
    weights[2].complete()
    weights[1].ready()
    v[...] = dot_nn(norm_self, wa[2]).astype(BF)
    weights[3].forward()
    weights[2].share()
    weights[5].issue()
    weights[3].complete()
    slot_fills = []
    for made, at in zip(slot_moves, (right, left, far)):
        made.landed()
        src = slots.at[slot_rows(at, t)]
        slot_fills.append(links.move(src, src, to_tp, slots.at[slot_rows(at, 1 - t)]).start())
    length = len_ref[g * count + w]
    query_at = lax.broadcasted_iota(jnp.int32, (2 * rows, rows), 0)
    query_at = jnp.where(query_at >= rows, query_at - rows, query_at)
    key_at = lax.broadcasted_iota(jnp.int32, (2 * rows, rows), 1)
    allowed_self = (key_at <= query_at) & (key_at < length)
    pairs = q.shape[1] // (2 * HEAD_DIM)
    attention_forward(pairs, q, k, v, ps, sc, allowed_self)

    def exchange_start(n):
        return links.move(part_out.at[n], part_in.at[n], to_tp, part_in.at[n]).start()

    def exchanged(n, made):
        made.landed()
        return part_out[n].astype(F32) + part_in[n].astype(F32)

    part_out[0] = dot_nt(sc[...], wa[3]).astype(BF)
    swap = exchange_start(0)
    weights[3].share()
    weights[4].forward()
    weights[6].issue()
    for made in slot_fills:
        made.landed()
    place = lax.broadcasted_iota(jnp.int32, (1, capacity), 1).astype(F32)
    for b in range(count):
        reads = jnp.sum(jnp.where(map_ref[:, b * rows : (b + 1) * rows] == w, 1.0, 0.0), axis=1, keepdims=True)
        valid_slot[0:1, b * capacity : (b + 1) * capacity] = jnp.where(place < reads, 1.0, 0.0)
    weights[2].ready()
    mk[...] = dot_nn(slots[...], wa[4]).astype(BF)
    mv[...] = dot_nn(slots[...], wa[5]).astype(BF)
    weights[4].complete()
    weights[5].forward()
    allowed_cross = jnp.broadcast_to(valid_slot[0:1, :], (2 * rows, slots.shape[0])) > 0.5
    one[...] = hidden + exchanged(0, swap)
    norm_cross = rms_rows(one[...], gain_sum[1:2, :])
    weights[3].ready()
    cq[...] = dot_nn(norm_cross, wa[6]).astype(BF)
    weights[4].share()
    weights[5].complete()
    weights[6].forward()
    attention_forward(pairs, cq, mk, mv, pc, cc, allowed_cross)
    part_out[1] = dot_nt(cc[...], wa[7]).astype(BF)
    swap = exchange_start(1)
    weights[5].share()
    weights[6].complete()
    weights[6].share()
    table_load.wait()
    flip_table(tab, tabt)
    copies.save(wa, wa_o)
    for src, dst in (
        (q, q_o), (k, k_o), (v, v_o), (sc, sc_o), (ps, ps_o), (mk, mk_o), (mv, mv_o), (cq, cq_o), (cc, cc_o), (pc, pc_o),
        (slots, sel_o), (one, one_o), (gain_sum, gain_o),
    ):
        copies.save(src, dst)
    two[...] = one[...] + exchanged(1, swap)
    copies.save(two, two_o)
    norm_ff = rms_rows(two[...], gain_sum[2:3, :])
    low, high = pl.ds(0, wide_cols), pl.ds(wide_cols, wide_cols)
    for f, cols in ((0, low), (1, high)):
        weights[4 + f].ready()
        ga[:, cols] = dot_nn(norm_ff, wgu[2 * f]).astype(BF)
        up[:, cols] = dot_nn(norm_ff, wgu[2 * f + 1]).astype(BF)
    copies.save(wgu, wgu_o)
    copies.save(ga, ga_o)
    copies.save(up, up_o)
    ff_hidden = (smooth_gate(ga[...].astype(F32)) * up[...].astype(F32)).astype(BF)
    weights[6].ready()
    copies.save(wd, wd_o)
    part_out[2] = (
        dot_nt(ff_hidden[:, :wide_cols], wd[0]) + dot_nt(ff_hidden[:, wide_cols:], wd[1])
    ).astype(BF)
    swap = exchange_start(2)
    three[...] = two[...] + exchanged(2, swap)
    block[...] = three[...].astype(BF)
    exit_rows[...] = rms_rows(three[...], gain_sum[3:4, :])
    copies.save(three, three_o)
    copies.save(block, block_o)
    grads = TableGrad(here, links, copies, tab, gt, rb, land_core, land_y, half_o)
    loss = exit_phase(
        here, links, exit_rows, tab, tabt, gt, rb, ids, len_ref, high_v, total, stats, packed_stats, stats_tp, stats_wide, coef, weight, acc,
        dx, joint, land_tp, land_far, land_near, swap_out, swap_in, grad_o, vocab, (grads.first, grads.second),
    )
    loss_o[...] = jnp.broadcast_to(loss, loss_o.shape)
    grads.settle()
    links.finish_rest(grads.ys)
    copies.finish()


def front(count, layer_input, memory, group_map, lengths, gain_parts, ids, weights, table):
    rows, width = layer_input.shape
    vocab = table.shape[0]
    heads, units = weights[0].shape[1], weights[8].shape[1]
    slots = count * max(2, 2 * rows // count)
    pairs = heads // (2 * HEAD_DIM)
    kept = [
        ((rows, width), BF), ((rows, width), F32), ((rows, width), F32), ((rows, width), F32),
        ((rows, heads), BF), ((rows, heads), BF), ((rows, heads), BF), ((rows, heads), BF),
        ((slots, heads), BF), ((slots, heads), BF), ((rows, heads), BF), ((rows, heads), BF),
        ((pairs, 2 * rows, rows), BF), ((pairs, 2 * rows, slots), BF),
        ((rows, units), BF), ((rows, units), BF), ((slots, width), BF),
        ((8, width, heads), BF), ((4, width, units // 2), BF), ((2, width, units // 2), BF), ((8, width), F32),
    ]
    high = tall(vocab)
    chunks, tokens = high // CHUNK, rows * count
    vmem, hbm, smem = (pl.BlockSpec(memory_space=space) for space in (pltpu.VMEM, pl.ANY, pltpu.SMEM))
    scratch = [
        ((8, width, heads), BF), ((4, width, units // 2), BF), ((2, width, units // 2), BF), ((count, 8, width), F32),
        ((slots, width), BF), ((slots, width), BF), ((3, rows, width), BF), ((3, rows, width), BF), ((8, slots), F32),
    ]
    scratch += kept[:16]
    scratch += [
        ((8, width), F32), ((rows, width), BF),
        ((high, width), BF), ((width, high), BF), ((high, tokens), BF), ((tokens, width), BF), ((chunks, tokens), F32),
        ((chunks, tokens), F32), ((8, tokens), F32), ((3 * tokens // 128, 128), F32), ((3 * tokens // 128, 128), F32),
        ((count, 3 * tokens // 128, 128), F32), ((chunks, tokens), F32),
        ((8, tokens), F32), ((width, rows), F32), ((4, rows, width), BF), ((4, rows // 2, width), BF), ((4, rows // 2, width), BF),
        ((2, rows // 4, width), BF), ((2, rows // 2, width), BF), ((rows // 2, width), BF), ((rows // 2, width), BF),
        ((high // 2, width), BF), ((max(16, CROSSED * CHUNK), width), BF),
    ]
    results = kept + [((rows, width), F32), ((8, 128), F32), ((high // 2, width), BF)]
    return pl.pallas_call(
        functools.partial(front_kernel, count, vocab),
        out_shape=[jax.ShapeDtypeStruct(shape, kind) for shape, kind in results],
        in_specs=[vmem, vmem, vmem, smem] + [vmem] * 5 + [hbm] * 12,
        out_specs=[hbm] * len(kept) + [vmem, vmem, hbm],
        scratch_shapes=[pltpu.VMEM(shape, kind) for shape, kind in scratch]
        + [pltpu.SemaphoreType.DMA((128,)), pltpu.SemaphoreType.DMA((128,)), pltpu.SemaphoreType.DMA((48,))],
        compiler_params=pltpu.CompilerParams(collective_id=0, has_side_effects=True, vmem_limit_bytes=VMEM_BYTES),
        name="forward_and_exit",
    )(layer_input, memory, group_map, lengths, *gain_parts, ids, *weights, table)


GELU_SCALE = 0.7978845608028654
GELU_CUBE = 0.044715


def norm_back(values, gain, grad):
    factor = lax.rsqrt(jnp.mean(values * values, axis=1, keepdims=True) + EPSILON)
    unit = values * factor
    scaled = grad * gain
    inner = jnp.mean(scaled * values, axis=1, keepdims=True)
    return jnp.sum(grad * unit, axis=0, keepdims=True), factor * scaled - unit * (factor * factor * inner)


def attention_backward(pairs, queries, keys, values, probs, context_grad, query_grad, key_grad, value_grad):
    factor = HEAD_DIM ** (-0.5)

    def step(p, carry):
        cols = pair_columns(p)
        grad = both_heads(context_grad[:, cols])
        soft = probs[p]
        soft_float = soft.astype(F32)
        soft_grad = dot_nt(grad, values[:, cols])
        inner = jnp.sum(soft_float * soft_grad, axis=1, keepdims=True)
        score_grad = (soft_float * (soft_grad - inner)).astype(BF)
        query_grad[:, cols] = (pick_heads(dot_nn(score_grad, keys[:, cols])) * factor).astype(BF)
        key_grad[:, cols] = (dot_tn(score_grad, both_heads(queries[:, cols])) * factor).astype(BF)
        value_grad[:, cols] = dot_tn(soft, grad).astype(BF)
        return carry

    lax.fori_loop(0, pairs, step, 0)


class WeightGrad:
    def __init__(self, here, links, copies, grads, first, depth, land_core, land_far, land_near, land_y, mine_out, out):
        self.here, self.links, self.copies = here, links, copies
        self.grads, self.mine, self.other = grads, first + here.c, first + 1 - here.c
        self.depth, self.half = depth, depth // 2
        self.land_core, self.land_far, self.land_near, self.land_y = land_core, land_far, land_near, land_y
        self.mine_out, self.out = mine_out, out

    def whole(self, at):
        return pl.ds(pl.multiple_of(at * self.depth, 16), self.depth)

    def part(self, at, which):
        return pl.ds(pl.multiple_of(at * self.depth + which * self.half, 16), self.half)

    def pair(self):
        self.core = self.links.move(
            self.grads.at[self.other], self.land_core, self.here.to_core, self.land_core
        ).start()

    def near(self, where, side, which, device):
        rows = pl.ds(which * self.half, self.half)
        return self.links.move(
            self.grads.at[self.mine, where], self.land_near.at[side, rows], device, self.land_near.at[side, rows]
        ).start()

    def add_core(self, where):
        self.grads[self.mine, where] = (
            self.grads[self.mine, where].astype(F32) + self.land_core[where].astype(F32)
        ).astype(BF)

    def ring(self):
        here = self.here
        self.core.landed()
        for at in (here.far, here.right, here.left):
            self.add_core(self.whole(at))
            if at is here.far:
                self.far = [
                    self.links.move(
                        self.grads.at[self.mine, self.part(at, e)], self.land_far.at[e], way, self.land_far.at[e]
                    ).start()
                    for e, way in enumerate((here.to_right, here.to_left))
                ]
        self.early = [
            self.near(self.part(here.right, 1), 0, 1, here.to_right),
            self.near(self.part(here.left, 0), 1, 0, here.to_left),
        ]
        self.add_core(self.whole(here.w))

    def pass_on(self):
        here = self.here
        self.late = []
        for e, side, way in ((0, here.right, here.to_right), (1, here.left, here.to_left)):
            self.far[e].landed()
            where = self.part(side, e)
            self.grads[self.mine, where] = (
                self.grads[self.mine, where].astype(F32) + self.land_far[e].astype(F32)
            ).astype(BF)
            self.late.append(self.near(where, e, e, way))

    def across(self):
        for made in self.early + self.late:
            made.landed()
        where = self.whole(self.here.w)
        self.mine_out[0] = (
            self.grads[self.mine, where].astype(F32) + self.land_near[0].astype(F32) + self.land_near[1].astype(F32)
        ).astype(BF)
        self.y = self.links.move(self.mine_out.at[0], self.land_y, self.here.to_y, self.land_y).start()

    def settle(self):
        self.y.landed()
        self.mine_out[1] = (self.mine_out[0].astype(F32) + self.land_y[...].astype(F32)).astype(BF)
        src = self.mine_out.at[1]
        self.copies.save(src, self.out.at[self.mine])
        self.share = self.links.move(
            src, self.out.at[self.mine], self.here.to_core, self.out.at[self.other]
        ).start()

    def done(self):
        self.share.landed()


class LateWeightGrad(WeightGrad):
    def quarter(self, at, which):
        size = self.depth // 4
        return pl.ds(pl.multiple_of(at * self.depth + (2 * self.here.yy + which) * size, 16), size)

    def cross(self, land_early):
        here = self.here
        self.core.landed()
        self.crossings = []
        self.land_early = land_early
        for at in range(here.count):
            self.add_core(self.whole(at))
            src, land = self.grads.at[self.mine, self.part(at, 1 - here.yy)], land_early.at[at]
            self.crossings.append(self.links.move(src, land, here.to_y, land).start())

    def near(self, where, side, which, device):
        rows = pl.ds(which * (self.half // 2), self.half // 2)
        return self.links.move(
            self.grads.at[self.mine, where], self.land_near.at[side, rows], device, self.land_near.at[side, rows]
        ).start()

    def far_land(self, which):
        return self.land_far.at[which, pl.ds(0, self.half // 2)]

    def ring(self):
        here = self.here
        for at, made in enumerate(self.crossings):
            made.landed()
            where = self.part(at, here.yy)
            self.grads[self.mine, where] = (
                self.grads[self.mine, where].astype(F32) + self.land_early[at].astype(F32)
            ).astype(BF)
        self.far = [
            self.links.move(
                self.grads.at[self.mine, self.quarter(here.far, e)], self.far_land(e), way, self.far_land(e)
            ).start()
            for e, way in enumerate((here.to_right, here.to_left))
        ]
        self.early = [
            self.near(self.quarter(here.right, 1), 0, 1, here.to_right),
            self.near(self.quarter(here.left, 0), 1, 0, here.to_left),
        ]

    def pass_on(self):
        here = self.here
        self.late = []
        for e, side, way in ((0, here.right, here.to_right), (1, here.left, here.to_left)):
            self.far[e].landed()
            where = self.quarter(side, e)
            self.grads[self.mine, where] = (
                self.grads[self.mine, where].astype(F32) + self.far_land(e)[...].astype(F32)
            ).astype(BF)
            self.late.append(self.near(where, e, e, way))

    def across(self):
        here = self.here
        for made in self.early + self.late:
            made.landed()
        where = self.part(here.w, here.yy)
        own, other = (pl.ds(pl.multiple_of(y * self.half, 16), self.half) for y in (here.yy, 1 - here.yy))
        self.mine_out[1, own] = (
            self.grads[self.mine, where].astype(F32)
            + self.land_near[0, 0 : self.half].astype(F32)
            + self.land_near[1, 0 : self.half].astype(F32)
        ).astype(BF)
        src = self.mine_out.at[1, own]
        self.y = self.links.move(src, src, here.to_y, self.mine_out.at[1, other]).start()

    def settle(self):
        self.y.landed()
        src = self.mine_out.at[1]
        self.copies.save(src, self.out.at[self.mine])
        self.share = self.links.move(
            src, self.out.at[self.mine], self.here.to_core, self.out.at[self.other]
        ).start()


def backward_kernel(
    count,
    lens, map_ref, x_h, og_h, eg_h, loss_h, one_h, two_h, three_h, q_h, k_h, v_h, cq_h, mk_h, mv_h, sc_h, cc_h, ps_h, pc_h,
    ga_h, up_h, sel_h, wa_h, wgu_h, wd_h, gain_h, half_h,
    in_o, mem_o, small_o, ga8_o, ggu_o, gd_o, table_o,
    x, og, eg, loss, one, two, three, q, k, v, cq, mk, mv, sc, cc, ps, pc, ga, up, sel, wa, wgu, wd, gain, tab, land_t,
    part_out, part_in, grad, dq, dk, dv, dmk, dmv, dctx, gate_grad, up_grad, ff_hidden,
    g8, ggu, gd, lc8, lcg, lcd, lf8, lfg, lfd, ln8, lng, lnd, ly8, lyg, lyd, mo8, mog, mod, land_early,
    back_slots, land_slots, got_slots, small, small_wide, small_land,
    send_sems, recv_sems, copy_sems,
):
    here = position(count)
    links, copies = Links(send_sems, recv_sems), Copies(copy_sems)
    w, t, c = here.w, here.t, here.c
    to_left, to_right, to_far, to_tp = (here.to_left, here.to_right, here.to_far, here.to_tp)
    loads = {}
    for src, dst in (
        (gain_h, gain), (three_h, three), (eg_h, eg), (og_h, og), (ga_h, ga), (up_h, up), (wd_h, wd), (half_h, tab), (wgu_h, wgu),
        (two_h, two), (wa_h, wa), (cc_h, cc), (pc_h, pc), (cq_h, cq), (mk_h, mk), (mv_h, mv), (sel_h, sel), (one_h, one),
        (sc_h, sc), (ps_h, ps), (q_h, q), (k_h, k), (v_h, v), (x_h, x), (loss_h, loss),
    ):
        loads[id(dst)] = copies.start(src, dst)

    def need(*refs):
        for ref in refs:
            loads.pop(id(ref)).wait()

    greet([to_left, to_right, to_far, here.to_core, here.to_y, to_tp])

    pieces = tab.shape[0] // CHUNK
    need(tab)
    crossing = [
        links.move(tab.at[pl.ds(i * CHUNK, CHUNK)], land_t.at[pl.ds(i * CHUNK, CHUNK)], here.to_y, land_t.at[pl.ds(i * CHUNK, CHUNK)]).start()
        for i in range(CROSSED, pieces)
    ]
    shares = []

    def settle_table(i):
        piece = pl.ds(i * CHUNK, CHUNK)
        if i >= CROSSED:
            crossing[i - CROSSED].landed()
            crossing[i - CROSSED].sent()
            tab[piece, :] = (tab[piece, :].astype(F32) + land_t[piece, :].astype(F32)).astype(BF)

        def rows(owner):
            return pl.ds(pl.multiple_of((owner * pieces + i) * CHUNK, CHUNK), CHUNK)

        copies.save(tab.at[piece], table_o.at[rows(c)])
        shares.append(
            links.move(tab.at[piece], table_o.at[rows(c)], here.to_core, table_o.at[rows(1 - c)]).start()
        )

    depth = g8.shape[1] // count

    def weight_pair(i):
        if i < 4:
            kind = LateWeightGrad if i < 2 else WeightGrad
            return kind(here, links, copies, g8, 2 * i, depth, lc8.at[i], lf8.at[i], ln8.at[i], ly8.at[i], mo8.at[i], ga8_o)
        if i == 4:
            return WeightGrad(here, links, copies, ggu, 0, depth, lcg, lfg, lng, lyg, mog, ggu_o)
        return WeightGrad(here, links, copies, gd, 0, depth, lcd, lfd, lnd, lyd, mod, gd_o)

    pair = [weight_pair(i) for i in range(6)]

    def exchange_start(n):
        return links.move(part_out.at[n], part_in.at[n], to_tp, part_in.at[n]).start()

    def exchanged(n, made):
        made.landed()
        return part_out[n].astype(F32) + part_in[n].astype(F32)

    small[...] = jnp.zeros_like(small)
    need(gain, three, eg, og)
    gain_row, back = norm_back(three[...], gain[3:4, :], eg[...])
    small[3:4, :] = gain_row
    grad[...] = og[...].astype(F32) + back
    branch = grad[...].astype(BF)
    need(ga, up, wd)
    units = wd.shape[2]
    for e in range(2):
        cols = slice(e * units, (e + 1) * units)
        act = ga[:, cols].astype(F32)
        up_act = up[:, cols].astype(F32)
        square = act * act
        bend = jnp.tanh(GELU_SCALE * (act + GELU_CUBE * act * square))
        gate = 0.5 * act * (1.0 + bend)
        slope = 0.5 * (1.0 + bend) + 0.5 * act * (1.0 - bend * bend) * (GELU_SCALE * (1.0 + 3.0 * GELU_CUBE * square))
        hidden_grad = dot_nn(branch, wd[e])
        gate_grad[:, cols] = (hidden_grad * up_act * slope).astype(BF)
        up_grad[:, cols] = (hidden_grad * gate).astype(BF)
        ff_hidden[:, cols] = (gate * up_act).astype(BF)
    need(wgu)
    total = dot_nt(gate_grad[:, :units], wgu[0]) + dot_nt(up_grad[:, :units], wgu[1])
    total += dot_nt(gate_grad[:, units:], wgu[2]) + dot_nt(up_grad[:, units:], wgu[3])
    part_out[0] = total.astype(BF)
    swap = exchange_start(0)
    need(two)
    norm_t = rms_rows(two[...], gain[2:3, :]).T
    ggu[0] = dot_nn(norm_t, gate_grad[...]).astype(BF)
    ggu[1] = dot_nn(norm_t, up_grad[...]).astype(BF)
    pair[4].pair()
    branch_rows = branch.T
    for e in range(2):
        gd[e] = dot_nn(branch_rows, ff_hidden[:, e * units : (e + 1) * units]).astype(BF)
    pair[5].pair()
    for i in range(CROSSED):
        settle_table(i)
    pair[4].ring()
    gain_row, back = norm_back(two[...], gain[2:3, :], exchanged(0, swap))
    small[2:3, :] = gain_row
    grad[...] += back

    branch = grad[...].astype(BF)
    need(wa, cc, pc, cq, mk, mv, sel)
    dctx[...] = dot_nn(branch, wa[7]).astype(BF)
    pairs = dctx.shape[1] // (2 * HEAD_DIM)
    attention_backward(pairs, cq, mk, mv, pc, dctx, dq, dmk, dmv)
    part_out[1] = dot_nt(dq[...], wa[6]).astype(BF)
    swap = exchange_start(1)
    pair[5].ring()
    pair[4].pass_on()
    need(one)
    slots_grad = (dot_nt(dmk[...], wa[4]) + dot_nt(dmv[...], wa[5])).astype(BF)
    capacity = slots_grad.shape[0] // count
    half_slots = capacity // 2
    for b in range(count):
        for e in range(2):
            start = b * capacity + e * half_slots
            back_slots[e, b * half_slots : (b + 1) * half_slots] = slots_grad[start : start + half_slots]
    mem_swap = links.move(back_slots.at[1 - t], land_slots, to_tp, land_slots).start()

    def slot_rows(at):
        return pl.ds(pl.multiple_of(at * half_slots, 16), half_slots)

    g8[7] = dot_nn(branch.T, cc[...]).astype(BF)
    norm_t = rms_rows(one[...], gain[1:2, :]).T
    g8[6] = dot_nn(norm_t, dq[...]).astype(BF)
    pair[3].pair()
    slots_t = sel[...].T
    g8[4] = dot_nn(slots_t, dmk[...]).astype(BF)
    g8[5] = dot_nn(slots_t, dmv[...]).astype(BF)
    pair[2].pair()
    pair[5].pass_on()
    pair[3].ring()
    pair[2].ring()
    mem_swap.landed()
    back_slots[t] = (back_slots[t].astype(F32) + land_slots[...].astype(F32)).astype(BF)
    returns = [
        links.move(back_slots.at[t, slot_rows(to)], got_slots.at[slot_rows(w)], device, got_slots.at[slot_rows(at)]).start()
        for device, to, at in ((to_left, here.left, here.right), (to_right, here.right, here.left), (to_far, here.far, here.far))
    ]
    got_slots[slot_rows(w), :] = back_slots[t, slot_rows(w), :]
    gain_row, back = norm_back(one[...], gain[1:2, :], exchanged(1, swap))
    small[1:2, :] = gain_row
    grad[...] += back

    branch = grad[...].astype(BF)
    need(sc, ps, q, k, v, x)
    dctx[...] = dot_nn(branch, wa[3]).astype(BF)
    attention_backward(pairs, q, k, v, ps, dctx, dq, dk, dv)
    part_out[2] = (dot_nt(dq[...], wa[0]) + dot_nt(dk[...], wa[1]) + dot_nt(dv[...], wa[2])).astype(BF)
    swap = exchange_start(2)
    pair[4].across()
    hidden = x[...].astype(F32)
    norm_t = rms_rows(hidden, gain[0:1, :]).T
    g8[0] = dot_nn(norm_t, dq[...]).astype(BF)
    g8[1] = dot_nn(norm_t, dk[...]).astype(BF)
    pair[0].pair()
    g8[2] = dot_nn(norm_t, dv[...]).astype(BF)
    g8[3] = dot_nn(branch.T, sc[...]).astype(BF)
    pair[1].pair()
    pair[3].pass_on()
    pair[2].pass_on()
    pair[0].cross(land_early.at[0])
    pair[1].cross(land_early.at[1])
    pair[5].across()
    for made in returns:
        made.landed()
    rows = x.shape[0]
    choose = slot_choice(map_ref[:, pl.ds(pl.multiple_of(w * rows, rows), rows)], slots_grad.shape[0], count, t)
    part_out[3] = dot_tn(choose, got_slots[...]).astype(BF)
    memory_swap = exchange_start(3)
    gain_row, back = norm_back(hidden, gain[0:1, :], exchanged(2, swap))
    small[0:1, :] = gain_row
    grad[...] += back
    copies.save(grad, in_o)
    pair[0].ring()
    pair[1].ring()
    need(loss)
    small[4:5, 0:128] = loss[0:1, :]

    small_wide[w] = small[...]
    sums = [
        links.move(small, small_wide.at[w], device, small_wide.at[at]).start()
        for device, at in ((to_left, here.right), (to_right, here.left), (to_far, here.far))
    ]
    settle_table(CROSSED)
    pair[0].pass_on()
    pair[1].pass_on()
    pair[3].across()
    pair[2].across()
    for made in sums:
        made.landed()
    total = small_wide[0]
    for b in range(1, count):
        total = total + small_wide[b]
    for n, way in enumerate((here.to_core, here.to_y)):
        small_land[2 * n] = total
        made = links.move(small_land.at[2 * n], small_land.at[2 * n + 1], way, small_land.at[2 * n + 1]).start()
        if n == 0:
            pair[0].across()
            pair[1].across()
        made.landed()
        total = total + small_land[2 * n + 1]
    small_o[...] = total
    mem_o[...] = exchanged(3, memory_swap)
    for i in range(CROSSED + 1, pieces):
        settle_table(i)
    for i in (4, 5, 3, 2, 0, 1):
        pair[i].settle()
    for i in (4, 5, 3, 2, 0, 1):
        pair[i].done()
    for made in shares:
        made.landed()
    links.finish_rest(crossing)
    copies.finish()


def backward_layer(count, lengths, group_map, kept, table_half):
    (layer_input, out_grad, exit_rows_grad, loss_part, one, two, three, q, k, v, cq, mk, mv, sc, cc, ps, pc, ga, up, sel,
     wa, wgu, wd, gains) = kept
    rows, width = layer_input.shape
    heads, units = wa.shape[2], ga.shape[1]
    slots, depth = sel.shape[0], width // count
    half, narrow = depth // 2, units // 2
    piece_rows = table_half.shape[0]
    high = 2 * piece_rows
    vmem, hbm = pl.BlockSpec(memory_space=pltpu.VMEM), pl.BlockSpec(memory_space=pl.ANY)

    def three_kinds(rows_of, lead=()):
        return [
            pltpu.VMEM((4,) + lead + (rows_of, heads), BF), pltpu.VMEM(lead + (rows_of, units), BF),
            pltpu.VMEM(lead + (rows_of, narrow), BF),
        ]

    scratch = [pltpu.VMEM(value.shape, value.dtype) for value in kept]
    scratch += [pltpu.VMEM((piece_rows, width), BF), pltpu.VMEM((piece_rows, width), BF)]
    scratch += [
        pltpu.VMEM((4, rows, width), BF), pltpu.VMEM((4, rows, width), BF), pltpu.VMEM((rows, width), F32),
        pltpu.VMEM((rows, heads), BF), pltpu.VMEM((rows, heads), BF), pltpu.VMEM((rows, heads), BF),
        pltpu.VMEM((slots, heads), BF), pltpu.VMEM((slots, heads), BF), pltpu.VMEM((rows, heads), BF),
        pltpu.VMEM((rows, units), BF), pltpu.VMEM((rows, units), BF), pltpu.VMEM((rows, units), BF),
        pltpu.VMEM((8, width, heads), BF), pltpu.VMEM((2, width, units), BF), pltpu.VMEM((2, width, narrow), BF),
    ]
    scratch += three_kinds(width)
    scratch += three_kinds(half, (2,))
    scratch += three_kinds(depth, (2,))
    scratch += three_kinds(depth)
    scratch += three_kinds(depth, (2,))
    scratch += [pltpu.VMEM((2, count, half, heads), BF)]
    scratch += [
        pltpu.VMEM((2, slots // 2, width), BF), pltpu.VMEM((slots // 2, width), BF), pltpu.VMEM((slots // 2, width), BF), pltpu.VMEM((8, width), F32),
        pltpu.VMEM((count, 8, width), F32), pltpu.VMEM((4, 8, width), F32),
        pltpu.SemaphoreType.DMA((96,)), pltpu.SemaphoreType.DMA((96,)), pltpu.SemaphoreType.DMA((48,)),
    ]
    return pl.pallas_call(
        functools.partial(backward_kernel, count),
        out_shape=[
            jax.ShapeDtypeStruct((rows, width), F32), jax.ShapeDtypeStruct((rows, width), F32),
            jax.ShapeDtypeStruct((8, width), F32), jax.ShapeDtypeStruct((8, depth, heads), BF),
            jax.ShapeDtypeStruct((2, depth, units), BF), jax.ShapeDtypeStruct((2, depth, narrow), BF),
            jax.ShapeDtypeStruct((high, width), BF),
        ],
        in_specs=[pl.BlockSpec(memory_space=pltpu.SMEM), vmem] + [hbm] * (len(kept) + 1),
        out_specs=[hbm, vmem, vmem, hbm, hbm, hbm, hbm],
        scratch_shapes=scratch,
        compiler_params=pltpu.CompilerParams(
            collective_id=2, has_side_effects=True, vmem_limit_bytes=VMEM_BYTES
        ),
        name="backward_layer",
    )(lengths, group_map, *kept, table_half)


def finish_kernel(
    vocab, small_ref, small_scalar, attn_h, gate_h, down_h, table_h, in_h, mem_h, block_h, *refs
):
    attn_o, gate_o, down_o = refs[:8], refs[8:10], refs[10]
    gains_o, loss_o, in_o, mem_o, block_o, table_o = refs[11:15], refs[15], refs[16], refs[17], refs[18], refs[19]
    rounded, wide, in_v, mem_v, block_v, attn_ref, gate_ref, down_ref, attn_v, gate_v, down_v, sems = refs[20:]
    copies = Copies(sems)
    rows = [pl.ds(i * CHUNK, min(CHUNK, vocab - i * CHUNK)) for i in range(rounded.shape[0] // CHUNK)]
    small_loads = [copies.start(src, dst) for src, dst in ((attn_h, attn_ref), (gate_h, gate_ref), (down_h, down_ref))]
    loads = [copies.start(table_h.at[where], rounded.at[where]) for where in rows]
    moved = [
        (copies.start(src, through), through, dst)
        for src, through, dst in ((in_h, in_v, in_o), (mem_h, mem_v, mem_o), (block_h, block_v, block_o))
    ]
    for load in small_loads:
        load.wait()
    narrow = down_ref.shape[2]
    for n, out in enumerate(attn_o):
        attn_v[n] = attn_ref[n].astype(F32)
        copies.save(attn_v.at[n], out)
    for n, out in enumerate(gate_o):
        gate_v[n] = gate_ref[n].astype(F32)
        copies.save(gate_v.at[n], out)
    for e in range(2):
        down_v[:, e * narrow : (e + 1) * narrow] = down_ref[e].astype(F32)
    copies.save(down_v, down_o)
    for where, load in zip(rows, loads):
        load.wait()
        wide[where, :] = rounded[where, :].astype(F32)
        copies.save(wide.at[where], table_o.at[where])
    for load, through, dst in moved:
        load.wait()
        copies.save(through, dst)
    depth = attn_ref.shape[1]
    width = small_ref.shape[1]
    turned = pltpu.roll(small_ref[...], width - lax.axis_index("wide") * depth, 1)
    for n, out in enumerate(gains_o):
        out[...] = turned[n : n + 1, 0:depth]
    loss_o[0, 0] = small_scalar[4, 0]
    copies.finish()


def finish(vocab, attn, gate, down, small, table, input_grad, memory_grad, block):
    depth, heads, units = attn.shape[1], attn.shape[2], gate.shape[2]
    vmem, hbm, smem = (pl.BlockSpec(memory_space=space) for space in (pltpu.VMEM, pl.ANY, pltpu.SMEM))
    high, width = table.shape

    def result(*shape):
        return jax.ShapeDtypeStruct(shape, F32)

    return pl.pallas_call(
        functools.partial(finish_kernel, vocab),
        out_shape=[result(depth, heads)] * 8 + [result(depth, units)] * 3 + [result(1, depth)] * 4 + [
            result(1, 1), result(*input_grad.shape), result(*memory_grad.shape),
            jax.ShapeDtypeStruct(block.shape, BF), result(vocab, width),
        ],
        in_specs=[vmem, smem] + [hbm] * 7,
        out_specs=[hbm] * 11 + [vmem] * 4 + [smem] + [hbm] * 4,
        scratch_shapes=[
            pltpu.VMEM((high, width), BF), pltpu.VMEM((high, width), F32), pltpu.VMEM(input_grad.shape, F32),
            pltpu.VMEM(memory_grad.shape, F32), pltpu.VMEM(block.shape, BF),
            pltpu.VMEM(attn.shape, BF), pltpu.VMEM(gate.shape, BF), pltpu.VMEM(down.shape, BF),
            pltpu.VMEM(attn.shape, F32), pltpu.VMEM(gate.shape, F32), pltpu.VMEM((depth, units), F32),
            pltpu.SemaphoreType.DMA((40,)),
        ],
        compiler_params=pltpu.CompilerParams(vmem_limit_bytes=VMEM_BYTES),
        name="finish",
    )(small, small, attn, gate, down, table, input_grad, memory_grad, block)


def fused_body(
    layer_input,
    memory,
    reader_map,
    target_ids,
    target_lengths,
    out_grad,
    self_q,
    self_k,
    self_v,
    self_o,
    cross_q,
    cross_k,
    cross_v,
    cross_o,
    ff_gate,
    ff_up,
    ff_out,
    gain_self,
    gain_cross,
    gain_ff,
    gain_exit,
    exit_table,
):
    count = lax.axis_size("wide")
    wide_index = lax.axis_index("wide")
    depth = gain_self.shape[0]
    group_map = reader_map[None, :]
    (
        block_output, resid_one, resid_two, resid_three, queries, keys, values, cross_queries, keys_read, values_read,
        context_self, context_cross, probs_self, probs_cross, gate_act, up_act, slots, attn_weights, gate_weights, down_weights,
        gains, exit_rows_grad, loss_part, table_half,
    ) = front(
        count, layer_input, memory, group_map, target_lengths, (gain_self, gain_cross, gain_ff, gain_exit), target_ids[None, :],
        (self_q, self_k, self_v, self_o, cross_q, cross_k, cross_v, cross_o, ff_gate, ff_up, ff_out), exit_table,
    )
    input_grad, memory_grad, small, attn_grads, gate_grads, down_grads, table_grad = backward_layer(
        count, target_lengths, group_map,
        (
            layer_input, out_grad, exit_rows_grad, loss_part, resid_one, resid_two, resid_three, queries, keys, values,
            cross_queries, keys_read, values_read, context_self, context_cross, probs_self, probs_cross, gate_act, up_act,
            slots, attn_weights, gate_weights, down_weights, gains,
        ),
        table_half,
    )
    done = finish(
        exit_table.shape[0], attn_grads, gate_grads, down_grads, small, table_grad, input_grad, memory_grad, block_output
    )
    attn, gate, down, gains, loss = done[:8], done[8:10], done[10], done[11:15], done[15]
    input_grad, memory_grad, block_output, table_grad = done[16:]
    return (
        block_output, loss[0, 0], input_grad, memory_grad, attn[0], attn[1], attn[2], attn[3], attn[6], attn[4], attn[5],
        attn[7], gate[0], gate[1], down, gains[0][0], gains[1][0], gains[2][0], gains[3][0], table_grad,
    )


def fits(mesh):
    return mesh.shape["wide"] == 4 and mesh.shape["tp"] == 2 and mesh.shape["grp"] == 4


def solution(mesh):
    placed = (
        P(("grp", "wide"), None),
        P(("grp", "wide"), None),
        P("grp"),
        P("grp"),
        P(),
        P(("grp", "wide"), None),
        P("wide", "tp"),
        P("wide", "tp"),
        P("wide", "tp"),
        P("wide", "tp"),
        P("wide", "tp"),
        P("wide", "tp"),
        P("wide", "tp"),
        P("wide", "tp"),
        P("wide", "tp"),
        P("wide", "tp"),
        P("wide", "tp"),
        P("wide"),
        P("wide"),
        P("wide"),
        P("wide"),
        P(("wide", "tp"), None),
    )
    return jax.shard_map(
        fused_body if fits(mesh) else plain_body,
        mesh=mesh,
        in_specs=placed,
        out_specs=(
            P(("grp", "wide"), None),
            P(),
            P(("grp", "wide"), None),
            P(("grp", "wide"), None),
            P("wide", "tp"),
            P("wide", "tp"),
            P("wide", "tp"),
            P("wide", "tp"),
            P("wide", "tp"),
            P("wide", "tp"),
            P("wide", "tp"),
            P("wide", "tp"),
            P("wide", "tp"),
            P("wide", "tp"),
            P("wide", "tp"),
            P("wide"),
            P("wide"),
            P("wide"),
            P("wide"),
            P(("wide", "tp"), None),
        ),
        check_vma=False,
    )
```
